32 devices in a mesh: section: 4 (over z), ctx: 8 (over y, x, core).
Axes of the slice: x: 2, y: 2, z: 4, core: 2. Of those that a mesh axis runs over, the one named last changes fastest.
Arguments:
- queries: bfloat16 [4, 2048, 3072], P('section', 'ctx'), may hold values from -160 to 160
- keys: bfloat16 [4, 2048, 512], P('section', 'ctx'), may hold values from -48 to 48
- values: bfloat16 [4, 2048, 512], P('section', 'ctx'), may hold values from -15 to 15
- cotangent: bfloat16 [4, 2048, 3072], P('section', 'ctx'), may hold values from -6 to 6
- router_logits: bfloat16 [4, 2048], P('section', 'ctx'), may hold values from -8 to 8
- positions: int32 [4, 2048], P('section', 'ctx'), may hold values from -1 to 8191, as said below
- counts: int32 [4, 8], P('section', 'ctx'), may hold values from 0 to 2, as said below
Outputs:
- handed: bfloat16 [4, 2048, 3072], P('section', 'ctx')
- value_grad: bfloat16 [4, 2048, 512], P('section', 'ctx')
- gate_grad: bfloat16 [4, 2048], P('section', 'ctx')
The draws below stay inside these ranges and needn't reach their ends.
Inputs may be any that keep to these rules, and one draw needn't show every extreme that they name: For every micro-batch and every shard c, the counts of shards 0 to c sum to c + 1 or c + 2; shard 0 holds 2 blocks; all counts of a micro-batch sum to 8. In shard c's slots, the first counts * 128 hold distinct positions in increasing order, all within c * 1024 to (c + 1) * 1024 - 1; the other slots hold -1.
All inputs are finite; a program needn't handle non-finite values.
Results may differ from the reference program's by a relative error of at most 0.0066.
Values may be sent and summed in bfloat16 or wider, within the bound.
No kernel may reach another device: no remote copies, remote signals or barrier semaphores. Data moves between devices by JAX's collectives and lax.ppermute only.
A program may use at most 128 MiB of HBM per device.

```python
import math
import jax
import jax.numpy as jnp
from jax import lax

QUERY_HEADS = 24
KEY_VALUE_HEADS = 4
HEAD_SIZE = 128
BLOCK_ROWS = 128
MAXB = 2
TOK_DEV = 1024
ROUTED_SLOTS = 2048
MICRO_BATCHES = 4
N_CTX = 8


def block_counts(key):
    carry_key = jax.random.fold_in(key, 11)
    carry_bits = jax.random.randint(carry_key, (MICRO_BATCHES, N_CTX), 0, 2).astype(jnp.int32)
    column = jnp.arange(N_CTX)[None, :]
    carry_bits = jnp.where(column == 0, 1, jnp.where(column == N_CTX - 1, 0, carry_bits)).astype(jnp.int32)
    carry_before = jnp.concatenate([jnp.zeros((MICRO_BATCHES, 1), jnp.int32), carry_bits[:, :-1]], axis=1)
    return (1 + carry_bits - carry_before).astype(jnp.int32)


def draw_counts(key, part):
    return block_counts(key)


def draw_positions(key, part):
    held_blocks = block_counts(key)
    slot_total = MAXB * BLOCK_ROWS
    noise_key = jax.random.fold_in(key, 23)
    noise_draw = jax.random.randint(noise_key, (MICRO_BATCHES, N_CTX, TOK_DEV), 0, 1 << 16)
    sort_scores = noise_draw * TOK_DEV + jnp.arange(TOK_DEV, dtype=jnp.int32)[None, None, :]
    shuffled = jnp.argsort(sort_scores, axis=-1)[..., :slot_total].astype(jnp.int32)
    slot_index = jnp.arange(slot_total, dtype=jnp.int32)[None, None, :]
    live_slot = slot_index < held_blocks[..., None] * BLOCK_ROWS
    sort_keys = jnp.where(live_slot, shuffled, shuffled + TOK_DEV)
    ranked = jnp.sort(sort_keys, axis=-1)
    shard_start = jnp.arange(N_CTX, dtype=jnp.int32)[None, :, None] * TOK_DEV
    placed = jnp.where(live_slot, ranked + shard_start, -1)
    return placed.reshape(MICRO_BATCHES, N_CTX * slot_total).astype(jnp.int32)


def head_draws(key):
    query_group_width = QUERY_HEADS // KEY_VALUE_HEADS
    total_row_count = N_CTX * MAXB * BLOCK_ROWS
    base_key = jax.random.fold_in(key, 37)
    random_key_first = jax.random.fold_in(base_key, 0)
    random_key_fifth = jax.random.fold_in(base_key, 4)
    key_row_block = 2.0 * jnp.clip(jax.random.normal(random_key_first, (MICRO_BATCHES, total_row_count, KEY_VALUE_HEADS, HEAD_SIZE)), -6.0, 6.0)
    query_row_block = jnp.clip(jax.random.normal(random_key_fifth, (MICRO_BATCHES, total_row_count, KEY_VALUE_HEADS, query_group_width, HEAD_SIZE)), -6.0, 6.0)
    return (query_row_block.reshape(MICRO_BATCHES, total_row_count, QUERY_HEADS * HEAD_SIZE), key_row_block.reshape(MICRO_BATCHES, total_row_count, KEY_VALUE_HEADS * HEAD_SIZE))


def draw_queries(key, part):
    return head_draws(key)[0].astype(jnp.bfloat16)


def draw_keys(key, part):
    return head_draws(key)[1].astype(jnp.bfloat16)


def levels(own_key, shape, cuts, low, top_value):
    loudness = 1.0
    for axis_at, blocks in cuts:
        heights = jax.random.uniform(jax.random.fold_in(jax.random.fold_in(own_key, 6), axis_at), (blocks,), jnp.float32, low / len(cuts), top_value / len(cuts))
        loudness = loudness * jnp.repeat(jnp.exp(heights), shape[axis_at] // blocks).reshape((-1,) + (1,) * (len(shape) - 1 - axis_at))
    return loudness


def gaussian(stream_key, shape, width, bound, shards=(), kind=jnp.bfloat16):
    drawn = width * jax.random.normal(stream_key, shape, jnp.float32)
    if shards:
        drawn = drawn * levels(stream_key, shape, shards, -0.22, 0.18)
    return jnp.clip(drawn, -bound, bound).astype(kind)


def setup_inputs(seed: int = 0) -> dict:
    arg_keys = jax.random.split(jax.random.key(seed), 8)
    queries = draw_queries(jax.random.fold_in(arg_keys[7], 71), 0)
    keys = draw_keys(jax.random.fold_in(arg_keys[7], 71), 0)
    values = gaussian(arg_keys[2], (MICRO_BATCHES, ROUTED_SLOTS, KEY_VALUE_HEADS * HEAD_SIZE), 3.0, 15.0, ((0, 4), (1, 8)))
    cotangent = gaussian(arg_keys[3], (MICRO_BATCHES, ROUTED_SLOTS, QUERY_HEADS * HEAD_SIZE), 1.0, 6.0, ((0, 4), (1, 8)))
    router_logits = gaussian(arg_keys[4], (MICRO_BATCHES, ROUTED_SLOTS), 2.0, 8.0, ((0, 4), (1, 8)))
    positions = draw_positions(jax.random.fold_in(arg_keys[7], 71), 0)
    counts = draw_counts(jax.random.fold_in(arg_keys[7], 71), 0)
    return dict(queries=queries, keys=keys, values=values, cotangent=cotangent, router_logits=router_logits, positions=positions, counts=counts)


def block_order(blocks_held):
    inclusive = jnp.cumsum(blocks_held).astype(jnp.int32)
    target = jnp.arange(N_CTX, dtype=jnp.int32)
    owner_shard = lax.optimization_barrier(jnp.sum((inclusive[None, :] <= target[:, None]).astype(jnp.int32), axis=1)).astype(jnp.int32)
    first_block = (inclusive - blocks_held).astype(jnp.int32)
    local_block = (target - first_block[owner_shard]).astype(jnp.int32)
    return (owner_shard * MAXB + local_block).astype(jnp.int32)

def one_section(bundle):
    queries, keys, values, cotangent, logits, places, blocks_held = bundle
    dense_order = block_order(blocks_held)
    query_group_width = QUERY_HEADS // KEY_VALUE_HEADS

    def sorted_positions(source):
        shaped = source.reshape((N_CTX * MAXB, BLOCK_ROWS) + source.shape[1:])
        return shaped[dense_order].reshape((N_CTX * BLOCK_ROWS,) + source.shape[1:])
    key_head_rows = sorted_positions(keys).astype(jnp.float32).reshape(N_CTX * BLOCK_ROWS, KEY_VALUE_HEADS, HEAD_SIZE)
    value_head_rows = sorted_positions(values).astype(jnp.float32).reshape(N_CTX * BLOCK_ROWS, KEY_VALUE_HEADS, HEAD_SIZE)
    key_places = sorted_positions(places)
    query_block_list = sorted_positions(queries).reshape(N_CTX, BLOCK_ROWS, KEY_VALUE_HEADS, query_group_width, HEAD_SIZE)
    grad_blocks = sorted_positions(cotangent).reshape(N_CTX, BLOCK_ROWS, QUERY_HEADS * HEAD_SIZE)
    logit_blocks = sorted_positions(logits).reshape(N_CTX, BLOCK_ROWS)
    place_blocks = key_places.reshape(N_CTX, BLOCK_ROWS)

    def per_block(grad_total, block_parts):
        query_part, grad_part, logit_part, place_part = block_parts
        scores = jnp.einsum('qhgd,khd->hgqk', query_part.astype(jnp.float32), key_head_rows) / math.sqrt(HEAD_SIZE)
        allowed = key_places[None, :] <= place_part[:, None]
        row_top = lax.optimization_barrier(jnp.max(jnp.where(allowed, scores, -jnp.inf), axis=-1))
        weights = jnp.where(allowed, jnp.exp(scores - row_top[..., None]), 0.0)
        weight_sum = lax.optimization_barrier(jnp.sum(weights, axis=-1))
        rounded = lax.optimization_barrier(weights.astype(jnp.bfloat16)).astype(jnp.float32)
        attended = jnp.einsum('hgqk,khd->qhgd', rounded, value_head_rows)
        attended = attended / jnp.transpose(weight_sum, (2, 0, 1))[..., None]
        attended = attended.reshape(BLOCK_ROWS, QUERY_HEADS * HEAD_SIZE)
        gate_values = jax.nn.sigmoid(logit_part.astype(jnp.float32))
        branch = (gate_values[:, None] * attended).astype(jnp.bfloat16)
        log_total = row_top + jnp.log(weight_sum)
        gradient_broad = grad_part.astype(jnp.float32)
        output_gradient = lax.optimization_barrier((gate_values[:, None] * gradient_broad).astype(jnp.bfloat16)).astype(jnp.float32)
        output_gradient = output_gradient.reshape(BLOCK_ROWS, KEY_VALUE_HEADS, query_group_width, HEAD_SIZE)
        probabilities = jnp.where(allowed, jnp.exp(scores - log_total[..., None]), 0.0)
        probabilities = lax.optimization_barrier(probabilities.astype(jnp.bfloat16)).astype(jnp.float32)
        grad_total = grad_total + jnp.einsum('hgqk,qhgd->khd', probabilities, output_gradient)
        gate_term = (gate_values * (1.0 - gate_values) * lax.optimization_barrier(jnp.sum(gradient_broad * attended, axis=1))).astype(jnp.bfloat16)
        return (grad_total, (branch, gate_term))
    initial_gradient = jnp.zeros((N_CTX * BLOCK_ROWS, KEY_VALUE_HEADS, HEAD_SIZE), jnp.float32)
    value_grand_sum, outputs = lax.scan(per_block, initial_gradient, (query_block_list, grad_blocks, logit_blocks, place_blocks))
    branches, gate_terms = outputs

    def to_owner(dense_rows):
        tail = dense_rows.shape[2:]
        empty_slots = jnp.zeros((N_CTX * MAXB, BLOCK_ROWS) + tail, dense_rows.dtype)
        return empty_slots.at[dense_order].set(dense_rows).reshape((N_CTX * MAXB * BLOCK_ROWS,) + tail)
    value_finished = value_grand_sum.astype(jnp.bfloat16).reshape(N_CTX, BLOCK_ROWS, KEY_VALUE_HEADS * HEAD_SIZE)
    return (to_owner(branches), to_owner(value_finished), to_owner(gate_terms))

def reference(queries, keys, values, cotangent, router_logits, positions, counts):
    branch_all, value_grad, gate_grad = lax.map(one_section, (queries, keys, values, cotangent, router_logits, positions, counts))
    handed = jnp.roll(branch_all, 1, axis=0)
    return (handed, value_grad, gate_grad)
```

```python
import math

import jax
import jax.numpy as jnp
from jax import lax
from jax.experimental import pallas as pl
from jax.experimental.pallas import tpu as pltpu
from jax.sharding import PartitionSpec as P

QUERY_HEADS = 24
KEY_VALUE_HEADS = 4
HEAD_SIZE = 128
BLOCK_ROWS = 128
MAXB = 2

CORES = 2
GROUP = QUERY_HEADS // KEY_VALUE_HEADS
LOCAL_HEADS = KEY_VALUE_HEADS // CORES
GROUP_WIDTH = GROUP * HEAD_SIZE
HALF_QUERY = LOCAL_HEADS * GROUP_WIDTH
HALF_KEY = LOCAL_HEADS * HEAD_SIZE
CHIP_BLOCKS = 2 * MAXB - 1
CHIP_ROWS = CHIP_BLOCKS * BLOCK_ROWS
META_ROWS = 16
SLOTS = MAXB * BLOCK_ROWS
MASKED = -1e30
VMEM_LIMIT = 48 * 1024 * 1024
f32 = jnp.float32
bf16 = jnp.bfloat16
i32 = jnp.int32
K_COL = HALF_QUERY
V_COL = HALF_QUERY + HALF_KEY
M_COL = HALF_QUERY + 2 * HALF_KEY
PAYLOAD = M_COL + HEAD_SIZE


def params():
    return pltpu.CompilerParams(vmem_limit_bytes=VMEM_LIMIT)


def whole(shape):
    return pl.BlockSpec(shape, lambda i, s: (0,) * len(shape))


def call(body, scalars, grid_in, operands, outs, out_specs, scratch=(), flops=0, moved=0):
    return pl.pallas_call(
        body,
        grid_spec=pltpu.PrefetchScalarGridSpec(
            num_scalar_prefetch=1,
            grid=(1,),
            in_specs=grid_in,
            out_specs=out_specs,
            scratch_shapes=list(scratch),
        ),
        out_shape=outs,
        compiler_params=params(),
        cost_estimate=pl.CostEstimate(flops=flops, bytes_accessed=moved, transcendentals=0),
    )(scalars, *operands)


def shape(rows, columns, kind=bf16):
    return jax.ShapeDtypeStruct((rows, columns), kind)


def rows_of(block):
    return pl.ds(pl.multiple_of(block * BLOCK_ROWS, BLOCK_ROWS), BLOCK_ROWS)


def pack_kernel(s, q, k, v, logits, out, column):
    count = s[1]
    for b in range(MAXB):
        row = logits[0:1, b * BLOCK_ROWS : (b + 1) * BLOCK_ROWS].astype(f32)
        tall = jnp.broadcast_to(row, (BLOCK_ROWS, BLOCK_ROWS)).T
        lane = lax.broadcasted_iota(i32, (BLOCK_ROWS, HEAD_SIZE), 1)
        meta = jnp.where(lane < HEAD_SIZE // 2, tall, count.astype(f32)).astype(bf16)
        rows = slice(b * BLOCK_ROWS, (b + 1) * BLOCK_ROWS)
        out[rows, M_COL:] = meta
        column[rows, :] = meta
    out[:, 0:HALF_QUERY] = q[...]
    out[:, K_COL:V_COL] = k[...]
    out[:, V_COL:M_COL] = v[...]


def as_scalar(x):
    return jnp.max(x.astype(f32)).astype(i32)


def chip_counts(s, meta):
    own = s[1]
    other = as_scalar(meta[0:META_ROWS, HEAD_SIZE // 2 :])
    first = jnp.where(s[0] == 0, own, other)
    return first, own + other


def place_of(block, first, core):
    on_first = block < first
    slot = jnp.where(on_first, block, block - first)
    mine = jnp.where(on_first, 0, 1) == core
    return mine, slot


def chip_kernel(s, k, v, kr, vr, meta, *outs):
    first, live = chip_counts(s, meta)
    for b in range(CHIP_BLOCKS):
        mine, slot = place_of(b, first, s[0])
        rows = slice(b * BLOCK_ROWS, (b + 1) * BLOCK_ROWS)

        def copy(keys, vals):
            for h in range(LOCAL_HEADS):
                cols = slice(h * HEAD_SIZE, (h + 1) * HEAD_SIZE)
                outs[h][rows, 0:HEAD_SIZE] = keys[rows_of(slot), cols]
                outs[h][rows, HEAD_SIZE:] = vals[rows_of(slot), cols]

        @pl.when(jnp.logical_and(b < live, mine))
        def _():
            copy(k, v)

        @pl.when(jnp.logical_and(b < live, jnp.logical_not(mine)))
        def _():
            copy(kr, vr)

        @pl.when(b >= live)
        def _():
            for h in range(LOCAL_HEADS):
                outs[h][rows, :] = jnp.zeros((BLOCK_ROWS, 2 * HEAD_SIZE), bf16)

    for h in range(LOCAL_HEADS):
        outs[h][CHIP_ROWS:, :] = jnp.broadcast_to(live.astype(f32), (META_ROWS, 2 * HEAD_SIZE)).astype(bf16)


def attend_kernel(chips, chunk, has_prior, s, *refs):
    q, qr, cot, cotr, column, columnr = refs[:6]
    at = 6
    kv = refs[at : at + chips]
    at += chips
    prior = refs[at : at + chips] if has_prior else None
    at += chips if has_prior else 0
    branch, gate_part = refs[at : at + 2]
    at += 2
    dvs = refs[at : at + chips]
    at += chips
    kd, vd, qs, og, scores, probs, top, acc, dv = refs[at:]

    first, live = chip_counts(s, columnr)
    core = s[0]
    ones = jnp.ones((BLOCK_ROWS, HEAD_SIZE), bf16)
    vd[...] = jnp.zeros_like(vd)
    dv[...] = jnp.zeros_like(dv)

    held = [live] + [as_scalar(kv[d][CHIP_ROWS:, 0:HEAD_SIZE]) for d in range(1, chips)]
    starts = [None] * chips
    position = jnp.int32(0)
    for d in list(range(1, chips)) + [0]:
        starts[d] = position
        for b in range(CHIP_BLOCKS):

            @pl.when(b < held[d])
            def _(d=d, b=b, position=position):
                rows = slice(b * BLOCK_ROWS, (b + 1) * BLOCK_ROWS)
                to = rows_of(position + b)
                kd[to, :] = kv[d][rows, 0:HEAD_SIZE]
                vd[to, 0:HEAD_SIZE] = kv[d][rows, HEAD_SIZE:]
                vd[to, HEAD_SIZE:] = ones

        position = position + held[d]
    base = starts[0]
    scale = math.log2(math.e) / math.sqrt(HEAD_SIZE)
    tall = GROUP * BLOCK_ROWS

    def part(j):
        return pl.ds(pl.multiple_of(j * chunk, chunk), chunk)

    def one_block(b, _):
        mine, slot = place_of(b, first, core)
        here = rows_of(slot)

        @pl.when(mine)
        def _():
            for i in range(GROUP):
                qs[i * BLOCK_ROWS : (i + 1) * BLOCK_ROWS, :] = q[here, i * HEAD_SIZE : (i + 1) * HEAD_SIZE]

        @pl.when(jnp.logical_not(mine))
        def _():
            for i in range(GROUP):
                qs[i * BLOCK_ROWS : (i + 1) * BLOCK_ROWS, :] = qr[here, i * HEAD_SIZE : (i + 1) * HEAD_SIZE]

        t = base + b
        last = t * BLOCK_ROWS // chunk

        def score(j):
            return lax.dot_general(
                qs[...], kd[part(j), :], (((1,), (1,)), ((), ())), preferred_element_type=f32
            )

        x = score(last)
        key = last * chunk + lax.broadcasted_iota(i32, (BLOCK_ROWS, chunk), 1)
        row = t * BLOCK_ROWS + lax.broadcasted_iota(i32, (BLOCK_ROWS, chunk), 0)
        allowed = key <= row
        x = jnp.where(allowed[None], x.reshape(GROUP, BLOCK_ROWS, chunk), MASKED).reshape(tall, chunk)
        scores[last] = x
        top[...] = jnp.max(x, axis=1, keepdims=True)

        def more(j, _):
            x = score(j)
            scores[j] = x
            top[...] = jnp.maximum(top[...], jnp.max(x, axis=1, keepdims=True))
            return 0

        lax.fori_loop(0, last, more, 0)
        acc[...] = jnp.zeros_like(acc)

        def weigh(j, _):
            p = jnp.exp2((scores[j] - top[...]) * scale).astype(bf16)
            probs[j] = p
            acc[...] += jnp.dot(p, vd[part(j), :], preferred_element_type=f32)
            return 0

        lax.fori_loop(0, last + 1, weigh, 0)

        def finish(grad, col):
            logit = jnp.broadcast_to(col[here, 0:1].astype(f32), (BLOCK_ROWS, HEAD_SIZE))
            gate = 1.0 / (1.0 + jnp.exp(-logit))
            total = jnp.zeros((BLOCK_ROWS, HEAD_SIZE), f32)
            for i in range(GROUP):
                rows = slice(i * BLOCK_ROWS, (i + 1) * BLOCK_ROWS)
                cols = slice(i * HEAD_SIZE, (i + 1) * HEAD_SIZE)
                inverse = 1.0 / acc[rows, HEAD_SIZE:]
                attended = acc[rows, 0:HEAD_SIZE] * inverse
                branch[rows_of(b), cols] = (gate * attended).astype(bf16)
                g = grad[here, cols].astype(f32)
                total = total + g * attended
                og[rows, :] = (gate * g * inverse).astype(bf16)
            gate_part[rows_of(b), :] = total

        @pl.when(mine)
        def _():
            finish(cot, column)

        @pl.when(jnp.logical_not(mine))
        def _():
            finish(cotr, columnr)

        def back(j, _):
            dv[part(j), :] += lax.dot_general(
                probs[j], og[...], (((0,), (0,)), ((), ())), preferred_element_type=f32
            )
            return 0

        lax.fori_loop(0, last + 1, back, 0)
        return 0

    lax.fori_loop(0, live, one_block, 0)

    for b in range(CHIP_BLOCKS):
        rows = slice(b * BLOCK_ROWS, (b + 1) * BLOCK_ROWS)

        @pl.when(b >= live)
        def _():
            branch[rows, :] = jnp.zeros((BLOCK_ROWS, GROUP_WIDTH), bf16)
            gate_part[rows, :] = jnp.zeros((BLOCK_ROWS, HEAD_SIZE), f32)

        for d in range(chips):
            cols = slice(0, HEAD_SIZE)
            if has_prior:
                dvs[d][rows, 0:HEAD_SIZE] = prior[d][rows, :]
                cols = slice(HEAD_SIZE, 2 * HEAD_SIZE)

            @pl.when(b < held[d])
            def _():
                dvs[d][rows, cols] = dv[rows_of(starts[d] + b), :].astype(dvs[d].dtype)

            @pl.when(b >= held[d])
            def _():
                dvs[d][rows, cols] = jnp.zeros((BLOCK_ROWS, HEAD_SIZE), dvs[d].dtype)

    lane = lax.broadcasted_iota(i32, (META_ROWS, GROUP_WIDTH), 1)
    branch[CHIP_ROWS:, :] = jnp.where(lane < HEAD_SIZE // 2, first.astype(f32), (live - first).astype(f32)).astype(bf16)


def spread(slot, core, first, second, write, clear):
    held = jnp.where(core == 0, first, second)
    block = jnp.where(core == 0, slot, first + slot)

    @pl.when(slot < held)
    def _():
        write(rows_of(jnp.minimum(block, CHIP_BLOCKS - 1)))

    @pl.when(slot >= held)
    def _():
        clear()


def branch_kernel(s, *refs):
    parts = refs[:LOCAL_HEADS]
    mine, theirs = refs[LOCAL_HEADS:]
    first = as_scalar(parts[0][CHIP_ROWS:, 0 : HEAD_SIZE // 2])
    second = as_scalar(parts[0][CHIP_ROWS:, HEAD_SIZE // 2 : HEAD_SIZE])
    for out, core in ((mine, s[0]), (theirs, 1 - s[0])):
        for slot in range(MAXB):
            rows = slice(slot * BLOCK_ROWS, (slot + 1) * BLOCK_ROWS)

            def write(source):
                for h in range(LOCAL_HEADS):
                    out[rows, h * GROUP_WIDTH : (h + 1) * GROUP_WIDTH] = parts[h][source, :]

            def clear():
                out[rows, :] = jnp.zeros((BLOCK_ROWS, HALF_QUERY), bf16)

            spread(slot, core, first, second, write, clear)


def join_kernel(s, mine, theirs, out):
    @pl.when(s[0] == 0)
    def _():
        out[:, 0:HALF_QUERY] = mine[...]
        out[:, HALF_QUERY:] = theirs[...]

    @pl.when(s[0] != 0)
    def _():
        out[:, 0:HALF_QUERY] = theirs[...]
        out[:, HALF_QUERY:] = mine[...]


def gradient_kernel(chips, s, *refs):
    columnr = refs[0]
    own = refs[1]
    arrived = refs[2 : 1 + chips]
    gate_parts = refs[1 + chips : 1 + chips + LOCAL_HEADS]
    mine, gate_mine, theirs = refs[1 + chips + LOCAL_HEADS :]
    first, live = chip_counts(s, columnr)
    second = live - first
    for which, core in ((0, s[0]), (1, 1 - s[0])):
        for slot in range(MAXB):
            rows = slice(slot * BLOCK_ROWS, (slot + 1) * BLOCK_ROWS)

            def write(source):
                total = own[source, :]
                for other in arrived:
                    total = total + other[source, :].astype(f32)
                summed = gate_parts[0][source, :]
                for h in range(1, LOCAL_HEADS):
                    summed = summed + gate_parts[h][source, :]
                summed = jnp.broadcast_to(jnp.sum(summed, axis=1, keepdims=True), (BLOCK_ROWS, HEAD_SIZE))
                if which == 0:
                    mine[rows, :] = total.astype(bf16)
                    gate_mine[rows, :] = summed
                else:
                    theirs[rows, 0:HALF_KEY] = total.astype(bf16)
                    high = summed.astype(bf16)
                    low = (summed - high.astype(f32)).astype(bf16)
                    lane = lax.broadcasted_iota(i32, (BLOCK_ROWS, HEAD_SIZE), 1)
                    theirs[rows, HALF_KEY:] = jnp.where(lane < HEAD_SIZE // 2, high, low)

            def clear():
                if which == 0:
                    mine[rows, :] = jnp.zeros((BLOCK_ROWS, HALF_KEY), bf16)
                    gate_mine[rows, :] = jnp.zeros((BLOCK_ROWS, HEAD_SIZE), f32)
                else:
                    theirs[rows, :] = jnp.zeros((BLOCK_ROWS, HALF_KEY + HEAD_SIZE), bf16)

            spread(slot, core, first, second, write, clear)


def finish_kernel(s, mine, gate_mine, theirs, column, out, gate_out):
    @pl.when(s[0] == 0)
    def _():
        out[:, 0:HALF_KEY] = mine[...]
        out[:, HALF_KEY:] = theirs[:, 0:HALF_KEY]

    @pl.when(s[0] != 0)
    def _():
        out[:, 0:HALF_KEY] = theirs[:, 0:HALF_KEY]
        out[:, HALF_KEY:] = mine[...]

    half = HALF_KEY + HEAD_SIZE // 2
    for b in range(MAXB):
        rows = slice(b * BLOCK_ROWS, (b + 1) * BLOCK_ROWS)
        total = (
            gate_mine[rows, 0:1]
            + theirs[rows, HALF_KEY : HALF_KEY + 1].astype(f32)
            + theirs[rows, half : half + 1].astype(f32)
        )
        logit = column[rows, 0:1].astype(f32)
        gate = 1.0 / (1.0 + jnp.exp(-logit))
        full = jnp.broadcast_to(gate * (1.0 - gate) * total, (BLOCK_ROWS, HEAD_SIZE)).T
        gate_out[0:1, rows] = full[0:1, :].astype(bf16)


def local(queries, keys, values, cotangent, router_logits, positions, counts):
    shards = lax.axis_size("ctx")
    sections = lax.axis_size("section")
    chips = shards // CORES
    core = lax.axis_index("ctx") % CORES
    scalars = jnp.stack([core.astype(i32), counts[0, 0]])
    q, k, v, cot = queries[0], keys[0], values[0], cotangent[0]

    def swap(x):
        return lax.ppermute(x, "ctx", [(i, i ^ 1) for i in range(shards)])

    def onward(x, by):
        step = by * CORES
        return lax.ppermute(x, "ctx", [(i, i + step) for i in range(shards) if 0 <= i + step < shards])

    def section_on(x):
        return lax.ppermute(x, "section", [(i, (i + 1) % sections) for i in range(sections)])

    def half_of(width, mine=True):
        return pl.BlockSpec((SLOTS, width), lambda i, s: (0, s[0] if mine else 1 - s[0]))

    def fixed(width, at):
        return pl.BlockSpec((SLOTS, width), lambda i, s: (0, at))

    column_spec = fixed(HEAD_SIZE, M_COL // HEAD_SIZE)
    payload, column = call(
        pack_kernel,
        scalars,
        [half_of(HALF_QUERY, False), half_of(HALF_KEY, False), half_of(HALF_KEY, False), whole((1, SLOTS))],
        (q, k, v, router_logits),
        (shape(SLOTS, PAYLOAD), shape(SLOTS, HEAD_SIZE)),
        (whole((SLOTS, PAYLOAD)), whole((SLOTS, HEAD_SIZE))),
        moved=2 * SLOTS * PAYLOAD * 2,
    )
    other = swap(payload)
    cot_other = swap(lax.dynamic_slice_in_dim(cot, (1 - core) * HALF_QUERY, HALF_QUERY, 1))
    packed_rows = CHIP_ROWS + META_ROWS
    packed = call(
        chip_kernel,
        scalars,
        [
            half_of(HALF_KEY),
            half_of(HALF_KEY),
            fixed(HALF_KEY, K_COL // HALF_KEY),
            fixed(HALF_KEY, V_COL // HALF_KEY),
            column_spec,
        ],
        (k, v, other, other, other),
        tuple(shape(packed_rows, 2 * HEAD_SIZE) for _ in range(LOCAL_HEADS)),
        tuple(whole((packed_rows, 2 * HEAD_SIZE)) for _ in range(LOCAL_HEADS)),
        moved=4 * packed_rows * HALF_KEY * 2,
    )
    gathered = [[packed[h]] + [onward(packed[h], d) for d in range(1, chips)] for h in range(LOCAL_HEADS)]

    chunk = min(4, shards) * BLOCK_ROWS
    steps = -(-shards * BLOCK_ROWS // chunk)
    reach = steps * chunk
    tall = GROUP * BLOCK_ROWS
    prior = []
    branches, gate_parts = [], []
    for h in range(LOCAL_HEADS):
        width = HEAD_SIZE * (2 if prior else 1)
        own_at = pl.BlockSpec((SLOTS, GROUP_WIDTH), lambda i, s, h=h: (0, s[0] * LOCAL_HEADS + h))
        results = call(
            lambda *refs, prior=bool(prior): attend_kernel(chips, chunk, prior, *refs),
            scalars,
            [own_at, fixed(GROUP_WIDTH, h), own_at, fixed(GROUP_WIDTH, h), whole((SLOTS, HEAD_SIZE)), column_spec]
            + [whole((packed_rows, 2 * HEAD_SIZE))] * chips
            + [whole((CHIP_ROWS, HEAD_SIZE)) for _ in prior],
            (q, other, cot, cot_other, column, other, *gathered[h], *prior),
            (shape(packed_rows, GROUP_WIDTH), shape(CHIP_ROWS, HEAD_SIZE, f32), shape(CHIP_ROWS, width, f32))
            + tuple(shape(CHIP_ROWS, width) for _ in range(chips - 1)),
            (whole((packed_rows, GROUP_WIDTH)), whole((CHIP_ROWS, HEAD_SIZE)))
            + (whole((CHIP_ROWS, width)),) * chips,
            scratch=(
                pltpu.VMEM((reach, HEAD_SIZE), bf16),
                pltpu.VMEM((reach, 2 * HEAD_SIZE), bf16),
                pltpu.VMEM((tall, HEAD_SIZE), bf16),
                pltpu.VMEM((tall, HEAD_SIZE), bf16),
                pltpu.VMEM((steps, tall, chunk), f32),
                pltpu.VMEM((steps, tall, chunk), bf16),
                pltpu.VMEM((tall, 1), f32),
                pltpu.VMEM((tall, 2 * HEAD_SIZE), f32),
                pltpu.VMEM((reach, HEAD_SIZE), f32),
            ),
            flops=12 * tall * HEAD_SIZE * reach,
            moved=6 * packed_rows * GROUP_WIDTH,
        )
        branches.append(section_on(results[0]))
        gate_parts.append(results[1])
        prior = results[2:]
    returned = [onward(prior[d], -d) for d in range(1, chips)]
    grad_mine, gate_mine, grad_theirs = call(
        lambda *refs: gradient_kernel(chips, *refs),
        scalars,
        [column_spec]
        + [whole((CHIP_ROWS, HALF_KEY))] * chips
        + [whole((CHIP_ROWS, HEAD_SIZE))] * LOCAL_HEADS,
        (other, prior[0], *returned, *gate_parts),
        (shape(SLOTS, HALF_KEY), shape(SLOTS, HEAD_SIZE, f32), shape(SLOTS, HALF_KEY + HEAD_SIZE)),
        (whole((SLOTS, HALF_KEY)), whole((SLOTS, HEAD_SIZE)), whole((SLOTS, HALF_KEY + HEAD_SIZE))),
        moved=8 * CHIP_ROWS * HALF_KEY,
    )
    grad_other = swap(grad_theirs)
    value_grad, gate_grad = call(
        finish_kernel,
        scalars,
        [
            whole((SLOTS, HALF_KEY)),
            whole((SLOTS, HEAD_SIZE)),
            whole((SLOTS, HALF_KEY + HEAD_SIZE)),
            whole((SLOTS, HEAD_SIZE)),
        ],
        (grad_mine, gate_mine, grad_other, column),
        (shape(SLOTS, CORES * HALF_KEY), shape(1, SLOTS)),
        (whole((SLOTS, CORES * HALF_KEY)), whole((1, SLOTS))),
        moved=8 * SLOTS * HALF_KEY,
    )
    branch_mine, branch_theirs = call(
        branch_kernel,
        scalars,
        [whole((packed_rows, GROUP_WIDTH))] * LOCAL_HEADS,
        tuple(branches),
        (shape(SLOTS, HALF_QUERY), shape(SLOTS, HALF_QUERY)),
        (whole((SLOTS, HALF_QUERY)), whole((SLOTS, HALF_QUERY))),
        moved=7 * SLOTS * HALF_QUERY,
    )
    branch_other = swap(branch_theirs)
    handed = call(
        join_kernel,
        scalars,
        [whole((SLOTS, HALF_QUERY))] * 2,
        (branch_mine, branch_other),
        shape(SLOTS, CORES * HALF_QUERY),
        whole((SLOTS, CORES * HALF_QUERY)),
        moved=8 * SLOTS * HALF_QUERY,
    )
    return (handed[None], value_grad[None], gate_grad)


def solution(mesh):
    rows = P("section", "ctx", None)
    flat = P("section", "ctx")
    return jax.shard_map(
        local,
        mesh=mesh,
        in_specs=(rows, rows, rows, rows, flat, flat, flat),
        out_specs=(rows, rows, flat),
        check_vma=False,
    )
```

```python
import math

import jax
import jax.numpy as jnp
from jax import lax
from jax.experimental import pallas as pl
from jax.experimental.pallas import tpu as pltpu
from jax.sharding import PartitionSpec as P

QUERY_HEADS = 24
KEY_VALUE_HEADS = 4
HEAD_SIZE = 128
BLOCK_ROWS = 128
MAXB = 2

CORES = 2
GROUP = QUERY_HEADS // KEY_VALUE_HEADS
LOCAL_HEADS = KEY_VALUE_HEADS // CORES
GROUP_WIDTH = GROUP * HEAD_SIZE
HALF_QUERY = LOCAL_HEADS * GROUP_WIDTH
HALF_KEY = LOCAL_HEADS * HEAD_SIZE
CHIP_BLOCKS = 2 * MAXB - 1
CHIP_ROWS = CHIP_BLOCKS * BLOCK_ROWS
META_ROWS = 16
SLOTS = MAXB * BLOCK_ROWS
MASKED = -1e30
VMEM_LIMIT = 48 * 1024 * 1024
f32 = jnp.float32
bf16 = jnp.bfloat16
i32 = jnp.int32
K_COL = HALF_QUERY
V_COL = HALF_QUERY + HALF_KEY
M_COL = HALF_QUERY + 2 * HALF_KEY
PAYLOAD = M_COL + HEAD_SIZE


def params(limit):
    return pltpu.CompilerParams(vmem_limit_bytes=limit)


def whole(shape):
    return pl.BlockSpec(shape, lambda i, s: (0,) * len(shape))


def call(body, scalars, grid_in, operands, outs, out_specs, scratch=(), flops=0, moved=0, limit=VMEM_LIMIT):
    return pl.pallas_call(
        body,
        grid_spec=pltpu.PrefetchScalarGridSpec(
            num_scalar_prefetch=1,
            grid=(1,),
            in_specs=grid_in,
            out_specs=out_specs,
            scratch_shapes=list(scratch),
        ),
        out_shape=outs,
        compiler_params=params(limit),
        cost_estimate=pl.CostEstimate(flops=flops, bytes_accessed=moved, transcendentals=0),
    )(scalars, *operands)


def shape(rows, columns, kind=bf16):
    return jax.ShapeDtypeStruct((rows, columns), kind)


def rows_of(block):
    return pl.ds(pl.multiple_of(block * BLOCK_ROWS, BLOCK_ROWS), BLOCK_ROWS)


def pack_kernel(s, q, k, v, logits, out, column, own, arrived):
    count = s[1]

    def half(source, width, core):
        return source.at[:, pl.ds(pl.multiple_of(core * width, width), width)]

    copies = [
        pltpu.make_async_copy(half(source, width, core), target, arrived.at[n])
        for n, (source, width, core, target) in enumerate(
            (
                (q, HALF_QUERY, 1 - s[0], out.at[:, 0:K_COL]),
                (k, HALF_KEY, 1 - s[0], out.at[:, K_COL:V_COL]),
                (v, HALF_KEY, 1 - s[0], out.at[:, V_COL:M_COL]),
                (k, HALF_KEY, s[0], own.at[:, 0:HALF_KEY]),
                (v, HALF_KEY, s[0], own.at[:, HALF_KEY:]),
            )
        )
    ]
    for copy in copies:
        copy.start()
    for b in range(MAXB):
        row = logits[0:1, b * BLOCK_ROWS : (b + 1) * BLOCK_ROWS].astype(f32)
        tall = jnp.broadcast_to(row, (BLOCK_ROWS, BLOCK_ROWS)).T
        lane = lax.broadcasted_iota(i32, (BLOCK_ROWS, HEAD_SIZE), 1)
        meta = jnp.where(lane < HEAD_SIZE // 2, tall, count.astype(f32)).astype(bf16)
        rows = slice(b * BLOCK_ROWS, (b + 1) * BLOCK_ROWS)
        out[rows, M_COL:] = meta
        column[rows, :] = meta
    for copy in copies:
        copy.wait()


def as_scalar(x):
    return jnp.max(x.astype(f32)).astype(i32)


def chip_counts(s, meta):
    own = s[1]
    other = as_scalar(meta[0:META_ROWS, HEAD_SIZE // 2 :])
    first = jnp.where(s[0] == 0, own, other)
    return first, own + other


def place_of(block, first, core):
    on_first = block < first
    slot = jnp.where(on_first, block, block - first)
    mine = jnp.where(on_first, 0, 1) == core
    return mine, slot


def chip_kernel(s, k, v, kr, vr, meta, *outs):
    first, live = chip_counts(s, meta)
    for b in range(CHIP_BLOCKS):
        mine, slot = place_of(b, first, s[0])
        rows = slice(b * BLOCK_ROWS, (b + 1) * BLOCK_ROWS)

        def copy(keys, vals):
            for h in range(LOCAL_HEADS):
                cols = slice(h * HEAD_SIZE, (h + 1) * HEAD_SIZE)
                outs[h][rows, 0:HEAD_SIZE] = keys[rows_of(slot), cols]
                outs[h][rows, HEAD_SIZE:] = vals[rows_of(slot), cols]

        @pl.when(jnp.logical_and(b < live, mine))
        def _():
            copy(k, v)

        @pl.when(jnp.logical_and(b < live, jnp.logical_not(mine)))
        def _():
            copy(kr, vr)

        @pl.when(b >= live)
        def _():
            for h in range(LOCAL_HEADS):
                outs[h][rows, :] = jnp.zeros((BLOCK_ROWS, 2 * HEAD_SIZE), bf16)

    for h in range(LOCAL_HEADS):
        outs[h][CHIP_ROWS:, :] = jnp.broadcast_to(live.astype(f32), (META_ROWS, 2 * HEAD_SIZE)).astype(bf16)


def attend_kernel(chips, chunk, has_prior, s, *refs):
    q, qr, cot, cotr, column, columnr = refs[:6]
    at = 6
    kv = refs[at : at + chips]
    at += chips
    prior = refs[at : at + chips] if has_prior else None
    at += chips if has_prior else 0
    branch, gate_part = refs[at : at + 2]
    at += 2
    dvs = refs[at : at + chips]
    at += chips
    kd, vd, qs, og, scores, probs, top, acc, dv = refs[at:]

    first, live = chip_counts(s, columnr)
    core = s[0]
    ones = jnp.ones((BLOCK_ROWS, HEAD_SIZE), bf16)
    vd[...] = jnp.zeros_like(vd)
    dv[...] = jnp.zeros_like(dv)

    held = [live] + [as_scalar(kv[d][CHIP_ROWS:, 0:HEAD_SIZE]) for d in range(1, chips)]
    starts = [None] * chips
    position = jnp.int32(0)
    for d in list(range(1, chips)) + [0]:
        starts[d] = position
        for b in range(CHIP_BLOCKS):

            @pl.when(b < held[d])
            def _(d=d, b=b, position=position):
                rows = slice(b * BLOCK_ROWS, (b + 1) * BLOCK_ROWS)
                to = rows_of(position + b)
                kd[to, :] = kv[d][rows, 0:HEAD_SIZE]
                vd[to, 0:HEAD_SIZE] = kv[d][rows, HEAD_SIZE:]
                vd[to, HEAD_SIZE:] = ones

        position = position + held[d]
    base = starts[0]
    scale = math.log2(math.e) / math.sqrt(HEAD_SIZE)
    tall = GROUP * BLOCK_ROWS

    def part(j):
        return pl.ds(pl.multiple_of(j * chunk, chunk), chunk)

    def one_block(b, _):
        mine, slot = place_of(b, first, core)
        here = rows_of(slot)

        @pl.when(mine)
        def _():
            for i in range(GROUP):
                qs[i * BLOCK_ROWS : (i + 1) * BLOCK_ROWS, :] = q[here, i * HEAD_SIZE : (i + 1) * HEAD_SIZE]

        @pl.when(jnp.logical_not(mine))
        def _():
            for i in range(GROUP):
                qs[i * BLOCK_ROWS : (i + 1) * BLOCK_ROWS, :] = qr[here, i * HEAD_SIZE : (i + 1) * HEAD_SIZE]

        t = base + b
        last = t * BLOCK_ROWS // chunk

        def score(j):
            return lax.dot_general(
                qs[...], kd[part(j), :], (((1,), (1,)), ((), ())), preferred_element_type=f32
            )

        x = score(last)
        key = last * chunk + lax.broadcasted_iota(i32, (BLOCK_ROWS, chunk), 1)
        row = t * BLOCK_ROWS + lax.broadcasted_iota(i32, (BLOCK_ROWS, chunk), 0)
        allowed = key <= row
        x = jnp.where(allowed[None], x.reshape(GROUP, BLOCK_ROWS, chunk), MASKED).reshape(tall, chunk)
        scores[last] = x
        top[...] = jnp.max(x, axis=1, keepdims=True)

        def more(j, _):
            x = score(j)
            scores[j] = x
            top[...] = jnp.maximum(top[...], jnp.max(x, axis=1, keepdims=True))
            return 0

        lax.fori_loop(0, last, more, 0)
        acc[...] = jnp.zeros_like(acc)

        def weigh(j, _):
            p = jnp.exp2((scores[j] - top[...]) * scale).astype(bf16)
            probs[j] = p
            acc[...] += jnp.dot(p, vd[part(j), :], preferred_element_type=f32)
            return 0

        lax.fori_loop(0, last + 1, weigh, 0)

        def finish(grad, col):
            logit = jnp.broadcast_to(col[here, 0:1].astype(f32), (BLOCK_ROWS, HEAD_SIZE))
            gate = 1.0 / (1.0 + jnp.exp(-logit))
            total = jnp.zeros((BLOCK_ROWS, HEAD_SIZE), f32)
            for i in range(GROUP):
                rows = slice(i * BLOCK_ROWS, (i + 1) * BLOCK_ROWS)
                cols = slice(i * HEAD_SIZE, (i + 1) * HEAD_SIZE)
                inverse = 1.0 / acc[rows, HEAD_SIZE:]
                attended = acc[rows, 0:HEAD_SIZE] * inverse
                branch[rows_of(b), cols] = (gate * attended).astype(bf16)
                g = grad[here, cols].astype(f32)
                total = total + g * attended
                og[rows, :] = (gate * g * inverse).astype(bf16)
            gate_part[rows_of(b), :] = total

        @pl.when(mine)
        def _():
            finish(cot, column)

        @pl.when(jnp.logical_not(mine))
        def _():
            finish(cotr, columnr)

        def back(j, _):
            dv[part(j), :] += lax.dot_general(
                probs[j], og[...], (((0,), (0,)), ((), ())), preferred_element_type=f32
            )
            return 0

        lax.fori_loop(0, last + 1, back, 0)
        return 0

    lax.fori_loop(0, live, one_block, 0)

    for b in range(CHIP_BLOCKS):
        rows = slice(b * BLOCK_ROWS, (b + 1) * BLOCK_ROWS)

        @pl.when(b >= live)
        def _():
            branch[rows, :] = jnp.zeros((BLOCK_ROWS, GROUP_WIDTH), bf16)
            gate_part[rows, :] = jnp.zeros((BLOCK_ROWS, HEAD_SIZE), f32)

        for d in range(chips):
            cols = slice(0, HEAD_SIZE)
            if has_prior:
                dvs[d][rows, 0:HEAD_SIZE] = prior[d][rows, :]
                cols = slice(HEAD_SIZE, 2 * HEAD_SIZE)

            @pl.when(b < held[d])
            def _():
                dvs[d][rows, cols] = dv[rows_of(starts[d] + b), :].astype(dvs[d].dtype)

            @pl.when(b >= held[d])
            def _():
                dvs[d][rows, cols] = jnp.zeros((BLOCK_ROWS, HEAD_SIZE), dvs[d].dtype)

    lane = lax.broadcasted_iota(i32, (META_ROWS, GROUP_WIDTH), 1)
    branch[CHIP_ROWS:, :] = jnp.where(lane < HEAD_SIZE // 2, first.astype(f32), (live - first).astype(f32)).astype(bf16)


def spread(slot, core, first, second, write, clear):
    held = jnp.where(core == 0, first, second)
    block = jnp.where(core == 0, slot, first + slot)

    @pl.when(slot < held)
    def _():
        write(rows_of(jnp.minimum(block, CHIP_BLOCKS - 1)))

    @pl.when(slot >= held)
    def _():
        clear()


def branch_kernel(s, part, mine, theirs):
    first = as_scalar(part[CHIP_ROWS:, 0 : HEAD_SIZE // 2])
    second = as_scalar(part[CHIP_ROWS:, HEAD_SIZE // 2 : HEAD_SIZE])
    for out, core in ((mine, s[0]), (theirs, 1 - s[0])):
        for slot in range(MAXB):
            rows = slice(slot * BLOCK_ROWS, (slot + 1) * BLOCK_ROWS)

            def write(source):
                out[rows, :] = part[source, :]

            def clear():
                out[rows, :] = jnp.zeros((BLOCK_ROWS, GROUP_WIDTH), bf16)

            spread(slot, core, first, second, write, clear)


def join_kernel(s, *refs):
    mine, theirs, out = refs[:LOCAL_HEADS], refs[LOCAL_HEADS:-1], refs[-1]
    for core in range(CORES):

        @pl.when(s[0] == core)
        def _():
            for h in range(LOCAL_HEADS):
                for at, part in ((core, mine[h]), (1 - core, theirs[h])):
                    start = at * HALF_QUERY + h * GROUP_WIDTH
                    out[:, start : start + GROUP_WIDTH] = part[...]


def gradient_kernel(chips, s, *refs):
    columnr = refs[0]
    own = refs[1]
    arrived = refs[2 : 1 + chips]
    gate_parts = refs[1 + chips : 1 + chips + LOCAL_HEADS]
    mine, gate_mine, theirs = refs[1 + chips + LOCAL_HEADS :]
    first, live = chip_counts(s, columnr)
    second = live - first
    for which, core in ((0, s[0]), (1, 1 - s[0])):
        for slot in range(MAXB):
            rows = slice(slot * BLOCK_ROWS, (slot + 1) * BLOCK_ROWS)

            def write(source):
                total = own[source, :]
                for other in arrived:
                    total = total + other[source, :].astype(f32)
                summed = gate_parts[0][source, :]
                for h in range(1, LOCAL_HEADS):
                    summed = summed + gate_parts[h][source, :]
                summed = jnp.broadcast_to(jnp.sum(summed, axis=1, keepdims=True), (BLOCK_ROWS, HEAD_SIZE))
                if which == 0:
                    mine[rows, :] = total.astype(bf16)
                    gate_mine[rows, :] = summed
                else:
                    theirs[rows, 0:HALF_KEY] = total.astype(bf16)
                    high = summed.astype(bf16)
                    low = (summed - high.astype(f32)).astype(bf16)
                    lane = lax.broadcasted_iota(i32, (BLOCK_ROWS, HEAD_SIZE), 1)
                    theirs[rows, HALF_KEY:] = jnp.where(lane < HEAD_SIZE // 2, high, low)

            def clear():
                if which == 0:
                    mine[rows, :] = jnp.zeros((BLOCK_ROWS, HALF_KEY), bf16)
                    gate_mine[rows, :] = jnp.zeros((BLOCK_ROWS, HEAD_SIZE), f32)
                else:
                    theirs[rows, :] = jnp.zeros((BLOCK_ROWS, HALF_KEY + HEAD_SIZE), bf16)

            spread(slot, core, first, second, write, clear)


def finish_kernel(s, mine, gate_mine, theirs, column, out, gate_out):
    @pl.when(s[0] == 0)
    def _():
        out[:, 0:HALF_KEY] = mine[...]
        out[:, HALF_KEY:] = theirs[:, 0:HALF_KEY]

    @pl.when(s[0] != 0)
    def _():
        out[:, 0:HALF_KEY] = theirs[:, 0:HALF_KEY]
        out[:, HALF_KEY:] = mine[...]

    half = HALF_KEY + HEAD_SIZE // 2
    for b in range(MAXB):
        rows = slice(b * BLOCK_ROWS, (b + 1) * BLOCK_ROWS)
        total = (
            gate_mine[rows, 0:1]
            + theirs[rows, HALF_KEY : HALF_KEY + 1].astype(f32)
            + theirs[rows, half : half + 1].astype(f32)
        )
        logit = column[rows, 0:1].astype(f32)
        gate = 1.0 / (1.0 + jnp.exp(-logit))
        full = jnp.broadcast_to(gate * (1.0 - gate) * total, (BLOCK_ROWS, HEAD_SIZE)).T
        gate_out[0:1, rows] = full[0:1, :].astype(bf16)


def local(queries, keys, values, cotangent, router_logits, positions, counts):
    shards = lax.axis_size("ctx")
    sections = lax.axis_size("section")
    chips = shards // CORES
    core = lax.axis_index("ctx") % CORES
    scalars = jnp.stack([core.astype(i32), counts[0, 0]])
    q, k, v, cot = queries[0], keys[0], values[0], cotangent[0]

    def swap(x):
        return lax.ppermute(x, "ctx", [(i, i ^ 1) for i in range(shards)])

    def onward(x, by):
        step = by * CORES
        return lax.ppermute(x, "ctx", [(i, i + step) for i in range(shards) if 0 <= i + step < shards])

    def section_on(x):
        return lax.ppermute(x, "section", [(i, (i + 1) % sections) for i in range(sections)])

    def fixed(width, at):
        return pl.BlockSpec((SLOTS, width), lambda i, s: (0, at))

    column_spec = fixed(HEAD_SIZE, M_COL // HEAD_SIZE)
    far = pl.BlockSpec(memory_space=pltpu.HBM)
    payload, column, own_kv = call(
        pack_kernel,
        scalars,
        [far, far, far, whole((1, SLOTS))],
        (q, k, v, router_logits),
        (shape(SLOTS, PAYLOAD), shape(SLOTS, HEAD_SIZE), shape(SLOTS, 2 * HALF_KEY)),
        (whole((SLOTS, PAYLOAD)), whole((SLOTS, HEAD_SIZE)), whole((SLOTS, 2 * HALF_KEY))),
        scratch=(pltpu.SemaphoreType.DMA((5,)),),
        limit=62 * 1024 * 1024,
        moved=2 * SLOTS * PAYLOAD * 2,
    )
    other = swap(payload)
    cot_other = swap(lax.dynamic_slice_in_dim(cot, (1 - core) * HALF_QUERY, HALF_QUERY, 1))
    packed_rows = CHIP_ROWS + META_ROWS
    packed = call(
        chip_kernel,
        scalars,
        [
            fixed(HALF_KEY, 0),
            fixed(HALF_KEY, 1),
            fixed(HALF_KEY, K_COL // HALF_KEY),
            fixed(HALF_KEY, V_COL // HALF_KEY),
            column_spec,
        ],
        (own_kv, own_kv, other, other, other),
        tuple(shape(packed_rows, 2 * HEAD_SIZE) for _ in range(LOCAL_HEADS)),
        tuple(whole((packed_rows, 2 * HEAD_SIZE)) for _ in range(LOCAL_HEADS)),
        moved=4 * packed_rows * HALF_KEY * 2,
    )
    gathered = [[packed[h]] + [onward(packed[h], d) for d in range(1, chips)] for h in range(LOCAL_HEADS)]

    chunk = min(4, shards) * BLOCK_ROWS
    steps = -(-shards * BLOCK_ROWS // chunk)
    reach = steps * chunk
    tall = GROUP * BLOCK_ROWS
    prior = []
    branches, gate_parts = [], []
    for h in range(LOCAL_HEADS):
        width = HEAD_SIZE * (2 if prior else 1)
        own_at = pl.BlockSpec((SLOTS, GROUP_WIDTH), lambda i, s, h=h: (0, s[0] * LOCAL_HEADS + h))
        results = call(
            lambda *refs, prior=bool(prior): attend_kernel(chips, chunk, prior, *refs),
            scalars,
            [own_at, fixed(GROUP_WIDTH, h), own_at, fixed(GROUP_WIDTH, h), whole((SLOTS, HEAD_SIZE)), column_spec]
            + [whole((packed_rows, 2 * HEAD_SIZE))] * chips
            + [whole((CHIP_ROWS, HEAD_SIZE)) for _ in prior],
            (q, other, cot, cot_other, column, other, *gathered[h], *prior),
            (shape(packed_rows, GROUP_WIDTH), shape(CHIP_ROWS, HEAD_SIZE, f32), shape(CHIP_ROWS, width, f32))
            + tuple(shape(CHIP_ROWS, width) for _ in range(chips - 1)),
            (whole((packed_rows, GROUP_WIDTH)), whole((CHIP_ROWS, HEAD_SIZE)))
            + (whole((CHIP_ROWS, width)),) * chips,
            scratch=(
                pltpu.VMEM((reach, HEAD_SIZE), bf16),
                pltpu.VMEM((reach, 2 * HEAD_SIZE), bf16),
                pltpu.VMEM((tall, HEAD_SIZE), bf16),
                pltpu.VMEM((tall, HEAD_SIZE), bf16),
                pltpu.VMEM((steps, tall, chunk), f32),
                pltpu.VMEM((steps, tall, chunk), bf16),
                pltpu.VMEM((tall, 1), f32),
                pltpu.VMEM((tall, 2 * HEAD_SIZE), f32),
                pltpu.VMEM((reach, HEAD_SIZE), f32),
            ),
            flops=100 * tall * HEAD_SIZE * reach,
            moved=6 * packed_rows * GROUP_WIDTH,
        )
        branches.append(section_on(results[0]))
        gate_parts.append(results[1])
        prior = results[2:]
    returned = [onward(prior[d], -d) for d in range(1, chips)]
    branches[0], *returned = lax.optimization_barrier((branches[0], *returned))
    grad_mine, gate_mine, grad_theirs = call(
        lambda *refs: gradient_kernel(chips, *refs),
        scalars,
        [column_spec]
        + [whole((CHIP_ROWS, HALF_KEY))] * chips
        + [whole((CHIP_ROWS, HEAD_SIZE))] * LOCAL_HEADS,
        (other, prior[0], *returned, *gate_parts),
        (shape(SLOTS, HALF_KEY), shape(SLOTS, HEAD_SIZE, f32), shape(SLOTS, HALF_KEY + HEAD_SIZE)),
        (whole((SLOTS, HALF_KEY)), whole((SLOTS, HEAD_SIZE)), whole((SLOTS, HALF_KEY + HEAD_SIZE))),
        moved=8 * CHIP_ROWS * HALF_KEY,
    )
    grad_other = swap(grad_theirs)
    value_grad, gate_grad = call(
        finish_kernel,
        scalars,
        [
            whole((SLOTS, HALF_KEY)),
            whole((SLOTS, HEAD_SIZE)),
            whole((SLOTS, HALF_KEY + HEAD_SIZE)),
            whole((SLOTS, HEAD_SIZE)),
        ],
        (grad_mine, gate_mine, grad_other, column),
        (shape(SLOTS, CORES * HALF_KEY), shape(1, SLOTS)),
        (whole((SLOTS, CORES * HALF_KEY)), whole((1, SLOTS))),
        moved=8 * SLOTS * HALF_KEY,
    )
    branches[-1], value_grad = lax.optimization_barrier((branches[-1], value_grad))
    mine, theirs = [], []
    for h in range(LOCAL_HEADS):
        kept, sent = call(
            branch_kernel,
            scalars,
            [whole((packed_rows, GROUP_WIDTH))],
            (branches[h],),
            (shape(SLOTS, GROUP_WIDTH), shape(SLOTS, GROUP_WIDTH)),
            (whole((SLOTS, GROUP_WIDTH)), whole((SLOTS, GROUP_WIDTH))),
            moved=7 * SLOTS * HALF_QUERY,
        )
        mine.append(kept)
        theirs.append(swap(sent))
    handed = call(
        join_kernel,
        scalars,
        [whole((SLOTS, GROUP_WIDTH))] * (2 * LOCAL_HEADS),
        (*mine, *theirs),
        shape(SLOTS, CORES * HALF_QUERY),
        whole((SLOTS, CORES * HALF_QUERY)),
        moved=8 * SLOTS * HALF_QUERY,
    )
    return (handed[None], value_grad[None], gate_grad)


def solution(mesh):
    rows = P("section", "ctx", None)
    flat = P("section", "ctx")
    return jax.shard_map(
        local,
        mesh=mesh,
        in_specs=(rows, rows, rows, rows, flat, flat, flat),
        out_specs=(rows, rows, flat),
        check_vma=False,
    )
```

```python
import math

import jax
import jax.numpy as jnp
from jax import lax
from jax.experimental import pallas as pl
from jax.experimental.pallas import tpu as pltpu
from jax.sharding import PartitionSpec as P

QUERY_HEADS = 24
KEY_VALUE_HEADS = 4
HEAD_SIZE = 128
BLOCK_ROWS = 128
MAXB = 2

CORES = 2
GROUP = QUERY_HEADS // KEY_VALUE_HEADS
LOCAL_HEADS = KEY_VALUE_HEADS // CORES
GROUP_WIDTH = GROUP * HEAD_SIZE
HALF_QUERY = LOCAL_HEADS * GROUP_WIDTH
HALF_KEY = LOCAL_HEADS * HEAD_SIZE
CHIP_BLOCKS = 2 * MAXB - 1
CHIP_ROWS = CHIP_BLOCKS * BLOCK_ROWS
META_ROWS = 16
SLOTS = MAXB * BLOCK_ROWS
MASKED = -1e30
VMEM_LIMIT = 48 * 1024 * 1024
f32 = jnp.float32
bf16 = jnp.bfloat16
i32 = jnp.int32
K_COL = HALF_QUERY
V_COL = HALF_QUERY + HALF_KEY
M_COL = HALF_QUERY + 2 * HALF_KEY
PAYLOAD = M_COL + HEAD_SIZE


def params(limit):
    return pltpu.CompilerParams(vmem_limit_bytes=limit)


def whole(shape):
    return pl.BlockSpec(shape, lambda i, s: (0,) * len(shape))


def call(body, scalars, grid_in, operands, outs, out_specs, scratch=(), flops=0, moved=0, limit=VMEM_LIMIT):
    return pl.pallas_call(
        body,
        grid_spec=pltpu.PrefetchScalarGridSpec(
            num_scalar_prefetch=1,
            grid=(1,),
            in_specs=grid_in,
            out_specs=out_specs,
            scratch_shapes=list(scratch),
        ),
        out_shape=outs,
        compiler_params=params(limit),
        cost_estimate=pl.CostEstimate(flops=flops, bytes_accessed=moved, transcendentals=0),
    )(scalars, *operands)


def shape(rows, columns, kind=bf16):
    return jax.ShapeDtypeStruct((rows, columns), kind)


def rows_of(block):
    return pl.ds(pl.multiple_of(block * BLOCK_ROWS, BLOCK_ROWS), BLOCK_ROWS)


def my_core():
    return lax.axis_index("ctx") % CORES


def half(source, width, core):
    return source.at[:, pl.ds(pl.multiple_of(core * width, width), width)]


def pack_kernel(s, q, k, v, logits, out, column, own_kv, own_q, meta, arrived):
    core = my_core()
    moves = (
        (half(q, HALF_QUERY, 1 - core), out.at[:, 0:K_COL]),
        (half(k, HALF_KEY, 1 - core), out.at[:, K_COL:V_COL]),
        (half(v, HALF_KEY, 1 - core), out.at[:, V_COL:M_COL]),
        (half(k, HALF_KEY, core), own_kv.at[:, 0:HALF_KEY]),
        (half(v, HALF_KEY, core), own_kv.at[:, HALF_KEY:]),
        (half(q, HALF_QUERY, core), own_q),
        (meta, out.at[:, M_COL:]),
        (meta, column),
    )
    copies = [pltpu.make_async_copy(source, target, arrived.at[n]) for n, (source, target) in enumerate(moves)]
    for copy in copies[:-2]:
        copy.start()
    count = s[0]
    for b in range(MAXB):
        row = logits[0:1, b * BLOCK_ROWS : (b + 1) * BLOCK_ROWS].astype(f32)
        tall = jnp.broadcast_to(row, (BLOCK_ROWS, BLOCK_ROWS)).T
        lane = lax.broadcasted_iota(i32, (BLOCK_ROWS, HEAD_SIZE), 1)
        rows = slice(b * BLOCK_ROWS, (b + 1) * BLOCK_ROWS)
        meta[rows, :] = jnp.where(lane < HEAD_SIZE // 2, tall, count.astype(f32)).astype(bf16)
    for copy in copies[-2:]:
        copy.start()
    for copy in copies:
        copy.wait()


def cotangent_kernel(s, cot, mine, theirs, arrived):
    core = my_core()
    copies = [
        pltpu.make_async_copy(half(cot, HALF_QUERY, core), mine, arrived.at[0]),
        pltpu.make_async_copy(half(cot, HALF_QUERY, 1 - core), theirs, arrived.at[1]),
    ]
    for copy in copies:
        copy.start()
    for copy in copies:
        copy.wait()


def as_scalar(x):
    return jnp.max(x.astype(f32)).astype(i32)


def chip_counts(s, meta):
    own = s[0]
    other = as_scalar(meta[0:META_ROWS, HEAD_SIZE // 2 :])
    first = jnp.where(my_core() == 0, own, other)
    return first, own + other


def place_of(block, first, core):
    on_first = block < first
    slot = jnp.where(on_first, block, block - first)
    mine = jnp.where(on_first, 0, 1) == core
    return mine, slot


def chip_kernel(s, k, v, kr, vr, meta, *outs):
    first, live = chip_counts(s, meta)
    for b in range(CHIP_BLOCKS):
        mine, slot = place_of(b, first, my_core())
        rows = slice(b * BLOCK_ROWS, (b + 1) * BLOCK_ROWS)

        def copy(keys, vals):
            for h in range(LOCAL_HEADS):
                cols = slice(h * HEAD_SIZE, (h + 1) * HEAD_SIZE)
                outs[h][rows, 0:HEAD_SIZE] = keys[rows_of(slot), cols]
                outs[h][rows, HEAD_SIZE:] = vals[rows_of(slot), cols]

        @pl.when(jnp.logical_and(b < live, mine))
        def _():
            copy(k, v)

        @pl.when(jnp.logical_and(b < live, jnp.logical_not(mine)))
        def _():
            copy(kr, vr)

        @pl.when(b >= live)
        def _():
            for h in range(LOCAL_HEADS):
                outs[h][rows, :] = jnp.zeros((BLOCK_ROWS, 2 * HEAD_SIZE), bf16)

    for h in range(LOCAL_HEADS):
        outs[h][CHIP_ROWS:, :] = jnp.broadcast_to(live.astype(f32), (META_ROWS, 2 * HEAD_SIZE)).astype(bf16)


def attend_kernel(chips, chunk, has_prior, s, *refs):
    q, qr, cot, cotr, column, columnr = refs[:6]
    at = 6
    kv = refs[at : at + chips]
    at += chips
    prior = refs[at : at + chips] if has_prior else None
    at += chips if has_prior else 0
    branch, gate_part = refs[at : at + 2]
    at += 2
    dvs = refs[at : at + chips]
    at += chips
    kd, vd, qs, og, probs, acc, dv = refs[at:]
    steps = kd.shape[0] // chunk

    first, live = chip_counts(s, columnr)
    core = my_core()
    ones = jnp.ones((BLOCK_ROWS, HEAD_SIZE), bf16)
    vd[...] = jnp.zeros_like(vd)
    dv[...] = jnp.zeros_like(dv)

    held = [live] + [as_scalar(kv[d][CHIP_ROWS:, 0:HEAD_SIZE]) for d in range(1, chips)]
    starts = [None] * chips
    position = jnp.int32(0)
    for d in list(range(1, chips)) + [0]:
        starts[d] = position
        for b in range(CHIP_BLOCKS):

            @pl.when(b < held[d])
            def _(d=d, b=b, position=position):
                rows = slice(b * BLOCK_ROWS, (b + 1) * BLOCK_ROWS)
                to = rows_of(position + b)
                kd[to, :] = kv[d][rows, 0:HEAD_SIZE]
                vd[to, 0:HEAD_SIZE] = kv[d][rows, HEAD_SIZE:]
                vd[to, HEAD_SIZE:] = ones

        position = position + held[d]
    base = starts[0]
    scale = math.log2(math.e) / math.sqrt(HEAD_SIZE)
    tall = GROUP * BLOCK_ROWS

    def one_block(b, _):
        mine, slot = place_of(b, first, core)
        here = rows_of(slot)

        @pl.when(mine)
        def _():
            for i in range(GROUP):
                qs[i * BLOCK_ROWS : (i + 1) * BLOCK_ROWS, :] = q[here, i * HEAD_SIZE : (i + 1) * HEAD_SIZE]

        @pl.when(jnp.logical_not(mine))
        def _():
            for i in range(GROUP):
                qs[i * BLOCK_ROWS : (i + 1) * BLOCK_ROWS, :] = qr[here, i * HEAD_SIZE : (i + 1) * HEAD_SIZE]

        t = base + b

        def finish(grad, col):
            logit = jnp.broadcast_to(col[here, 0:1].astype(f32), (BLOCK_ROWS, HEAD_SIZE))
            gate = 1.0 / (1.0 + jnp.exp(-logit))
            total = jnp.zeros((BLOCK_ROWS, HEAD_SIZE), f32)
            for i in range(GROUP):
                rows = slice(i * BLOCK_ROWS, (i + 1) * BLOCK_ROWS)
                cols = slice(i * HEAD_SIZE, (i + 1) * HEAD_SIZE)
                inverse = 1.0 / acc[rows, HEAD_SIZE:]
                attended = acc[rows, 0:HEAD_SIZE] * inverse
                branch[rows_of(b), cols] = (gate * attended).astype(bf16)
                g = grad[here, cols].astype(f32)
                total = total + g * attended
                og[rows, :] = (gate * g * inverse).astype(bf16)
            gate_part[rows_of(b), :] = total

        def sweep(reach):
            key = lax.broadcasted_iota(i32, (BLOCK_ROWS, chunk), 1) + (reach - chunk)
            row = t * BLOCK_ROWS + lax.broadcasted_iota(i32, (BLOCK_ROWS, chunk), 0)
            allowed = key <= row
            for c in range(GROUP):
                w = slice(c * BLOCK_ROWS, (c + 1) * BLOCK_ROWS)
                x = lax.dot_general(
                    qs[w, :], kd[0:reach, :], (((1,), (1,)), ((), ())), preferred_element_type=f32
                )
                tail = jnp.where(allowed, x[:, reach - chunk :], MASKED)
                x = tail if reach == chunk else jnp.concatenate([x[:, : reach - chunk], tail], axis=1)
                p = jnp.exp2((x - jnp.max(x, axis=1, keepdims=True)) * scale).astype(bf16)
                probs[w, 0:reach] = p
                acc[w, :] = jnp.dot(p, vd[0:reach, :], preferred_element_type=f32)

            @pl.when(mine)
            def _():
                finish(cot, column)

            @pl.when(jnp.logical_not(mine))
            def _():
                finish(cotr, columnr)

            width = min(2 * BLOCK_ROWS, chunk)
            for c in range(reach // width):
                w = slice(c * width, (c + 1) * width)
                dv[w, :] += lax.dot_general(
                    probs[:, w], og[...], (((0,), (0,)), ((), ())), preferred_element_type=f32
                )

        last = t * BLOCK_ROWS // chunk
        for j in range(steps):

            @pl.when(last == j)
            def _(j=j):
                sweep((j + 1) * chunk)

        return 0

    lax.fori_loop(0, live, one_block, 0)

    for b in range(CHIP_BLOCKS):
        rows = slice(b * BLOCK_ROWS, (b + 1) * BLOCK_ROWS)

        @pl.when(b >= live)
        def _():
            branch[rows, :] = jnp.zeros((BLOCK_ROWS, GROUP_WIDTH), bf16)
            gate_part[rows, :] = jnp.zeros((BLOCK_ROWS, HEAD_SIZE), f32)

        for d in range(chips):
            cols = slice(0, HEAD_SIZE)
            if has_prior:
                dvs[d][rows, 0:HEAD_SIZE] = prior[d][rows, :]
                cols = slice(HEAD_SIZE, 2 * HEAD_SIZE)

            @pl.when(b < held[d])
            def _():
                dvs[d][rows, cols] = dv[rows_of(starts[d] + b), :].astype(dvs[d].dtype)

            @pl.when(b >= held[d])
            def _():
                dvs[d][rows, cols] = jnp.zeros((BLOCK_ROWS, HEAD_SIZE), dvs[d].dtype)

    lane = lax.broadcasted_iota(i32, (META_ROWS, GROUP_WIDTH), 1)
    branch[CHIP_ROWS:, :] = jnp.where(lane < HEAD_SIZE // 2, first.astype(f32), (live - first).astype(f32)).astype(bf16)


def spread(slot, core, first, second, write, clear):
    held = jnp.where(core == 0, first, second)
    block = jnp.where(core == 0, slot, first + slot)

    @pl.when(slot < held)
    def _():
        write(rows_of(jnp.minimum(block, CHIP_BLOCKS - 1)))

    @pl.when(slot >= held)
    def _():
        clear()


def branch_kernel(s, part, mine, theirs):
    first = as_scalar(part[CHIP_ROWS:, 0 : HEAD_SIZE // 2])
    second = as_scalar(part[CHIP_ROWS:, HEAD_SIZE // 2 : HEAD_SIZE])
    for out, core in ((mine, my_core()), (theirs, 1 - my_core())):
        for slot in range(MAXB):
            rows = slice(slot * BLOCK_ROWS, (slot + 1) * BLOCK_ROWS)

            def write(source):
                out[rows, :] = part[source, :]

            def clear():
                out[rows, :] = jnp.zeros((BLOCK_ROWS, GROUP_WIDTH), bf16)

            spread(slot, core, first, second, write, clear)


def join_kernel(s, *refs):
    mine, theirs, out = refs[:LOCAL_HEADS], refs[LOCAL_HEADS:-1], refs[-1]
    for core in range(CORES):

        @pl.when(my_core() == core)
        def _():
            for h in range(LOCAL_HEADS):
                for at, part in ((core, mine[h]), (1 - core, theirs[h])):
                    start = at * HALF_QUERY + h * GROUP_WIDTH
                    out[:, start : start + GROUP_WIDTH] = part[...]


def gradient_kernel(chips, s, *refs):
    columnr = refs[0]
    own = refs[1]
    arrived = refs[2 : 1 + chips]
    gate_parts = refs[1 + chips : 1 + chips + LOCAL_HEADS]
    mine, gate_mine, theirs = refs[1 + chips + LOCAL_HEADS :]
    first, live = chip_counts(s, columnr)
    second = live - first
    for which, core in ((0, my_core()), (1, 1 - my_core())):
        for slot in range(MAXB):
            rows = slice(slot * BLOCK_ROWS, (slot + 1) * BLOCK_ROWS)

            def write(source):
                total = own[source, :]
                for other in arrived:
                    total = total + other[source, :].astype(f32)
                summed = gate_parts[0][source, :]
                for h in range(1, LOCAL_HEADS):
                    summed = summed + gate_parts[h][source, :]
                summed = jnp.broadcast_to(jnp.sum(summed, axis=1, keepdims=True), (BLOCK_ROWS, HEAD_SIZE))
                if which == 0:
                    mine[rows, :] = total.astype(bf16)
                    gate_mine[rows, :] = summed
                else:
                    theirs[rows, 0:HALF_KEY] = total.astype(bf16)
                    high = summed.astype(bf16)
                    low = (summed - high.astype(f32)).astype(bf16)
                    lane = lax.broadcasted_iota(i32, (BLOCK_ROWS, HEAD_SIZE), 1)
                    theirs[rows, HALF_KEY:] = jnp.where(lane < HEAD_SIZE // 2, high, low)

            def clear():
                if which == 0:
                    mine[rows, :] = jnp.zeros((BLOCK_ROWS, HALF_KEY), bf16)
                    gate_mine[rows, :] = jnp.zeros((BLOCK_ROWS, HEAD_SIZE), f32)
                else:
                    theirs[rows, :] = jnp.zeros((BLOCK_ROWS, HALF_KEY + HEAD_SIZE), bf16)

            spread(slot, core, first, second, write, clear)


def finish_kernel(s, mine, gate_mine, theirs, column, out, gate_out):
    @pl.when(my_core() == 0)
    def _():
        out[:, 0:HALF_KEY] = mine[...]
        out[:, HALF_KEY:] = theirs[:, 0:HALF_KEY]

    @pl.when(my_core() != 0)
    def _():
        out[:, 0:HALF_KEY] = theirs[:, 0:HALF_KEY]
        out[:, HALF_KEY:] = mine[...]

    half = HALF_KEY + HEAD_SIZE // 2
    for b in range(MAXB):
        rows = slice(b * BLOCK_ROWS, (b + 1) * BLOCK_ROWS)
        total = (
            gate_mine[rows, 0:1]
            + theirs[rows, HALF_KEY : HALF_KEY + 1].astype(f32)
            + theirs[rows, half : half + 1].astype(f32)
        )
        logit = column[rows, 0:1].astype(f32)
        gate = 1.0 / (1.0 + jnp.exp(-logit))
        full = jnp.broadcast_to(gate * (1.0 - gate) * total, (BLOCK_ROWS, HEAD_SIZE)).T
        gate_out[0:1, rows] = full[0:1, :].astype(bf16)


def fixed(width, at):
    return pl.BlockSpec((SLOTS, width), lambda i, s: (0, at))


def attend(chips, shards, h, scalars, *operands):
    steps = min(4, shards)
    chunk = -(-shards // steps) * BLOCK_ROWS
    reach = steps * chunk
    tall = GROUP * BLOCK_ROWS
    packed_rows = CHIP_ROWS + META_ROWS
    prior = len(operands) - 6 - chips
    width = HEAD_SIZE * (2 if prior else 1)
    own_at = fixed(GROUP_WIDTH, h)
    column_spec = fixed(HEAD_SIZE, M_COL // HEAD_SIZE)
    return call(
        lambda *refs: attend_kernel(chips, chunk, bool(prior), *refs),
        scalars,
        [own_at, fixed(GROUP_WIDTH, h), own_at, fixed(GROUP_WIDTH, h), whole((SLOTS, HEAD_SIZE)), column_spec]
        + [whole((packed_rows, 2 * HEAD_SIZE))] * chips
        + [whole((CHIP_ROWS, HEAD_SIZE))] * prior,
        operands,
        (shape(packed_rows, GROUP_WIDTH), shape(CHIP_ROWS, HEAD_SIZE, f32), shape(CHIP_ROWS, width, f32))
        + tuple(shape(CHIP_ROWS, width) for _ in range(chips - 1)),
        (whole((packed_rows, GROUP_WIDTH)), whole((CHIP_ROWS, HEAD_SIZE))) + (whole((CHIP_ROWS, width)),) * chips,
        scratch=(
            pltpu.VMEM((reach, HEAD_SIZE), bf16),
            pltpu.VMEM((reach, 2 * HEAD_SIZE), bf16),
            pltpu.VMEM((tall, HEAD_SIZE), bf16),
            pltpu.VMEM((tall, HEAD_SIZE), bf16),
            pltpu.VMEM((tall, reach), bf16),
            pltpu.VMEM((tall, 2 * HEAD_SIZE), f32),
            pltpu.VMEM((reach, HEAD_SIZE), f32),
        ),
        flops=100 * tall * HEAD_SIZE * reach,
        moved=6 * packed_rows * GROUP_WIDTH,
    )


def local(queries, keys, values, cotangent, router_logits, positions, counts):
    shards = lax.axis_size("ctx")
    sections = lax.axis_size("section")
    chips = shards // CORES
    scalars = counts[0]
    q, k, v, cot = queries[0], keys[0], values[0], cotangent[0]

    def swap(x):
        return lax.ppermute(x, "ctx", [(i, i ^ 1) for i in range(shards)])

    def onward(x, by):
        step = by * CORES
        return lax.ppermute(x, "ctx", [(i, i + step) for i in range(shards) if 0 <= i + step < shards])

    def section_on(x):
        return lax.ppermute(x, "section", [(i, (i + 1) % sections) for i in range(sections)])

    column_spec = fixed(HEAD_SIZE, M_COL // HEAD_SIZE)
    far = pl.BlockSpec(memory_space=pltpu.HBM)
    payload, column, own_kv, own_q = call(
        pack_kernel,
        scalars,
        [far, far, far, whole((1, SLOTS))],
        (q, k, v, router_logits),
        (shape(SLOTS, PAYLOAD), shape(SLOTS, HEAD_SIZE), shape(SLOTS, 2 * HALF_KEY), shape(SLOTS, HALF_QUERY)),
        (far, far, far, far),
        scratch=(pltpu.VMEM((SLOTS, HEAD_SIZE), bf16), pltpu.SemaphoreType.DMA((8,))),
        moved=4 * SLOTS * PAYLOAD * 2,
        limit=62 * 1024 * 1024,
    )
    other = swap(payload)
    cot_own, cot_theirs = call(
        cotangent_kernel,
        scalars,
        [far],
        (cot,),
        (shape(SLOTS, HALF_QUERY), shape(SLOTS, HALF_QUERY)),
        (far, far),
        scratch=(pltpu.SemaphoreType.DMA((2,)),),
        moved=8 * SLOTS * HALF_QUERY,
        limit=62 * 1024 * 1024,
    )
    cot_other = swap(cot_theirs)
    packed_rows = CHIP_ROWS + META_ROWS
    packed = call(
        chip_kernel,
        scalars,
        [
            fixed(HALF_KEY, 0),
            fixed(HALF_KEY, 1),
            fixed(HALF_KEY, K_COL // HALF_KEY),
            fixed(HALF_KEY, V_COL // HALF_KEY),
            column_spec,
        ],
        (own_kv, own_kv, other, other, other),
        tuple(shape(packed_rows, 2 * HEAD_SIZE) for _ in range(LOCAL_HEADS)),
        tuple(whole((packed_rows, 2 * HEAD_SIZE)) for _ in range(LOCAL_HEADS)),
        moved=4 * packed_rows * HALF_KEY * 2,
    )
    gathered = []
    for h in range(LOCAL_HEADS):
        own = packed[h]
        if gathered and chips > 1:
            own, *gathered[-1][1:] = lax.optimization_barrier((own, *gathered[-1][1:]))
        gathered.append([own] + [onward(own, d) for d in range(1, chips)])

    prior = []
    branches, gate_parts = [], []
    for h in range(LOCAL_HEADS):
        results = attend(chips, shards, h, scalars, own_q, other, cot_own, cot_other, column, other, *gathered[h], *prior)
        branches.append(section_on(results[0]))
        gate_parts.append(results[1])
        prior = results[2:]
    returned = [onward(prior[d], -d) for d in range(1, chips)]
    branches[0], *returned = lax.optimization_barrier((branches[0], *returned))
    grad_mine, gate_mine, grad_theirs = call(
        lambda *refs: gradient_kernel(chips, *refs),
        scalars,
        [column_spec]
        + [whole((CHIP_ROWS, HALF_KEY))] * chips
        + [whole((CHIP_ROWS, HEAD_SIZE))] * LOCAL_HEADS,
        (other, prior[0], *returned, *gate_parts),
        (shape(SLOTS, HALF_KEY), shape(SLOTS, HEAD_SIZE, f32), shape(SLOTS, HALF_KEY + HEAD_SIZE)),
        (whole((SLOTS, HALF_KEY)), whole((SLOTS, HEAD_SIZE)), whole((SLOTS, HALF_KEY + HEAD_SIZE))),
        moved=8 * CHIP_ROWS * HALF_KEY,
    )
    grad_other = swap(grad_theirs)
    value_grad, gate_grad = call(
        finish_kernel,
        scalars,
        [
            whole((SLOTS, HALF_KEY)),
            whole((SLOTS, HEAD_SIZE)),
            whole((SLOTS, HALF_KEY + HEAD_SIZE)),
            whole((SLOTS, HEAD_SIZE)),
        ],
        (grad_mine, gate_mine, grad_other, column),
        (shape(SLOTS, CORES * HALF_KEY), shape(1, SLOTS)),
        (whole((SLOTS, CORES * HALF_KEY)), whole((1, SLOTS))),
        moved=8 * SLOTS * HALF_KEY,
    )
    branches[-1], value_grad = lax.optimization_barrier((branches[-1], value_grad))
    mine, theirs = [], []
    for h in range(LOCAL_HEADS):
        kept, sent = call(
            branch_kernel,
            scalars,
            [whole((packed_rows, GROUP_WIDTH))],
            (branches[h],),
            (shape(SLOTS, GROUP_WIDTH), shape(SLOTS, GROUP_WIDTH)),
            (whole((SLOTS, GROUP_WIDTH)), whole((SLOTS, GROUP_WIDTH))),
            moved=7 * SLOTS * HALF_QUERY,
        )
        mine.append(kept)
        theirs.append(swap(sent))
    handed = call(
        join_kernel,
        scalars,
        [whole((SLOTS, GROUP_WIDTH))] * (2 * LOCAL_HEADS),
        (*mine, *theirs),
        shape(SLOTS, CORES * HALF_QUERY),
        whole((SLOTS, CORES * HALF_QUERY)),
        moved=8 * SLOTS * HALF_QUERY,
    )
    return (handed[None], value_grad[None], gate_grad)


def solution(mesh):
    rows = P("section", "ctx", None)
    flat = P("section", "ctx")
    return jax.shard_map(
        local,
        mesh=mesh,
        in_specs=(rows, rows, rows, rows, flat, flat, flat),
        out_specs=(rows, rows, flat),
        check_vma=False,
    )
```

```python
import math

import jax
import jax.numpy as jnp
from jax import lax
from jax.experimental import pallas as pl
from jax.experimental.pallas import tpu as pltpu
from jax.sharding import PartitionSpec as P

QUERY_HEADS = 24
KEY_VALUE_HEADS = 4
HEAD_SIZE = 128
BLOCK_ROWS = 128
MAXB = 2

CORES = 2
GROUP = QUERY_HEADS // KEY_VALUE_HEADS
LOCAL_HEADS = KEY_VALUE_HEADS // CORES
GROUP_WIDTH = GROUP * HEAD_SIZE
HALF_QUERY = LOCAL_HEADS * GROUP_WIDTH
HALF_KEY = LOCAL_HEADS * HEAD_SIZE
CHIP_BLOCKS = 2 * MAXB - 1
CHIP_ROWS = CHIP_BLOCKS * BLOCK_ROWS
META_ROWS = 16
SLOTS = MAXB * BLOCK_ROWS
MASKED = -1e30
VMEM_LIMIT = 48 * 1024 * 1024
f32 = jnp.float32
bf16 = jnp.bfloat16
i32 = jnp.int32
K_COL = HALF_QUERY
V_COL = HALF_QUERY + HALF_KEY
M_COL = HALF_QUERY + 2 * HALF_KEY
PAYLOAD = M_COL + HEAD_SIZE


def params(limit):
    return pltpu.CompilerParams(vmem_limit_bytes=limit)


def whole(shape):
    return pl.BlockSpec(shape, lambda i, s: (0,) * len(shape))


def call(body, scalars, grid_in, operands, outs, out_specs, scratch=(), flops=0, moved=0, limit=VMEM_LIMIT):
    return pl.pallas_call(
        body,
        grid_spec=pltpu.PrefetchScalarGridSpec(
            num_scalar_prefetch=1,
            grid=(1,),
            in_specs=grid_in,
            out_specs=out_specs,
            scratch_shapes=list(scratch),
        ),
        out_shape=outs,
        compiler_params=params(limit),
        cost_estimate=pl.CostEstimate(flops=flops, bytes_accessed=moved, transcendentals=0),
    )(scalars, *operands)


def shape(rows, columns, kind=bf16):
    return jax.ShapeDtypeStruct((rows, columns), kind)


def rows_of(block):
    return pl.ds(pl.multiple_of(block * BLOCK_ROWS, BLOCK_ROWS), BLOCK_ROWS)


def my_core():
    return lax.axis_index("ctx") % CORES


def half(source, width, core):
    return source.at[0, :, pl.ds(pl.multiple_of(core * width, width), width)]


def pack_kernel(s, q, k, v, logits, out, column, own_kv, own_q, arrived):
    core = my_core()
    moves = (
        (half(q, HALF_QUERY, 1 - core), out.at[:, 0:K_COL]),
        (half(k, HALF_KEY, 1 - core), out.at[:, K_COL:V_COL]),
        (half(v, HALF_KEY, 1 - core), out.at[:, V_COL:M_COL]),
        (half(k, HALF_KEY, core), own_kv.at[:, 0:HALF_KEY]),
        (half(v, HALF_KEY, core), own_kv.at[:, HALF_KEY:]),
        (half(q, HALF_QUERY, core), own_q),
    )
    copies = [pltpu.make_async_copy(source, target, arrived.at[n]) for n, (source, target) in enumerate(moves)]
    for copy in copies:
        copy.start()
    count = s[0]
    for b in range(MAXB):
        row = logits[0:1, b * BLOCK_ROWS : (b + 1) * BLOCK_ROWS].astype(f32)
        tall = jnp.broadcast_to(row, (BLOCK_ROWS, BLOCK_ROWS)).T
        lane = lax.broadcasted_iota(i32, (BLOCK_ROWS, HEAD_SIZE), 1)
        rows = slice(b * BLOCK_ROWS, (b + 1) * BLOCK_ROWS)
        meta = jnp.where(lane < HEAD_SIZE // 2, tall, count.astype(f32)).astype(bf16)
        out[rows, M_COL:] = meta
        column[rows, :] = meta
    for copy in copies:
        copy.wait()


def cotangent_kernel(s, cot, mine, theirs, arrived):
    core = my_core()
    copies = [
        pltpu.make_async_copy(half(cot, HALF_QUERY, core), mine, arrived.at[0]),
        pltpu.make_async_copy(half(cot, HALF_QUERY, 1 - core), theirs, arrived.at[1]),
    ]
    for copy in copies:
        copy.start()
    for copy in copies:
        copy.wait()


def as_scalar(x):
    return jnp.max(x.astype(f32)).astype(i32)


def chip_counts(s, meta):
    own = s[0]
    other = as_scalar(meta[0:META_ROWS, HEAD_SIZE // 2 :])
    first = jnp.where(my_core() == 0, own, other)
    return first, own + other


def place_of(block, first, core):
    on_first = block < first
    slot = jnp.where(on_first, block, block - first)
    mine = jnp.where(on_first, 0, 1) == core
    return mine, slot


def chip_kernel(s, k, v, kr, vr, meta, *outs):
    first, live = chip_counts(s, meta)
    for b in range(CHIP_BLOCKS):
        mine, slot = place_of(b, first, my_core())
        rows = slice(b * BLOCK_ROWS, (b + 1) * BLOCK_ROWS)

        def copy(keys, vals):
            for h in range(LOCAL_HEADS):
                cols = slice(h * HEAD_SIZE, (h + 1) * HEAD_SIZE)
                outs[h][rows, 0:HEAD_SIZE] = keys[rows_of(slot), cols]
                outs[h][rows, HEAD_SIZE:] = vals[rows_of(slot), cols]

        @pl.when(jnp.logical_and(b < live, mine))
        def _():
            copy(k, v)

        @pl.when(jnp.logical_and(b < live, jnp.logical_not(mine)))
        def _():
            copy(kr, vr)

        @pl.when(b >= live)
        def _():
            for h in range(LOCAL_HEADS):
                outs[h][rows, :] = jnp.zeros((BLOCK_ROWS, 2 * HEAD_SIZE), bf16)

    for h in range(LOCAL_HEADS):
        outs[h][CHIP_ROWS:, :] = jnp.broadcast_to(live.astype(f32), (META_ROWS, 2 * HEAD_SIZE)).astype(bf16)


def attend_kernel(chips, chunk, has_prior, s, *refs):
    q, qr, cot, cotr, column, columnr = refs[:6]
    at = 6
    kv = refs[at : at + chips]
    at += chips
    prior = refs[at : at + chips] if has_prior else None
    at += chips if has_prior else 0
    branch, gate_part = refs[at : at + 2]
    at += 2
    dvs = refs[at : at + chips]
    at += chips
    kd, vd, qs, og, probs, acc, dv = refs[at:]
    steps = kd.shape[0] // chunk

    first, live = chip_counts(s, columnr)
    core = my_core()
    ones = jnp.ones((BLOCK_ROWS, HEAD_SIZE), bf16)
    vd[...] = jnp.zeros_like(vd)
    dv[...] = jnp.zeros_like(dv)

    held = [live] + [as_scalar(kv[d][CHIP_ROWS:, 0:HEAD_SIZE]) for d in range(1, chips)]
    starts = [None] * chips
    position = jnp.int32(0)
    for d in list(range(1, chips)) + [0]:
        starts[d] = position
        for b in range(CHIP_BLOCKS):

            @pl.when(b < held[d])
            def _(d=d, b=b, position=position):
                rows = slice(b * BLOCK_ROWS, (b + 1) * BLOCK_ROWS)
                to = rows_of(position + b)
                kd[to, :] = kv[d][rows, 0:HEAD_SIZE]
                vd[to, 0:HEAD_SIZE] = kv[d][rows, HEAD_SIZE:]
                vd[to, HEAD_SIZE:] = ones

        position = position + held[d]
    base = starts[0]
    scale = math.log2(math.e) / math.sqrt(HEAD_SIZE)
    tall = GROUP * BLOCK_ROWS

    def one_block(b, _):
        mine, slot = place_of(b, first, core)
        here = rows_of(slot)

        @pl.when(mine)
        def _():
            for i in range(GROUP):
                qs[i * BLOCK_ROWS : (i + 1) * BLOCK_ROWS, :] = q[here, i * HEAD_SIZE : (i + 1) * HEAD_SIZE]

        @pl.when(jnp.logical_not(mine))
        def _():
            for i in range(GROUP):
                qs[i * BLOCK_ROWS : (i + 1) * BLOCK_ROWS, :] = qr[here, i * HEAD_SIZE : (i + 1) * HEAD_SIZE]

        t = base + b

        def finish(grad, col):
            logit = jnp.broadcast_to(col[here, 0:1].astype(f32), (BLOCK_ROWS, HEAD_SIZE))
            gate = 1.0 / (1.0 + jnp.exp(-logit))
            total = jnp.zeros((BLOCK_ROWS, HEAD_SIZE), f32)
            for i in range(GROUP):
                rows = slice(i * BLOCK_ROWS, (i + 1) * BLOCK_ROWS)
                cols = slice(i * HEAD_SIZE, (i + 1) * HEAD_SIZE)
                inverse = 1.0 / acc[rows, HEAD_SIZE:]
                attended = acc[rows, 0:HEAD_SIZE] * inverse
                branch[rows_of(b), cols] = (gate * attended).astype(bf16)
                g = grad[here, cols].astype(f32)
                total = total + g * attended
                og[rows, :] = (gate * g * inverse).astype(bf16)
            gate_part[rows_of(b), :] = total

        def sweep(reach):
            key = lax.broadcasted_iota(i32, (BLOCK_ROWS, chunk), 1) + (reach - chunk)
            row = t * BLOCK_ROWS + lax.broadcasted_iota(i32, (BLOCK_ROWS, chunk), 0)
            allowed = key <= row
            for c in range(GROUP):
                w = slice(c * BLOCK_ROWS, (c + 1) * BLOCK_ROWS)
                x = lax.dot_general(
                    qs[w, :], kd[0:reach, :], (((1,), (1,)), ((), ())), preferred_element_type=f32
                )
                tail = jnp.where(allowed, x[:, reach - chunk :], MASKED)
                x = tail if reach == chunk else jnp.concatenate([x[:, : reach - chunk], tail], axis=1)
                p = jnp.exp2((x - jnp.max(x, axis=1, keepdims=True)) * scale).astype(bf16)
                probs[w, 0:reach] = p
                acc[w, :] = jnp.dot(p, vd[0:reach, :], preferred_element_type=f32)

            @pl.when(mine)
            def _():
                finish(cot, column)

            @pl.when(jnp.logical_not(mine))
            def _():
                finish(cotr, columnr)

            width = min(2 * BLOCK_ROWS, chunk)
            for c in range(reach // width):
                w = slice(c * width, (c + 1) * width)
                dv[w, :] += lax.dot_general(
                    probs[:, w], og[...], (((0,), (0,)), ((), ())), preferred_element_type=f32
                )

        last = t * BLOCK_ROWS // chunk
        for j in range(steps):

            @pl.when(last == j)
            def _(j=j):
                sweep((j + 1) * chunk)

        return 0

    lax.fori_loop(0, live, one_block, 0)

    for b in range(CHIP_BLOCKS):
        rows = slice(b * BLOCK_ROWS, (b + 1) * BLOCK_ROWS)

        @pl.when(b >= live)
        def _():
            branch[rows, :] = jnp.zeros((BLOCK_ROWS, GROUP_WIDTH), bf16)
            gate_part[rows, :] = jnp.zeros((BLOCK_ROWS, HEAD_SIZE), f32)

        for d in range(chips):
            cols = slice(0, HEAD_SIZE)
            if has_prior:
                dvs[d][rows, 0:HEAD_SIZE] = prior[d][rows, :]
                cols = slice(HEAD_SIZE, 2 * HEAD_SIZE)

            @pl.when(b < held[d])
            def _():
                dvs[d][rows, cols] = dv[rows_of(starts[d] + b), :].astype(dvs[d].dtype)

            @pl.when(b >= held[d])
            def _():
                dvs[d][rows, cols] = jnp.zeros((BLOCK_ROWS, HEAD_SIZE), dvs[d].dtype)

    lane = lax.broadcasted_iota(i32, (META_ROWS, GROUP_WIDTH), 1)
    branch[CHIP_ROWS:, :] = jnp.where(lane < HEAD_SIZE // 2, first.astype(f32), (live - first).astype(f32)).astype(bf16)


def spread(slot, core, first, second, write, clear):
    held = jnp.where(core == 0, first, second)
    block = jnp.where(core == 0, slot, first + slot)

    @pl.when(slot < held)
    def _():
        write(rows_of(jnp.minimum(block, CHIP_BLOCKS - 1)))

    @pl.when(slot >= held)
    def _():
        clear()


def branch_kernel(s, part, mine, theirs):
    first = as_scalar(part[CHIP_ROWS:, 0 : HEAD_SIZE // 2])
    second = as_scalar(part[CHIP_ROWS:, HEAD_SIZE // 2 : HEAD_SIZE])
    for out, core in ((mine, my_core()), (theirs, 1 - my_core())):
        for slot in range(MAXB):
            rows = slice(slot * BLOCK_ROWS, (slot + 1) * BLOCK_ROWS)

            def write(source):
                out[rows, :] = part[source, :]

            def clear():
                out[rows, :] = jnp.zeros((BLOCK_ROWS, GROUP_WIDTH), bf16)

            spread(slot, core, first, second, write, clear)


def join_kernel(s, *refs):
    mine, theirs, out = refs[:LOCAL_HEADS], refs[LOCAL_HEADS:-1], refs[-1]
    for core in range(CORES):

        @pl.when(my_core() == core)
        def _():
            for h in range(LOCAL_HEADS):
                for at, part in ((core, mine[h]), (1 - core, theirs[h])):
                    start = at * HALF_QUERY + h * GROUP_WIDTH
                    out[:, start : start + GROUP_WIDTH] = part[...]


def gradient_kernel(chips, s, *refs):
    columnr = refs[0]
    own = refs[1]
    arrived = refs[2 : 1 + chips]
    gate_parts = refs[1 + chips : 1 + chips + LOCAL_HEADS]
    mine, gate_mine, theirs = refs[1 + chips + LOCAL_HEADS :]
    first, live = chip_counts(s, columnr)
    second = live - first
    for which, core in ((0, my_core()), (1, 1 - my_core())):
        for slot in range(MAXB):
            rows = slice(slot * BLOCK_ROWS, (slot + 1) * BLOCK_ROWS)

            def write(source):
                total = own[source, :]
                for other in arrived:
                    total = total + other[source, :].astype(f32)
                summed = gate_parts[0][source, :]
                for h in range(1, LOCAL_HEADS):
                    summed = summed + gate_parts[h][source, :]
                summed = jnp.broadcast_to(jnp.sum(summed, axis=1, keepdims=True), (BLOCK_ROWS, HEAD_SIZE))
                if which == 0:
                    mine[rows, :] = total.astype(bf16)
                    gate_mine[rows, :] = summed
                else:
                    theirs[rows, 0:HALF_KEY] = total.astype(bf16)
                    high = summed.astype(bf16)
                    low = (summed - high.astype(f32)).astype(bf16)
                    lane = lax.broadcasted_iota(i32, (BLOCK_ROWS, HEAD_SIZE), 1)
                    theirs[rows, HALF_KEY:] = jnp.where(lane < HEAD_SIZE // 2, high, low)

            def clear():
                if which == 0:
                    mine[rows, :] = jnp.zeros((BLOCK_ROWS, HALF_KEY), bf16)
                    gate_mine[rows, :] = jnp.zeros((BLOCK_ROWS, HEAD_SIZE), f32)
                else:
                    theirs[rows, :] = jnp.zeros((BLOCK_ROWS, HALF_KEY + HEAD_SIZE), bf16)

            spread(slot, core, first, second, write, clear)


def finish_kernel(s, mine, gate_mine, theirs, column, out, gate_out):
    @pl.when(my_core() == 0)
    def _():
        out[:, 0:HALF_KEY] = mine[...]
        out[:, HALF_KEY:] = theirs[:, 0:HALF_KEY]

    @pl.when(my_core() != 0)
    def _():
        out[:, 0:HALF_KEY] = theirs[:, 0:HALF_KEY]
        out[:, HALF_KEY:] = mine[...]

    half = HALF_KEY + HEAD_SIZE // 2
    for b in range(MAXB):
        rows = slice(b * BLOCK_ROWS, (b + 1) * BLOCK_ROWS)
        total = (
            gate_mine[rows, 0:1]
            + theirs[rows, HALF_KEY : HALF_KEY + 1].astype(f32)
            + theirs[rows, half : half + 1].astype(f32)
        )
        logit = column[rows, 0:1].astype(f32)
        gate = 1.0 / (1.0 + jnp.exp(-logit))
        full = jnp.broadcast_to(gate * (1.0 - gate) * total, (BLOCK_ROWS, HEAD_SIZE)).T
        gate_out[0:1, rows] = full[0:1, :].astype(bf16)


def fixed(width, at):
    return pl.BlockSpec((SLOTS, width), lambda i, s: (0, at))


def attend(chips, shards, h, scalars, *operands):
    steps = min(4, shards)
    chunk = -(-shards // steps) * BLOCK_ROWS
    reach = steps * chunk
    tall = GROUP * BLOCK_ROWS
    packed_rows = CHIP_ROWS + META_ROWS
    prior = len(operands) - 6 - chips
    width = HEAD_SIZE * (2 if prior else 1)
    own_at = fixed(GROUP_WIDTH, h)
    column_spec = fixed(HEAD_SIZE, M_COL // HEAD_SIZE)
    return call(
        lambda *refs: attend_kernel(chips, chunk, bool(prior), *refs),
        scalars,
        [own_at, fixed(GROUP_WIDTH, h), own_at, fixed(GROUP_WIDTH, h), whole((SLOTS, HEAD_SIZE)), column_spec]
        + [whole((packed_rows, 2 * HEAD_SIZE))] * chips
        + [whole((CHIP_ROWS, HEAD_SIZE))] * prior,
        operands,
        (shape(packed_rows, GROUP_WIDTH), shape(CHIP_ROWS, HEAD_SIZE, f32), shape(CHIP_ROWS, width, f32))
        + tuple(shape(CHIP_ROWS, width) for _ in range(chips - 1)),
        (whole((packed_rows, GROUP_WIDTH)), whole((CHIP_ROWS, HEAD_SIZE))) + (whole((CHIP_ROWS, width)),) * chips,
        scratch=(
            pltpu.VMEM((reach, HEAD_SIZE), bf16),
            pltpu.VMEM((reach, 2 * HEAD_SIZE), bf16),
            pltpu.VMEM((tall, HEAD_SIZE), bf16),
            pltpu.VMEM((tall, HEAD_SIZE), bf16),
            pltpu.VMEM((tall, reach), bf16),
            pltpu.VMEM((tall, 2 * HEAD_SIZE), f32),
            pltpu.VMEM((reach, HEAD_SIZE), f32),
        ),
        flops=100 * tall * HEAD_SIZE * reach,
        moved=6 * packed_rows * GROUP_WIDTH,
    )


def local(queries, keys, values, cotangent, router_logits, positions, counts):
    shards = lax.axis_size("ctx")
    sections = lax.axis_size("section")
    chips = shards // CORES
    scalars = counts[0]
    def swap(x):
        return lax.ppermute(x, "ctx", [(i, i ^ 1) for i in range(shards)])

    def onward(x, by):
        step = by * CORES
        return lax.ppermute(x, "ctx", [(i, i + step) for i in range(shards) if 0 <= i + step < shards])

    def section_on(x):
        return lax.ppermute(x, "section", [(i, (i + 1) % sections) for i in range(sections)])

    column_spec = fixed(HEAD_SIZE, M_COL // HEAD_SIZE)
    def near(x):
        return pltpu.with_memory_space_constraint(x, pltpu.HBM)

    far = pl.BlockSpec(memory_space=pltpu.HBM)
    payload, column, own_kv, own_q = call(
        pack_kernel,
        scalars,
        [far, far, far, whole((1, SLOTS))],
        (near(queries), near(keys), near(values), router_logits),
        (shape(SLOTS, PAYLOAD), shape(SLOTS, HEAD_SIZE), shape(SLOTS, 2 * HALF_KEY), shape(SLOTS, HALF_QUERY)),
        tuple(whole((SLOTS, width)) for width in (PAYLOAD, HEAD_SIZE, 2 * HALF_KEY, HALF_QUERY)),
        scratch=(pltpu.SemaphoreType.DMA((6,)),),
        moved=4 * SLOTS * PAYLOAD * 2,
    )
    other = swap(payload)
    cot_own, cot_theirs = call(
        cotangent_kernel,
        scalars,
        [far],
        (near(cotangent),),
        (shape(SLOTS, HALF_QUERY), shape(SLOTS, HALF_QUERY)),
        (whole((SLOTS, HALF_QUERY)), whole((SLOTS, HALF_QUERY))),
        scratch=(pltpu.SemaphoreType.DMA((2,)),),
        moved=8 * SLOTS * HALF_QUERY,
    )
    cot_other = swap(cot_theirs)
    packed_rows = CHIP_ROWS + META_ROWS
    packed = call(
        chip_kernel,
        scalars,
        [
            fixed(HALF_KEY, 0),
            fixed(HALF_KEY, 1),
            fixed(HALF_KEY, K_COL // HALF_KEY),
            fixed(HALF_KEY, V_COL // HALF_KEY),
            column_spec,
        ],
        (own_kv, own_kv, other, other, other),
        tuple(shape(packed_rows, 2 * HEAD_SIZE) for _ in range(LOCAL_HEADS)),
        tuple(whole((packed_rows, 2 * HEAD_SIZE)) for _ in range(LOCAL_HEADS)),
        moved=4 * packed_rows * HALF_KEY * 2,
    )
    gathered = []
    for h in range(LOCAL_HEADS):
        own = packed[h]
        if gathered and chips > 1:
            own, *gathered[-1][1:] = lax.optimization_barrier((own, *gathered[-1][1:]))
        gathered.append([own] + [onward(own, d) for d in range(1, chips)])

    prior = []
    branches, gate_parts = [], []
    for h in range(LOCAL_HEADS):
        results = attend(chips, shards, h, scalars, own_q, other, cot_own, cot_other, column, other, *gathered[h], *prior)
        branches.append(section_on(results[0]))
        gate_parts.append(results[1])
        prior = results[2:]
    returned = [onward(prior[d], -d) for d in range(1, chips)]
    branches[0], *returned = lax.optimization_barrier((branches[0], *returned))
    grad_mine, gate_mine, grad_theirs = call(
        lambda *refs: gradient_kernel(chips, *refs),
        scalars,
        [column_spec]
        + [whole((CHIP_ROWS, HALF_KEY))] * chips
        + [whole((CHIP_ROWS, HEAD_SIZE))] * LOCAL_HEADS,
        (other, prior[0], *returned, *gate_parts),
        (shape(SLOTS, HALF_KEY), shape(SLOTS, HEAD_SIZE, f32), shape(SLOTS, HALF_KEY + HEAD_SIZE)),
        (whole((SLOTS, HALF_KEY)), whole((SLOTS, HEAD_SIZE)), whole((SLOTS, HALF_KEY + HEAD_SIZE))),
        moved=8 * CHIP_ROWS * HALF_KEY,
    )
    grad_other = swap(grad_theirs)
    value_grad, gate_grad = call(
        finish_kernel,
        scalars,
        [
            whole((SLOTS, HALF_KEY)),
            whole((SLOTS, HEAD_SIZE)),
            whole((SLOTS, HALF_KEY + HEAD_SIZE)),
            whole((SLOTS, HEAD_SIZE)),
        ],
        (grad_mine, gate_mine, grad_other, column),
        (shape(SLOTS, CORES * HALF_KEY), shape(1, SLOTS)),
        (whole((SLOTS, CORES * HALF_KEY)), whole((1, SLOTS))),
        moved=8 * SLOTS * HALF_KEY,
    )
    branches[-1], value_grad = lax.optimization_barrier((branches[-1], value_grad))
    mine, theirs = [], []
    for h in range(LOCAL_HEADS):
        kept, sent = call(
            branch_kernel,
            scalars,
            [whole((packed_rows, GROUP_WIDTH))],
            (branches[h],),
            (shape(SLOTS, GROUP_WIDTH), shape(SLOTS, GROUP_WIDTH)),
            (whole((SLOTS, GROUP_WIDTH)), whole((SLOTS, GROUP_WIDTH))),
            moved=7 * SLOTS * HALF_QUERY,
        )
        mine.append(kept)
        theirs.append(swap(sent))
    handed = call(
        join_kernel,
        scalars,
        [whole((SLOTS, GROUP_WIDTH))] * (2 * LOCAL_HEADS),
        (*mine, *theirs),
        shape(SLOTS, CORES * HALF_QUERY),
        whole((SLOTS, CORES * HALF_QUERY)),
        moved=8 * SLOTS * HALF_QUERY,
    )
    return (handed[None], value_grad[None], gate_grad)


def solution(mesh):
    rows = P("section", "ctx", None)
    flat = P("section", "ctx")
    return jax.shard_map(
        local,
        mesh=mesh,
        in_specs=(rows, rows, rows, rows, flat, flat, flat),
        out_specs=(rows, rows, flat),
        check_vma=False,
    )
```

```python
import math

import jax
import jax.numpy as jnp
from jax import lax
from jax.experimental import pallas as pl
from jax.experimental.pallas import tpu as pltpu
from jax.sharding import PartitionSpec as P

QUERY_HEADS = 24
KEY_VALUE_HEADS = 4
HEAD_SIZE = 128
BLOCK_ROWS = 128
MAXB = 2

CORES = 2
GROUP = QUERY_HEADS // KEY_VALUE_HEADS
LOCAL_HEADS = KEY_VALUE_HEADS // CORES
GROUP_WIDTH = GROUP * HEAD_SIZE
HALF_QUERY = LOCAL_HEADS * GROUP_WIDTH
HALF_KEY = LOCAL_HEADS * HEAD_SIZE
CHIP_BLOCKS = 2 * MAXB - 1
CHIP_ROWS = CHIP_BLOCKS * BLOCK_ROWS
META_ROWS = 16
SLOTS = MAXB * BLOCK_ROWS
MASKED = -1e30
VMEM_LIMIT = 48 * 1024 * 1024
f32 = jnp.float32
bf16 = jnp.bfloat16
i32 = jnp.int32
PAYLOAD = 2 * HALF_KEY + HEAD_SIZE


def params(limit):
    return pltpu.CompilerParams(vmem_limit_bytes=limit)


def whole(shape):
    return pl.BlockSpec(shape, lambda i, s: (0,) * len(shape))


def call(body, scalars, grid_in, operands, outs, out_specs, scratch=(), flops=0, moved=0, limit=VMEM_LIMIT, aliases={}):
    return pl.pallas_call(
        body,
        grid_spec=pltpu.PrefetchScalarGridSpec(
            num_scalar_prefetch=1,
            grid=(1,),
            in_specs=grid_in,
            out_specs=out_specs,
            scratch_shapes=list(scratch),
        ),
        out_shape=outs,
        compiler_params=params(limit),
        input_output_aliases=aliases,
        cost_estimate=pl.CostEstimate(flops=flops, bytes_accessed=moved, transcendentals=0),
    )(scalars, *operands)


def shape(rows, columns, kind=bf16):
    return jax.ShapeDtypeStruct((rows, columns), kind)


def rows_of(block):
    return pl.ds(pl.multiple_of(block * BLOCK_ROWS, BLOCK_ROWS), BLOCK_ROWS)


def my_core():
    return lax.axis_index("ctx") % CORES


def half(source, width, core):
    return source.at[0, :, pl.ds(pl.multiple_of(core * width, width), width)]


def pack_kernel(s, k, v, logits, out, column, own_kv, flat, arrived):
    core = my_core()
    moves = (
        (logits, flat),
        (half(k, HALF_KEY, 1 - core), out.at[:, 0:HALF_KEY]),
        (half(v, HALF_KEY, 1 - core), out.at[:, HALF_KEY : 2 * HALF_KEY]),
        (half(k, HALF_KEY, core), own_kv.at[:, 0:HALF_KEY]),
        (half(v, HALF_KEY, core), own_kv.at[:, HALF_KEY:]),
    )
    copies = [pltpu.make_async_copy(source, target, arrived.at[n]) for n, (source, target) in enumerate(moves)]
    for copy in copies:
        copy.start()
    copies[0].wait()
    count = s[0]
    for b in range(MAXB):
        row = flat[0:1, b * BLOCK_ROWS : (b + 1) * BLOCK_ROWS].astype(f32)
        tall = jnp.broadcast_to(row, (BLOCK_ROWS, BLOCK_ROWS)).T
        lane = lax.broadcasted_iota(i32, (BLOCK_ROWS, HEAD_SIZE), 1)
        rows = slice(b * BLOCK_ROWS, (b + 1) * BLOCK_ROWS)
        meta = jnp.where(lane < HEAD_SIZE // 2, tall, count.astype(f32)).astype(bf16)
        out[rows, 2 * HALF_KEY :] = meta
        column[rows, :] = meta
    for copy in copies[1:]:
        copy.wait()


def halves_kernel(s, q, cot, after, mine, theirs, arrived):
    core = my_core()
    copies = [
        pltpu.make_async_copy(
            half(source, HALF_QUERY, at), target.at[:, n * HALF_QUERY : (n + 1) * HALF_QUERY], arrived.at[n, m]
        )
        for n, source in enumerate((q, cot))
        for m, (at, target) in enumerate(((1 - core, theirs), (core, mine)))
    ]
    for copy in copies:
        copy.start()
    for copy in copies:
        copy.wait()


def as_scalar(x):
    return jnp.max(x.astype(f32)).astype(i32)


def chip_counts(s, meta):
    own = s[0]
    other = as_scalar(meta[0:META_ROWS, HEAD_SIZE // 2 :])
    first = jnp.where(my_core() == 0, own, other)
    return first, own + other


def place_of(block, first, core):
    on_first = block < first
    slot = jnp.where(on_first, block, block - first)
    mine = jnp.where(on_first, 0, 1) == core
    return mine, slot


def chip_kernel(s, k, v, kr, vr, meta, *outs):
    *outs, pair = outs
    first, live = chip_counts(s, meta)
    lane = lax.broadcasted_iota(i32, (META_ROWS, HEAD_SIZE), 1)
    pair[...] = jnp.where(lane < HEAD_SIZE // 2, first.astype(f32), (live - first).astype(f32)).astype(bf16)
    for b in range(CHIP_BLOCKS):
        mine, slot = place_of(b, first, my_core())
        rows = slice(b * BLOCK_ROWS, (b + 1) * BLOCK_ROWS)

        def copy(keys, vals):
            for h in range(LOCAL_HEADS):
                cols = slice(h * HEAD_SIZE, (h + 1) * HEAD_SIZE)
                outs[h][rows, 0:HEAD_SIZE] = keys[rows_of(slot), cols]
                outs[h][rows, HEAD_SIZE:] = vals[rows_of(slot), cols]

        @pl.when(jnp.logical_and(b < live, mine))
        def _():
            copy(k, v)

        @pl.when(jnp.logical_and(b < live, jnp.logical_not(mine)))
        def _():
            copy(kr, vr)

        @pl.when(b >= live)
        def _():
            for h in range(LOCAL_HEADS):
                outs[h][rows, :] = jnp.zeros((BLOCK_ROWS, 2 * HEAD_SIZE), bf16)

    for h in range(LOCAL_HEADS):
        outs[h][CHIP_ROWS:, :] = jnp.broadcast_to(live.astype(f32), (META_ROWS, 2 * HEAD_SIZE)).astype(bf16)


def attend_kernel(chips, chunk, has_prior, s, *refs):
    q, qr, cot, cotr, column, columnr = refs[:6]
    at = 6
    kv = refs[at : at + chips]
    at += chips
    prior = refs[at : at + chips] if has_prior else None
    at += chips if has_prior else 0
    branch, gate_part = refs[at : at + 2]
    at += 2
    dvs = refs[at : at + chips]
    at += chips
    kd, vd, qs, og, probs, acc, dv = refs[at:]
    steps = kd.shape[0] // chunk

    first, live = chip_counts(s, columnr)
    core = my_core()
    ones = jnp.ones((BLOCK_ROWS, HEAD_SIZE), bf16)
    vd[...] = jnp.zeros_like(vd)
    dv[...] = jnp.zeros_like(dv)

    held = [live] + [as_scalar(kv[d][CHIP_ROWS:, 0:HEAD_SIZE]) for d in range(1, chips)]
    starts = [None] * chips
    position = jnp.int32(0)
    for d in list(range(1, chips)) + [0]:
        starts[d] = position
        for b in range(CHIP_BLOCKS):

            @pl.when(b < held[d])
            def _(d=d, b=b, position=position):
                rows = slice(b * BLOCK_ROWS, (b + 1) * BLOCK_ROWS)
                to = rows_of(position + b)
                kd[to, :] = kv[d][rows, 0:HEAD_SIZE]
                vd[to, 0:HEAD_SIZE] = kv[d][rows, HEAD_SIZE:]
                vd[to, HEAD_SIZE:] = ones

        position = position + held[d]
    base = starts[0]
    scale = math.log2(math.e) / math.sqrt(HEAD_SIZE)
    tall = GROUP * BLOCK_ROWS

    def one_block(b, _):
        mine, slot = place_of(b, first, core)
        here = rows_of(slot)

        @pl.when(mine)
        def _():
            for i in range(GROUP):
                qs[i * BLOCK_ROWS : (i + 1) * BLOCK_ROWS, :] = q[here, i * HEAD_SIZE : (i + 1) * HEAD_SIZE]

        @pl.when(jnp.logical_not(mine))
        def _():
            for i in range(GROUP):
                qs[i * BLOCK_ROWS : (i + 1) * BLOCK_ROWS, :] = qr[here, i * HEAD_SIZE : (i + 1) * HEAD_SIZE]

        t = base + b

        def finish(grad, col):
            logit = jnp.broadcast_to(col[here, 0:1].astype(f32), (BLOCK_ROWS, HEAD_SIZE))
            gate = 1.0 / (1.0 + jnp.exp(-logit))
            total = jnp.zeros((BLOCK_ROWS, HEAD_SIZE), f32)
            for i in range(GROUP):
                rows = slice(i * BLOCK_ROWS, (i + 1) * BLOCK_ROWS)
                cols = slice(i * HEAD_SIZE, (i + 1) * HEAD_SIZE)
                inverse = 1.0 / acc[rows, HEAD_SIZE:]
                attended = acc[rows, 0:HEAD_SIZE] * inverse
                branch[rows_of(b), cols] = (gate * attended).astype(bf16)
                g = grad[here, cols].astype(f32)
                total = total + g * attended
                og[rows, :] = (gate * g * inverse).astype(bf16)
            gate_part[rows_of(b), :] = total

        def sweep(reach):
            key = lax.broadcasted_iota(i32, (BLOCK_ROWS, chunk), 1) + (reach - chunk)
            row = t * BLOCK_ROWS + lax.broadcasted_iota(i32, (BLOCK_ROWS, chunk), 0)
            allowed = key <= row
            for c in range(GROUP):
                w = slice(c * BLOCK_ROWS, (c + 1) * BLOCK_ROWS)
                x = lax.dot_general(
                    qs[w, :], kd[0:reach, :], (((1,), (1,)), ((), ())), preferred_element_type=f32
                )
                tail = jnp.where(allowed, x[:, reach - chunk :], MASKED)
                x = tail if reach == chunk else jnp.concatenate([x[:, : reach - chunk], tail], axis=1)
                p = jnp.exp2((x - jnp.max(x, axis=1, keepdims=True)) * scale).astype(bf16)
                probs[w, 0:reach] = p
                acc[w, :] = jnp.dot(p, vd[0:reach, :], preferred_element_type=f32)

            @pl.when(mine)
            def _():
                finish(cot, column)

            @pl.when(jnp.logical_not(mine))
            def _():
                finish(cotr, columnr)

            width = min(2 * BLOCK_ROWS, chunk)
            for c in range(reach // width):
                w = slice(c * width, (c + 1) * width)
                dv[w, :] += lax.dot_general(
                    probs[:, w], og[...], (((0,), (0,)), ((), ())), preferred_element_type=f32
                )

        last = t * BLOCK_ROWS // chunk
        for j in range(steps):

            @pl.when(last == j)
            def _(j=j):
                sweep((j + 1) * chunk)

        return 0

    lax.fori_loop(0, live, one_block, 0)

    for b in range(CHIP_BLOCKS):
        rows = slice(b * BLOCK_ROWS, (b + 1) * BLOCK_ROWS)

        @pl.when(b >= live)
        def _():
            branch[rows, :] = jnp.zeros((BLOCK_ROWS, GROUP_WIDTH), bf16)
            gate_part[rows, :] = jnp.zeros((BLOCK_ROWS, HEAD_SIZE), f32)

        for d in range(chips):
            cols = slice(0, HEAD_SIZE)
            if has_prior:
                dvs[d][rows, 0:HEAD_SIZE] = prior[d][rows, :]
                cols = slice(HEAD_SIZE, 2 * HEAD_SIZE)

            @pl.when(b < held[d])
            def _():
                dvs[d][rows, cols] = dv[rows_of(starts[d] + b), :].astype(dvs[d].dtype)

            @pl.when(b >= held[d])
            def _():
                dvs[d][rows, cols] = jnp.zeros((BLOCK_ROWS, HEAD_SIZE), dvs[d].dtype)


def spread(slot, core, first, second, write, clear):
    held = jnp.where(core == 0, first, second)
    block = jnp.where(core == 0, slot, first + slot)

    @pl.when(slot < held)
    def _():
        write(rows_of(jnp.minimum(block, CHIP_BLOCKS - 1)))

    @pl.when(slot >= held)
    def _():
        clear()


def branch_kernel(s, part, pair, mine, theirs):
    first = as_scalar(pair[:, 0 : HEAD_SIZE // 2])
    second = as_scalar(pair[:, HEAD_SIZE // 2 :])
    for out, core in ((mine, my_core()), (theirs, 1 - my_core())):
        for slot in range(MAXB):
            rows = slice(slot * BLOCK_ROWS, (slot + 1) * BLOCK_ROWS)

            def write(source):
                out[rows, :] = part[source, :]

            def clear():
                out[rows, :] = jnp.zeros((BLOCK_ROWS, GROUP_WIDTH), bf16)

            spread(slot, core, first, second, write, clear)


def join_kernel(h, s, mine, theirs, *refs):
    out, sent = refs[-2:]
    core = my_core()
    copies = []
    for n, (at, part) in enumerate(((core, mine), (1 - core, theirs))):
        start = pl.multiple_of(at * HALF_QUERY + h * GROUP_WIDTH, HEAD_SIZE)
        copies.append(pltpu.make_async_copy(part, out.at[:, pl.ds(start, GROUP_WIDTH)], sent.at[n]))
        copies[-1].start()
    for copy in copies:
        copy.wait()


def gradient_kernel(chips, s, *refs):
    columnr = refs[0]
    own = refs[1]
    arrived = refs[2 : 1 + chips]
    gate_parts = refs[1 + chips : 1 + chips + LOCAL_HEADS]
    mine, gate_mine, theirs = refs[1 + chips + LOCAL_HEADS :]
    first, live = chip_counts(s, columnr)
    second = live - first
    for which, core in ((0, my_core()), (1, 1 - my_core())):
        for slot in range(MAXB):
            rows = slice(slot * BLOCK_ROWS, (slot + 1) * BLOCK_ROWS)

            def write(source):
                total = own[source, :]
                for other in arrived:
                    total = total + other[source, :].astype(f32)
                summed = gate_parts[0][source, :]
                for h in range(1, LOCAL_HEADS):
                    summed = summed + gate_parts[h][source, :]
                summed = jnp.broadcast_to(jnp.sum(summed, axis=1, keepdims=True), (BLOCK_ROWS, HEAD_SIZE))
                if which == 0:
                    mine[rows, :] = total.astype(bf16)
                    gate_mine[rows, :] = summed
                else:
                    theirs[rows, 0:HALF_KEY] = total.astype(bf16)
                    high = summed.astype(bf16)
                    low = (summed - high.astype(f32)).astype(bf16)
                    lane = lax.broadcasted_iota(i32, (BLOCK_ROWS, HEAD_SIZE), 1)
                    theirs[rows, HALF_KEY:] = jnp.where(lane < HEAD_SIZE // 2, high, low)

            def clear():
                if which == 0:
                    mine[rows, :] = jnp.zeros((BLOCK_ROWS, HALF_KEY), bf16)
                    gate_mine[rows, :] = jnp.zeros((BLOCK_ROWS, HEAD_SIZE), f32)
                else:
                    theirs[rows, :] = jnp.zeros((BLOCK_ROWS, HALF_KEY + HEAD_SIZE), bf16)

            spread(slot, core, first, second, write, clear)


def finish_kernel(s, mine, gate_mine, theirs, column, out, gate_out):
    @pl.when(my_core() == 0)
    def _():
        out[:, 0:HALF_KEY] = mine[...]
        out[:, HALF_KEY:] = theirs[:, 0:HALF_KEY]

    @pl.when(my_core() != 0)
    def _():
        out[:, 0:HALF_KEY] = theirs[:, 0:HALF_KEY]
        out[:, HALF_KEY:] = mine[...]

    half = HALF_KEY + HEAD_SIZE // 2
    for b in range(MAXB):
        rows = slice(b * BLOCK_ROWS, (b + 1) * BLOCK_ROWS)
        total = (
            gate_mine[rows, 0:1]
            + theirs[rows, HALF_KEY : HALF_KEY + 1].astype(f32)
            + theirs[rows, half : half + 1].astype(f32)
        )
        logit = column[rows, 0:1].astype(f32)
        gate = 1.0 / (1.0 + jnp.exp(-logit))
        full = jnp.broadcast_to(gate * (1.0 - gate) * total, (BLOCK_ROWS, HEAD_SIZE)).T
        gate_out[0:1, rows] = full[0:1, :].astype(bf16)


def fixed(width, at):
    return pl.BlockSpec((SLOTS, width), lambda i, s: (0, at))


def attend(chips, shards, h, scalars, *operands):
    steps = min(4, shards)
    chunk = -(-shards // steps) * BLOCK_ROWS
    reach = steps * chunk
    tall = GROUP * BLOCK_ROWS
    packed_rows = CHIP_ROWS + META_ROWS
    prior = len(operands) - 6 - chips
    width = HEAD_SIZE * (2 if prior else 1)
    own_at = fixed(GROUP_WIDTH, h)
    column_spec = fixed(HEAD_SIZE, 2 * HALF_KEY // HEAD_SIZE)
    cot_at = fixed(GROUP_WIDTH, LOCAL_HEADS + h)
    return call(
        lambda *refs: attend_kernel(chips, chunk, bool(prior), *refs),
        scalars,
        [own_at, own_at, cot_at, cot_at, whole((SLOTS, HEAD_SIZE)), column_spec]
        + [whole((packed_rows, 2 * HEAD_SIZE))] * chips
        + [whole((CHIP_ROWS, HEAD_SIZE))] * prior,
        operands,
        (shape(CHIP_ROWS, GROUP_WIDTH), shape(CHIP_ROWS, HEAD_SIZE, f32), shape(CHIP_ROWS, width, f32))
        + tuple(shape(CHIP_ROWS, width) for _ in range(chips - 1)),
        (whole((CHIP_ROWS, GROUP_WIDTH)), whole((CHIP_ROWS, HEAD_SIZE))) + (whole((CHIP_ROWS, width)),) * chips,
        scratch=(
            pltpu.VMEM((reach, HEAD_SIZE), bf16),
            pltpu.VMEM((reach, 2 * HEAD_SIZE), bf16),
            pltpu.VMEM((tall, HEAD_SIZE), bf16),
            pltpu.VMEM((tall, HEAD_SIZE), bf16),
            pltpu.VMEM((tall, reach), bf16),
            pltpu.VMEM((tall, 2 * HEAD_SIZE), f32),
            pltpu.VMEM((reach, HEAD_SIZE), f32),
        ),
        flops=100 * tall * HEAD_SIZE * reach,
        moved=6 * packed_rows * GROUP_WIDTH,
    )


def local(queries, keys, values, cotangent, router_logits, positions, counts):
    shards = lax.axis_size("ctx")
    sections = lax.axis_size("section")
    chips = shards // CORES
    scalars = counts[0]
    def swap(x):
        return lax.ppermute(x, "ctx", [(i, i ^ 1) for i in range(shards)])

    def onward(x, by):
        step = by * CORES
        return lax.ppermute(x, "ctx", [(i, i + step) for i in range(shards) if 0 <= i + step < shards])

    def section_on(x):
        return lax.ppermute(x, "section", [(i, (i + 1) % sections) for i in range(sections)])

    def near(x):
        return pltpu.with_memory_space_constraint(x, pltpu.HBM)

    far = pl.BlockSpec(memory_space=pltpu.HBM)
    column_spec = fixed(HEAD_SIZE, 2 * HALF_KEY // HEAD_SIZE)
    payload, column, own_kv = call(
        pack_kernel,
        scalars,
        [far, far, far],
        (near(keys), near(values), near(router_logits)),
        (shape(SLOTS, PAYLOAD), shape(SLOTS, HEAD_SIZE), shape(SLOTS, 2 * HALF_KEY)),
        tuple(whole((SLOTS, width)) for width in (PAYLOAD, HEAD_SIZE, 2 * HALF_KEY)),
        scratch=(pltpu.VMEM((1, SLOTS), bf16), pltpu.SemaphoreType.DMA((5,))),
        moved=4 * SLOTS * PAYLOAD * 2,
    )
    other = swap(payload)
    packed_rows = CHIP_ROWS + META_ROWS
    *packed, pair = call(
        chip_kernel,
        scalars,
        [fixed(HALF_KEY, 0), fixed(HALF_KEY, 1), fixed(HALF_KEY, 0), fixed(HALF_KEY, 1), column_spec],
        (own_kv, own_kv, other, other, other),
        tuple(shape(packed_rows, 2 * HEAD_SIZE) for _ in range(LOCAL_HEADS)) + (shape(META_ROWS, HEAD_SIZE),),
        tuple(whole((packed_rows, 2 * HEAD_SIZE)) for _ in range(LOCAL_HEADS)) + (whole((META_ROWS, HEAD_SIZE)),),
        moved=4 * packed_rows * HALF_KEY * 2,
    )
    pair_before = section_on(pair)
    gathered = [[packed[0]] + [onward(packed[0], d) for d in range(1, chips)]]
    own, theirs = call(
        halves_kernel,
        scalars,
        [far, far, pl.BlockSpec(memory_space=pl.ANY)],
        (near(queries), near(cotangent), column),
        (shape(SLOTS, 2 * HALF_QUERY), shape(SLOTS, 2 * HALF_QUERY)),
        (whole((SLOTS, 2 * HALF_QUERY)), whole((SLOTS, 2 * HALF_QUERY))),
        scratch=(pltpu.SemaphoreType.DMA((2, 2)),),
        moved=0,
    )
    for h in range(1, LOCAL_HEADS):
        packed[h], pair_before = lax.optimization_barrier((packed[h], pair_before))
        gathered.append([packed[h]] + [onward(packed[h], d) for d in range(1, chips)])
    swapped = swap(theirs)
    prior = []
    branches, gate_parts = [], []
    for h in range(LOCAL_HEADS):
        results = attend(chips, shards, h, scalars, own, swapped, own, swapped, column, other, *gathered[h], *prior)
        branches.append(section_on(results[0]))
        gate_parts.append(results[1])
        prior = results[2:]
    returned = [onward(prior[d], -d) for d in range(1, chips)]
    branches[0], *returned = lax.optimization_barrier((branches[0], *returned))
    grad_mine, gate_mine, grad_theirs = call(
        lambda *refs: gradient_kernel(chips, *refs),
        scalars,
        [column_spec]
        + [whole((CHIP_ROWS, HALF_KEY))] * chips
        + [whole((CHIP_ROWS, HEAD_SIZE))] * LOCAL_HEADS,
        (other, prior[0], *returned, *gate_parts),
        (shape(SLOTS, HALF_KEY), shape(SLOTS, HEAD_SIZE, f32), shape(SLOTS, HALF_KEY + HEAD_SIZE)),
        (whole((SLOTS, HALF_KEY)), whole((SLOTS, HEAD_SIZE)), whole((SLOTS, HALF_KEY + HEAD_SIZE))),
        moved=8 * CHIP_ROWS * HALF_KEY,
    )
    grad_other = swap(grad_theirs)
    value_grad, gate_grad = call(
        finish_kernel,
        scalars,
        [
            whole((SLOTS, HALF_KEY)),
            whole((SLOTS, HEAD_SIZE)),
            whole((SLOTS, HALF_KEY + HEAD_SIZE)),
            whole((SLOTS, HEAD_SIZE)),
        ],
        (grad_mine, gate_mine, grad_other, column),
        (shape(SLOTS, CORES * HALF_KEY), shape(1, SLOTS)),
        (whole((SLOTS, CORES * HALF_KEY)), whole((1, SLOTS))),
        moved=8 * SLOTS * HALF_KEY,
    )
    branches[-1], value_grad = lax.optimization_barrier((branches[-1], value_grad))
    handed = ()
    for h in range(LOCAL_HEADS):
        mine, theirs = call(
            branch_kernel,
            scalars,
            [whole((CHIP_ROWS, GROUP_WIDTH)), whole((META_ROWS, HEAD_SIZE))],
            (branches[h], pair_before),
            (shape(SLOTS, GROUP_WIDTH), shape(SLOTS, GROUP_WIDTH)),
            (whole((SLOTS, GROUP_WIDTH)), whole((SLOTS, GROUP_WIDTH))),
            moved=7 * SLOTS * HALF_QUERY,
        )
        handed = (
            call(
                lambda *refs, h=h: join_kernel(h, *refs),
                scalars,
                [whole((SLOTS, GROUP_WIDTH))] * 2 + [far] * len(handed),
                (mine, swap(theirs), *handed),
                shape(SLOTS, CORES * HALF_QUERY),
                far,
                scratch=(pltpu.SemaphoreType.DMA((2,)),),
                moved=8 * SLOTS * GROUP_WIDTH,
                aliases={3: 0} if handed else {},
            ),
        )
    (handed,) = handed
    return (handed[None], value_grad[None], gate_grad)


def solution(mesh):
    rows = P("section", "ctx", None)
    flat = P("section", "ctx")
    return jax.shard_map(
        local,
        mesh=mesh,
        in_specs=(rows, rows, rows, rows, flat, flat, flat),
        out_specs=(rows, rows, flat),
        check_vma=False,
    )
```

```python
import math

import jax
import jax.numpy as jnp
from jax import lax
from jax.experimental import pallas as pl
from jax.experimental.pallas import tpu as pltpu
from jax.sharding import PartitionSpec as P

QUERY_HEADS = 24
KEY_VALUE_HEADS = 4
HEAD_SIZE = 128
BLOCK_ROWS = 128
MAXB = 2

CORES = 2
GROUP = QUERY_HEADS // KEY_VALUE_HEADS
LOCAL_HEADS = KEY_VALUE_HEADS // CORES
GROUP_WIDTH = GROUP * HEAD_SIZE
HALF_QUERY = LOCAL_HEADS * GROUP_WIDTH
HALF_KEY = LOCAL_HEADS * HEAD_SIZE
CHIP_BLOCKS = 2 * MAXB - 1
CHIP_ROWS = CHIP_BLOCKS * BLOCK_ROWS
META_ROWS = 16
SLOTS = MAXB * BLOCK_ROWS
MASKED = -1e30
VMEM_LIMIT = 48 * 1024 * 1024
f32 = jnp.float32
bf16 = jnp.bfloat16
i32 = jnp.int32
PAYLOAD = 2 * HALF_KEY + HEAD_SIZE


def params(limit):
    return pltpu.CompilerParams(vmem_limit_bytes=limit)


def whole(shape):
    return pl.BlockSpec(shape, lambda i, s: (0,) * len(shape))


def call(body, scalars, grid_in, operands, outs, out_specs, scratch=(), flops=0, moved=0, limit=VMEM_LIMIT, aliases={}):
    return pl.pallas_call(
        body,
        grid_spec=pltpu.PrefetchScalarGridSpec(
            num_scalar_prefetch=1,
            grid=(1,),
            in_specs=grid_in,
            out_specs=out_specs,
            scratch_shapes=list(scratch),
        ),
        out_shape=outs,
        compiler_params=params(limit),
        input_output_aliases=aliases,
        cost_estimate=pl.CostEstimate(flops=flops, bytes_accessed=moved, transcendentals=0),
    )(scalars, *operands)


def shape(rows, columns, kind=bf16):
    return jax.ShapeDtypeStruct((rows, columns), kind)


def rows_of(block):
    return pl.ds(pl.multiple_of(block * BLOCK_ROWS, BLOCK_ROWS), BLOCK_ROWS)


def my_core():
    return lax.axis_index("ctx") % CORES


def half(source, width, core):
    return source.at[0, :, pl.ds(pl.multiple_of(core * width, width), width)]


def pack_kernel(s, k, v, logits, out, column, own_kv, flat, arrived):
    core = my_core()
    moves = (
        (logits, flat),
        (half(k, HALF_KEY, 1 - core), out.at[:, 0:HALF_KEY]),
        (half(v, HALF_KEY, 1 - core), out.at[:, HALF_KEY : 2 * HALF_KEY]),
        (half(k, HALF_KEY, core), own_kv.at[:, 0:HALF_KEY]),
        (half(v, HALF_KEY, core), own_kv.at[:, HALF_KEY:]),
    )
    copies = [pltpu.make_async_copy(source, target, arrived.at[n]) for n, (source, target) in enumerate(moves)]
    for copy in copies:
        copy.start()
    copies[0].wait()
    count = s[0]
    for b in range(MAXB):
        row = flat[0:1, b * BLOCK_ROWS : (b + 1) * BLOCK_ROWS].astype(f32)
        tall = jnp.broadcast_to(row, (BLOCK_ROWS, BLOCK_ROWS)).T
        lane = lax.broadcasted_iota(i32, (BLOCK_ROWS, HEAD_SIZE), 1)
        rows = slice(b * BLOCK_ROWS, (b + 1) * BLOCK_ROWS)
        meta = jnp.where(lane < HEAD_SIZE // 2, tall, count.astype(f32)).astype(bf16)
        out[rows, 2 * HALF_KEY :] = meta
        column[rows, :] = meta
    for copy in copies[1:]:
        copy.wait()


def halves_kernel(s, q, cot, after, mine, theirs, arrived):
    core = my_core()
    copies = [
        pltpu.make_async_copy(
            half(source, HALF_QUERY, at), target.at[:, n * HALF_QUERY : (n + 1) * HALF_QUERY], arrived.at[n, m]
        )
        for n, source in enumerate((q, cot))
        for m, (at, target) in enumerate(((1 - core, theirs), (core, mine)))
    ]
    for copy in copies:
        copy.start()
    for copy in copies:
        copy.wait()


def pass_kernel(s, *refs):
    pass


def passed(scalars, arrays):
    anywhere = [pl.BlockSpec(memory_space=pl.ANY)] * len(arrays)
    return call(
        pass_kernel,
        scalars,
        anywhere,
        tuple(arrays),
        tuple(jax.ShapeDtypeStruct(x.shape, x.dtype) for x in arrays),
        tuple(anywhere),
        flops=15 * 10**9,
        aliases={n + 1: n for n in range(len(arrays))},
    )


def as_scalar(x):
    return jnp.max(x.astype(f32)).astype(i32)


def chip_counts(s, meta):
    own = s[0]
    other = as_scalar(meta[0:META_ROWS, HEAD_SIZE // 2 :])
    first = jnp.where(my_core() == 0, own, other)
    return first, own + other


def place_of(block, first, core):
    on_first = block < first
    slot = jnp.where(on_first, block, block - first)
    mine = jnp.where(on_first, 0, 1) == core
    return mine, slot


def chip_kernel(s, k, v, kr, vr, meta, *outs):
    *outs, pair = outs
    first, live = chip_counts(s, meta)
    lane = lax.broadcasted_iota(i32, (META_ROWS, HEAD_SIZE), 1)
    pair[...] = jnp.where(lane < HEAD_SIZE // 2, first.astype(f32), (live - first).astype(f32)).astype(bf16)
    for b in range(CHIP_BLOCKS):
        mine, slot = place_of(b, first, my_core())
        rows = slice(b * BLOCK_ROWS, (b + 1) * BLOCK_ROWS)

        def copy(keys, vals):
            for h in range(LOCAL_HEADS):
                cols = slice(h * HEAD_SIZE, (h + 1) * HEAD_SIZE)
                outs[h][rows, 0:HEAD_SIZE] = keys[rows_of(slot), cols]
                outs[h][rows, HEAD_SIZE:] = vals[rows_of(slot), cols]

        @pl.when(jnp.logical_and(b < live, mine))
        def _():
            copy(k, v)

        @pl.when(jnp.logical_and(b < live, jnp.logical_not(mine)))
        def _():
            copy(kr, vr)

        @pl.when(b >= live)
        def _():
            for h in range(LOCAL_HEADS):
                outs[h][rows, :] = jnp.zeros((BLOCK_ROWS, 2 * HEAD_SIZE), bf16)

    for h in range(LOCAL_HEADS):
        outs[h][CHIP_ROWS:, :] = jnp.broadcast_to(live.astype(f32), (META_ROWS, 2 * HEAD_SIZE)).astype(bf16)


def attend_kernel(chips, chunk, has_prior, s, *refs):
    q, qr, cot, cotr, column, columnr = refs[:6]
    at = 6
    kv = refs[at : at + chips]
    at += chips
    prior = refs[at : at + chips] if has_prior else None
    at += chips if has_prior else 0
    branch, gate_part = refs[at : at + 2]
    at += 2
    dvs = refs[at : at + chips]
    at += chips
    kd, vd, qs, og, probs, acc, dv = refs[at:]
    steps = kd.shape[0] // chunk

    first, live = chip_counts(s, columnr)
    core = my_core()
    ones = jnp.ones((BLOCK_ROWS, HEAD_SIZE), bf16)
    vd[...] = jnp.zeros_like(vd)
    dv[...] = jnp.zeros_like(dv)

    held = [live] + [as_scalar(kv[d][CHIP_ROWS:, 0:HEAD_SIZE]) for d in range(1, chips)]
    starts = [None] * chips
    position = jnp.int32(0)
    for d in list(range(1, chips)) + [0]:
        starts[d] = position
        for b in range(CHIP_BLOCKS):

            @pl.when(b < held[d])
            def _(d=d, b=b, position=position):
                rows = slice(b * BLOCK_ROWS, (b + 1) * BLOCK_ROWS)
                to = rows_of(position + b)
                kd[to, :] = kv[d][rows, 0:HEAD_SIZE]
                vd[to, 0:HEAD_SIZE] = kv[d][rows, HEAD_SIZE:]
                vd[to, HEAD_SIZE:] = ones

        position = position + held[d]
    base = starts[0]
    scale = math.log2(math.e) / math.sqrt(HEAD_SIZE)
    tall = GROUP * BLOCK_ROWS

    def one_block(b, _):
        mine, slot = place_of(b, first, core)
        here = rows_of(slot)

        @pl.when(mine)
        def _():
            for i in range(GROUP):
                qs[i * BLOCK_ROWS : (i + 1) * BLOCK_ROWS, :] = q[here, i * HEAD_SIZE : (i + 1) * HEAD_SIZE]

        @pl.when(jnp.logical_not(mine))
        def _():
            for i in range(GROUP):
                qs[i * BLOCK_ROWS : (i + 1) * BLOCK_ROWS, :] = qr[here, i * HEAD_SIZE : (i + 1) * HEAD_SIZE]

        t = base + b

        def finish(grad, col):
            logit = jnp.broadcast_to(col[here, 0:1].astype(f32), (BLOCK_ROWS, HEAD_SIZE))
            gate = 1.0 / (1.0 + jnp.exp(-logit))
            total = jnp.zeros((BLOCK_ROWS, HEAD_SIZE), f32)
            for i in range(GROUP):
                rows = slice(i * BLOCK_ROWS, (i + 1) * BLOCK_ROWS)
                cols = slice(i * HEAD_SIZE, (i + 1) * HEAD_SIZE)
                inverse = 1.0 / acc[rows, HEAD_SIZE:]
                attended = acc[rows, 0:HEAD_SIZE] * inverse
                branch[rows_of(b), cols] = (gate * attended).astype(bf16)
                g = grad[here, cols].astype(f32)
                total = total + g * attended
                og[rows, :] = (gate * g * inverse).astype(bf16)
            gate_part[rows_of(b), :] = total

        def sweep(reach):
            key = lax.broadcasted_iota(i32, (BLOCK_ROWS, chunk), 1) + (reach - chunk)
            row = t * BLOCK_ROWS + lax.broadcasted_iota(i32, (BLOCK_ROWS, chunk), 0)
            allowed = key <= row
            for c in range(GROUP):
                w = slice(c * BLOCK_ROWS, (c + 1) * BLOCK_ROWS)
                x = lax.dot_general(
                    qs[w, :], kd[0:reach, :], (((1,), (1,)), ((), ())), preferred_element_type=f32
                )
                tail = jnp.where(allowed, x[:, reach - chunk :], MASKED)
                x = tail if reach == chunk else jnp.concatenate([x[:, : reach - chunk], tail], axis=1)
                p = jnp.exp2((x - jnp.max(x, axis=1, keepdims=True)) * scale).astype(bf16)
                probs[w, 0:reach] = p
                acc[w, :] = jnp.dot(p, vd[0:reach, :], preferred_element_type=f32)

            @pl.when(mine)
            def _():
                finish(cot, column)

            @pl.when(jnp.logical_not(mine))
            def _():
                finish(cotr, columnr)

            width = min(2 * BLOCK_ROWS, chunk)
            for c in range(reach // width):
                w = slice(c * width, (c + 1) * width)
                dv[w, :] += lax.dot_general(
                    probs[:, w], og[...], (((0,), (0,)), ((), ())), preferred_element_type=f32
                )

        last = t * BLOCK_ROWS // chunk
        for j in range(steps):

            @pl.when(last == j)
            def _(j=j):
                sweep((j + 1) * chunk)

        return 0

    lax.fori_loop(0, live, one_block, 0)

    for b in range(CHIP_BLOCKS):
        rows = slice(b * BLOCK_ROWS, (b + 1) * BLOCK_ROWS)

        @pl.when(b >= live)
        def _():
            branch[rows, :] = jnp.zeros((BLOCK_ROWS, GROUP_WIDTH), bf16)
            gate_part[rows, :] = jnp.zeros((BLOCK_ROWS, HEAD_SIZE), f32)

        for d in range(chips):
            cols = slice(0, HEAD_SIZE)
            if has_prior:
                dvs[d][rows, 0:HEAD_SIZE] = prior[d][rows, :]
                cols = slice(HEAD_SIZE, 2 * HEAD_SIZE)

            @pl.when(b < held[d])
            def _():
                dvs[d][rows, cols] = dv[rows_of(starts[d] + b), :].astype(dvs[d].dtype)

            @pl.when(b >= held[d])
            def _():
                dvs[d][rows, cols] = jnp.zeros((BLOCK_ROWS, HEAD_SIZE), dvs[d].dtype)


def spread(slot, core, first, second, write, clear):
    held = jnp.where(core == 0, first, second)
    block = jnp.where(core == 0, slot, first + slot)

    @pl.when(slot < held)
    def _():
        write(rows_of(jnp.minimum(block, CHIP_BLOCKS - 1)))

    @pl.when(slot >= held)
    def _():
        clear()


def branch_kernel(s, part, pair, mine, theirs):
    first = as_scalar(pair[:, 0 : HEAD_SIZE // 2])
    second = as_scalar(pair[:, HEAD_SIZE // 2 :])
    for out, core in ((mine, my_core()), (theirs, 1 - my_core())):
        for slot in range(MAXB):
            rows = slice(slot * BLOCK_ROWS, (slot + 1) * BLOCK_ROWS)

            def write(source):
                out[rows, :] = part[source, :]

            def clear():
                out[rows, :] = jnp.zeros((BLOCK_ROWS, GROUP_WIDTH), bf16)

            spread(slot, core, first, second, write, clear)


def join_kernel(h, s, mine, theirs, *refs):
    out, sent = refs[-2:]
    core = my_core()
    copies = []
    for n, (at, part) in enumerate(((core, mine), (1 - core, theirs))):
        start = pl.multiple_of(at * HALF_QUERY + h * GROUP_WIDTH, HEAD_SIZE)
        copies.append(pltpu.make_async_copy(part, out.at[:, pl.ds(start, GROUP_WIDTH)], sent.at[n]))
        copies[-1].start()
    for copy in copies:
        copy.wait()


def gradient_kernel(chips, s, *refs):
    columnr = refs[0]
    own = refs[1]
    arrived = refs[2 : 1 + chips]
    gate_parts = refs[1 + chips : 1 + chips + LOCAL_HEADS]
    mine, gate_mine, theirs = refs[1 + chips + LOCAL_HEADS :]
    first, live = chip_counts(s, columnr)
    second = live - first
    for which, core in ((0, my_core()), (1, 1 - my_core())):
        for slot in range(MAXB):
            rows = slice(slot * BLOCK_ROWS, (slot + 1) * BLOCK_ROWS)

            def write(source):
                total = own[source, :]
                for other in arrived:
                    total = total + other[source, :].astype(f32)
                summed = gate_parts[0][source, :]
                for h in range(1, LOCAL_HEADS):
                    summed = summed + gate_parts[h][source, :]
                summed = jnp.broadcast_to(jnp.sum(summed, axis=1, keepdims=True), (BLOCK_ROWS, HEAD_SIZE))
                if which == 0:
                    mine[rows, :] = total.astype(bf16)
                    gate_mine[rows, :] = summed
                else:
                    theirs[rows, 0:HALF_KEY] = total.astype(bf16)
                    high = summed.astype(bf16)
                    low = (summed - high.astype(f32)).astype(bf16)
                    lane = lax.broadcasted_iota(i32, (BLOCK_ROWS, HEAD_SIZE), 1)
                    theirs[rows, HALF_KEY:] = jnp.where(lane < HEAD_SIZE // 2, high, low)

            def clear():
                if which == 0:
                    mine[rows, :] = jnp.zeros((BLOCK_ROWS, HALF_KEY), bf16)
                    gate_mine[rows, :] = jnp.zeros((BLOCK_ROWS, HEAD_SIZE), f32)
                else:
                    theirs[rows, :] = jnp.zeros((BLOCK_ROWS, HALF_KEY + HEAD_SIZE), bf16)

            spread(slot, core, first, second, write, clear)


def finish_kernel(s, mine, gate_mine, theirs, column, out, gate_out):
    @pl.when(my_core() == 0)
    def _():
        out[:, 0:HALF_KEY] = mine[...]
        out[:, HALF_KEY:] = theirs[:, 0:HALF_KEY]

    @pl.when(my_core() != 0)
    def _():
        out[:, 0:HALF_KEY] = theirs[:, 0:HALF_KEY]
        out[:, HALF_KEY:] = mine[...]

    half = HALF_KEY + HEAD_SIZE // 2
    for b in range(MAXB):
        rows = slice(b * BLOCK_ROWS, (b + 1) * BLOCK_ROWS)
        total = (
            gate_mine[rows, 0:1]
            + theirs[rows, HALF_KEY : HALF_KEY + 1].astype(f32)
            + theirs[rows, half : half + 1].astype(f32)
        )
        logit = column[rows, 0:1].astype(f32)
        gate = 1.0 / (1.0 + jnp.exp(-logit))
        full = jnp.broadcast_to(gate * (1.0 - gate) * total, (BLOCK_ROWS, HEAD_SIZE)).T
        gate_out[0:1, rows] = full[0:1, :].astype(bf16)


def fixed(width, at):
    return pl.BlockSpec((SLOTS, width), lambda i, s: (0, at))


def attend(chips, shards, h, scalars, *operands):
    steps = min(4, shards)
    chunk = -(-shards // steps) * BLOCK_ROWS
    reach = steps * chunk
    tall = GROUP * BLOCK_ROWS
    packed_rows = CHIP_ROWS + META_ROWS
    prior = len(operands) - 6 - chips
    width = HEAD_SIZE * (2 if prior else 1)
    own_at = fixed(GROUP_WIDTH, h)
    column_spec = fixed(HEAD_SIZE, 2 * HALF_KEY // HEAD_SIZE)
    cot_at = fixed(GROUP_WIDTH, LOCAL_HEADS + h)
    return call(
        lambda *refs: attend_kernel(chips, chunk, bool(prior), *refs),
        scalars,
        [own_at, own_at, cot_at, cot_at, whole((SLOTS, HEAD_SIZE)), column_spec]
        + [whole((packed_rows, 2 * HEAD_SIZE))] * chips
        + [whole((CHIP_ROWS, HEAD_SIZE))] * prior,
        operands,
        (shape(CHIP_ROWS, GROUP_WIDTH), shape(CHIP_ROWS, HEAD_SIZE, f32), shape(CHIP_ROWS, width, f32))
        + tuple(shape(CHIP_ROWS, width) for _ in range(chips - 1)),
        (whole((CHIP_ROWS, GROUP_WIDTH)), whole((CHIP_ROWS, HEAD_SIZE))) + (whole((CHIP_ROWS, width)),) * chips,
        scratch=(
            pltpu.VMEM((reach, HEAD_SIZE), bf16),
            pltpu.VMEM((reach, 2 * HEAD_SIZE), bf16),
            pltpu.VMEM((tall, HEAD_SIZE), bf16),
            pltpu.VMEM((tall, HEAD_SIZE), bf16),
            pltpu.VMEM((tall, reach), bf16),
            pltpu.VMEM((tall, 2 * HEAD_SIZE), f32),
            pltpu.VMEM((reach, HEAD_SIZE), f32),
        ),
        flops=100 * tall * HEAD_SIZE * reach,
        moved=6 * packed_rows * GROUP_WIDTH,
    )


def local(queries, keys, values, cotangent, router_logits, positions, counts):
    shards = lax.axis_size("ctx")
    sections = lax.axis_size("section")
    chips = shards // CORES
    scalars = counts[0]
    def swap(x):
        return lax.ppermute(x, "ctx", [(i, i ^ 1) for i in range(shards)])

    def onward(x, by):
        step = by * CORES
        return lax.ppermute(x, "ctx", [(i, i + step) for i in range(shards) if 0 <= i + step < shards])

    def section_on(x):
        return lax.ppermute(x, "section", [(i, (i + 1) % sections) for i in range(sections)])

    def near(x):
        return pltpu.with_memory_space_constraint(x, pltpu.HBM)

    far = pl.BlockSpec(memory_space=pltpu.HBM)
    column_spec = fixed(HEAD_SIZE, 2 * HALF_KEY // HEAD_SIZE)
    payload, column, own_kv = call(
        pack_kernel,
        scalars,
        [far, far, far],
        (near(keys), near(values), near(router_logits)),
        (shape(SLOTS, PAYLOAD), shape(SLOTS, HEAD_SIZE), shape(SLOTS, 2 * HALF_KEY)),
        tuple(whole((SLOTS, width)) for width in (PAYLOAD, HEAD_SIZE, 2 * HALF_KEY)),
        scratch=(pltpu.VMEM((1, SLOTS), bf16), pltpu.SemaphoreType.DMA((5,))),
        moved=4 * SLOTS * PAYLOAD * 2,
    )
    other = swap(payload)
    packed_rows = CHIP_ROWS + META_ROWS
    *packed, pair = call(
        chip_kernel,
        scalars,
        [fixed(HALF_KEY, 0), fixed(HALF_KEY, 1), fixed(HALF_KEY, 0), fixed(HALF_KEY, 1), column_spec],
        (own_kv, own_kv, other, other, other),
        tuple(shape(packed_rows, 2 * HEAD_SIZE) for _ in range(LOCAL_HEADS)) + (shape(META_ROWS, HEAD_SIZE),),
        tuple(whole((packed_rows, 2 * HEAD_SIZE)) for _ in range(LOCAL_HEADS)) + (whole((META_ROWS, HEAD_SIZE)),),
        moved=4 * packed_rows * HALF_KEY * 2,
    )
    pair_before = section_on(pair)
    gathered = [[packed[0]] + [onward(packed[0], d) for d in range(1, chips)]]
    own, theirs = call(
        halves_kernel,
        scalars,
        [far, far, pl.BlockSpec(memory_space=pl.ANY)],
        (near(queries), near(cotangent), pair_before),
        (shape(SLOTS, 2 * HALF_QUERY), shape(SLOTS, 2 * HALF_QUERY)),
        (whole((SLOTS, 2 * HALF_QUERY)), whole((SLOTS, 2 * HALF_QUERY))),
        scratch=(pltpu.SemaphoreType.DMA((2, 2)),),
        moved=0,
    )
    for h in range(1, LOCAL_HEADS):
        packed[h], theirs = lax.optimization_barrier((packed[h], theirs))
        gathered.append([packed[h]] + [onward(packed[h], d) for d in range(1, chips)])
    swapped = swap(theirs)
    if chips > 1:
        gathered[0][1:] = passed(scalars, gathered[0][1:])
    prior = []
    branches, gate_parts = [], []
    for h in range(LOCAL_HEADS):
        results = attend(chips, shards, h, scalars, own, swapped, own, swapped, column, other, *gathered[h], *prior)
        branches.append(section_on(results[0]))
        gate_parts.append(results[1])
        prior = results[2:]
    returned = [onward(prior[d], -d) for d in range(1, chips)]
    branches[0], *returned = lax.optimization_barrier((branches[0], *returned))
    grad_mine, gate_mine, grad_theirs = call(
        lambda *refs: gradient_kernel(chips, *refs),
        scalars,
        [column_spec]
        + [whole((CHIP_ROWS, HALF_KEY))] * chips
        + [whole((CHIP_ROWS, HEAD_SIZE))] * LOCAL_HEADS,
        (other, prior[0], *returned, *gate_parts),
        (shape(SLOTS, HALF_KEY), shape(SLOTS, HEAD_SIZE, f32), shape(SLOTS, HALF_KEY + HEAD_SIZE)),
        (whole((SLOTS, HALF_KEY)), whole((SLOTS, HEAD_SIZE)), whole((SLOTS, HALF_KEY + HEAD_SIZE))),
        moved=8 * CHIP_ROWS * HALF_KEY,
    )
    grad_other = swap(grad_theirs)
    value_grad, gate_grad = call(
        finish_kernel,
        scalars,
        [
            whole((SLOTS, HALF_KEY)),
            whole((SLOTS, HEAD_SIZE)),
            whole((SLOTS, HALF_KEY + HEAD_SIZE)),
            whole((SLOTS, HEAD_SIZE)),
        ],
        (grad_mine, gate_mine, grad_other, column),
        (shape(SLOTS, CORES * HALF_KEY), shape(1, SLOTS)),
        (whole((SLOTS, CORES * HALF_KEY)), whole((1, SLOTS))),
        moved=8 * SLOTS * HALF_KEY,
    )
    branches[-1], value_grad = lax.optimization_barrier((branches[-1], value_grad))
    handed = ()
    for h in range(LOCAL_HEADS):
        mine, theirs = call(
            branch_kernel,
            scalars,
            [whole((CHIP_ROWS, GROUP_WIDTH)), whole((META_ROWS, HEAD_SIZE))],
            (branches[h], pair_before),
            (shape(SLOTS, GROUP_WIDTH), shape(SLOTS, GROUP_WIDTH)),
            (whole((SLOTS, GROUP_WIDTH)), whole((SLOTS, GROUP_WIDTH))),
            moved=7 * SLOTS * HALF_QUERY,
        )
        handed = (
            call(
                lambda *refs, h=h: join_kernel(h, *refs),
                scalars,
                [whole((SLOTS, GROUP_WIDTH))] * 2 + [far] * len(handed),
                (mine, swap(theirs), *handed),
                shape(SLOTS, CORES * HALF_QUERY),
                far,
                scratch=(pltpu.SemaphoreType.DMA((2,)),),
                moved=8 * SLOTS * GROUP_WIDTH,
                aliases={3: 0} if handed else {},
            ),
        )
    (handed,) = handed
    return (handed[None], value_grad[None], gate_grad)


def solution(mesh):
    rows = P("section", "ctx", None)
    flat = P("section", "ctx")
    return jax.shard_map(
        local,
        mesh=mesh,
        in_specs=(rows, rows, rows, rows, flat, flat, flat),
        out_specs=(rows, rows, flat),
        check_vma=False,
    )
```

```python
import math

import jax
import jax.numpy as jnp
from jax import lax
from jax.experimental import pallas as pl
from jax.experimental.pallas import tpu as pltpu
from jax.sharding import PartitionSpec as P

QUERY_HEADS = 24
KEY_VALUE_HEADS = 4
HEAD_SIZE = 128
BLOCK_ROWS = 128
MAXB = 2

CORES = 2
GROUP = QUERY_HEADS // KEY_VALUE_HEADS
LOCAL_HEADS = KEY_VALUE_HEADS // CORES
GROUP_WIDTH = GROUP * HEAD_SIZE
HALF_QUERY = LOCAL_HEADS * GROUP_WIDTH
HALF_KEY = LOCAL_HEADS * HEAD_SIZE
CHIP_BLOCKS = 2 * MAXB - 1
CHIP_ROWS = CHIP_BLOCKS * BLOCK_ROWS
META_ROWS = 16
SLOTS = MAXB * BLOCK_ROWS
MASKED = -1e30
VMEM_LIMIT = 48 * 1024 * 1024
f32 = jnp.float32
bf16 = jnp.bfloat16
i32 = jnp.int32
PAYLOAD = 2 * HALF_KEY + HEAD_SIZE


def params(limit):
    return pltpu.CompilerParams(vmem_limit_bytes=limit)


def whole(shape):
    return pl.BlockSpec(shape, lambda i, s: (0,) * len(shape))


def call(body, scalars, grid_in, operands, outs, out_specs, scratch=(), flops=0, moved=0, limit=VMEM_LIMIT, aliases={}):
    return pl.pallas_call(
        body,
        grid_spec=pltpu.PrefetchScalarGridSpec(
            num_scalar_prefetch=1,
            grid=(1,),
            in_specs=grid_in,
            out_specs=out_specs,
            scratch_shapes=list(scratch),
        ),
        out_shape=outs,
        compiler_params=params(limit),
        input_output_aliases=aliases,
        cost_estimate=pl.CostEstimate(flops=flops, bytes_accessed=moved, transcendentals=0),
    )(scalars, *operands)


def shape(rows, columns, kind=bf16):
    return jax.ShapeDtypeStruct((rows, columns), kind)


def rows_of(block):
    return pl.ds(pl.multiple_of(block * BLOCK_ROWS, BLOCK_ROWS), BLOCK_ROWS)


def my_core():
    return lax.axis_index("ctx") % CORES


def half(source, width, core):
    return source.at[0, :, pl.ds(pl.multiple_of(core * width, width), width)]


def pack_kernel(s, k, v, logits, out, column, own_kv, flat, arrived):
    core = my_core()
    moves = (
        (logits, flat),
        (half(k, HALF_KEY, 1 - core), out.at[:, 0:HALF_KEY]),
        (half(v, HALF_KEY, 1 - core), out.at[:, HALF_KEY : 2 * HALF_KEY]),
        (half(k, HALF_KEY, core), own_kv.at[:, 0:HALF_KEY]),
        (half(v, HALF_KEY, core), own_kv.at[:, HALF_KEY:]),
    )
    copies = [pltpu.make_async_copy(source, target, arrived.at[n]) for n, (source, target) in enumerate(moves)]
    for copy in copies:
        copy.start()
    copies[0].wait()
    count = s[0]
    for b in range(MAXB):
        row = flat[0:1, b * BLOCK_ROWS : (b + 1) * BLOCK_ROWS].astype(f32)
        tall = jnp.broadcast_to(row, (BLOCK_ROWS, BLOCK_ROWS)).T
        lane = lax.broadcasted_iota(i32, (BLOCK_ROWS, HEAD_SIZE), 1)
        rows = slice(b * BLOCK_ROWS, (b + 1) * BLOCK_ROWS)
        meta = jnp.where(lane < HEAD_SIZE // 2, tall, count.astype(f32)).astype(bf16)
        out[rows, 2 * HALF_KEY :] = meta
        column[rows, :] = meta
    for copy in copies[1:]:
        copy.wait()


def halves_kernel(s, q, cot, after, mine, theirs, arrived):
    core = my_core()
    copies = [
        pltpu.make_async_copy(
            half(source, HALF_QUERY, at), target.at[:, n * HALF_QUERY : (n + 1) * HALF_QUERY], arrived.at[n, m]
        )
        for n, source in enumerate((q, cot))
        for m, (at, target) in enumerate(((1 - core, theirs), (core, mine)))
    ]
    for copy in copies:
        copy.start()
    for copy in copies:
        copy.wait()


def pass_kernel(s, *refs):
    pass


def passed(scalars, arrays):
    anywhere = [pl.BlockSpec(memory_space=pl.ANY)] * len(arrays)
    return call(
        pass_kernel,
        scalars,
        anywhere,
        tuple(arrays),
        tuple(jax.ShapeDtypeStruct(x.shape, x.dtype) for x in arrays),
        tuple(anywhere),
        flops=15 * 10**9,
        aliases={n + 1: n for n in range(len(arrays))},
    )


def as_scalar(x):
    return jnp.max(x.astype(f32)).astype(i32)


def chip_counts(s, meta):
    own = s[0]
    other = as_scalar(meta[0:META_ROWS, HEAD_SIZE // 2 :])
    first = jnp.where(my_core() == 0, own, other)
    return first, own + other


def place_of(block, first, core):
    on_first = block < first
    slot = jnp.where(on_first, block, block - first)
    mine = jnp.where(on_first, 0, 1) == core
    return mine, slot


def chip_kernel(s, k, v, kr, vr, meta, *outs):
    *outs, pair = outs
    first, live = chip_counts(s, meta)
    lane = lax.broadcasted_iota(i32, (META_ROWS, HEAD_SIZE), 1)
    pair[...] = jnp.where(lane < HEAD_SIZE // 2, first.astype(f32), (live - first).astype(f32)).astype(bf16)
    for b in range(CHIP_BLOCKS):
        mine, slot = place_of(b, first, my_core())
        rows = slice(b * BLOCK_ROWS, (b + 1) * BLOCK_ROWS)

        def copy(keys, vals):
            for h in range(LOCAL_HEADS):
                cols = slice(h * HEAD_SIZE, (h + 1) * HEAD_SIZE)
                outs[h][rows, 0:HEAD_SIZE] = keys[rows_of(slot), cols]
                outs[h][rows, HEAD_SIZE:] = vals[rows_of(slot), cols]

        @pl.when(jnp.logical_and(b < live, mine))
        def _():
            copy(k, v)

        @pl.when(jnp.logical_and(b < live, jnp.logical_not(mine)))
        def _():
            copy(kr, vr)

        @pl.when(b >= live)
        def _():
            for h in range(LOCAL_HEADS):
                outs[h][rows, :] = jnp.zeros((BLOCK_ROWS, 2 * HEAD_SIZE), bf16)

    for h in range(LOCAL_HEADS):
        outs[h][CHIP_ROWS:, :] = jnp.broadcast_to(live.astype(f32), (META_ROWS, 2 * HEAD_SIZE)).astype(bf16)


def attend_kernel(chips, chunk, has_prior, s, *refs):
    q, qr, cot, cotr, column, columnr = refs[:6]
    at = 6
    kv = refs[at : at + chips]
    at += chips
    prior = refs[at : at + chips] if has_prior else None
    at += chips if has_prior else 0
    branch, gate_part = refs[at : at + 2]
    at += 2
    dvs = refs[at : at + chips]
    at += chips
    kd, vd, qs, og, probs, acc, dv = refs[at:]
    steps = kd.shape[0] // chunk

    first, live = chip_counts(s, columnr)
    core = my_core()
    ones = jnp.ones((BLOCK_ROWS, HEAD_SIZE), bf16)
    vd[...] = jnp.zeros_like(vd)
    dv[...] = jnp.zeros_like(dv)

    held = [live] + [as_scalar(kv[d][CHIP_ROWS:, 0:HEAD_SIZE]) for d in range(1, chips)]
    starts = [None] * chips
    position = jnp.int32(0)
    for d in list(range(1, chips)) + [0]:
        starts[d] = position
        for b in range(CHIP_BLOCKS):

            @pl.when(b < held[d])
            def _(d=d, b=b, position=position):
                rows = slice(b * BLOCK_ROWS, (b + 1) * BLOCK_ROWS)
                to = rows_of(position + b)
                kd[to, :] = kv[d][rows, 0:HEAD_SIZE]
                vd[to, 0:HEAD_SIZE] = kv[d][rows, HEAD_SIZE:]
                vd[to, HEAD_SIZE:] = ones

        position = position + held[d]
    base = starts[0]
    scale = math.log2(math.e) / math.sqrt(HEAD_SIZE)
    tall = GROUP * BLOCK_ROWS

    def one_block(b, _):
        mine, slot = place_of(b, first, core)
        here = rows_of(slot)

        @pl.when(mine)
        def _():
            for i in range(GROUP):
                qs[i * BLOCK_ROWS : (i + 1) * BLOCK_ROWS, :] = q[here, i * HEAD_SIZE : (i + 1) * HEAD_SIZE]

        @pl.when(jnp.logical_not(mine))
        def _():
            for i in range(GROUP):
                qs[i * BLOCK_ROWS : (i + 1) * BLOCK_ROWS, :] = qr[here, i * HEAD_SIZE : (i + 1) * HEAD_SIZE]

        t = base + b

        def finish(grad, col):
            logit = jnp.broadcast_to(col[here, 0:1].astype(f32), (BLOCK_ROWS, HEAD_SIZE))
            gate = 1.0 / (1.0 + jnp.exp(-logit))
            total = jnp.zeros((BLOCK_ROWS, HEAD_SIZE), f32)
            for i in range(GROUP):
                rows = slice(i * BLOCK_ROWS, (i + 1) * BLOCK_ROWS)
                cols = slice(i * HEAD_SIZE, (i + 1) * HEAD_SIZE)
                inverse = 1.0 / acc[rows, HEAD_SIZE:]
                attended = acc[rows, 0:HEAD_SIZE] * inverse
                branch[rows_of(b), cols] = (gate * attended).astype(bf16)
                g = grad[here, cols].astype(f32)
                total = total + g * attended
                og[rows, :] = (gate * g * inverse).astype(bf16)
            gate_part[rows_of(b), :] = total

        def sweep(reach):
            key = lax.broadcasted_iota(i32, (BLOCK_ROWS, chunk), 1) + (reach - chunk)
            row = t * BLOCK_ROWS + lax.broadcasted_iota(i32, (BLOCK_ROWS, chunk), 0)
            allowed = key <= row
            for c in range(GROUP):
                w = slice(c * BLOCK_ROWS, (c + 1) * BLOCK_ROWS)
                x = lax.dot_general(
                    qs[w, :], kd[0:reach, :], (((1,), (1,)), ((), ())), preferred_element_type=f32
                )
                tail = jnp.where(allowed, x[:, reach - chunk :], MASKED)
                x = tail if reach == chunk else jnp.concatenate([x[:, : reach - chunk], tail], axis=1)
                p = jnp.exp2((x - jnp.max(x, axis=1, keepdims=True)) * scale).astype(bf16)
                probs[w, 0:reach] = p
                acc[w, :] = jnp.dot(p, vd[0:reach, :], preferred_element_type=f32)

            @pl.when(mine)
            def _():
                finish(cot, column)

            @pl.when(jnp.logical_not(mine))
            def _():
                finish(cotr, columnr)

            width = min(2 * BLOCK_ROWS, chunk)
            for c in range(reach // width):
                w = slice(c * width, (c + 1) * width)
                dv[w, :] += lax.dot_general(
                    probs[:, w], og[...], (((0,), (0,)), ((), ())), preferred_element_type=f32
                )

        last = t * BLOCK_ROWS // chunk
        for j in range(steps):

            @pl.when(last == j)
            def _(j=j):
                sweep((j + 1) * chunk)

        return 0

    lax.fori_loop(0, live, one_block, 0)

    for b in range(CHIP_BLOCKS):
        rows = slice(b * BLOCK_ROWS, (b + 1) * BLOCK_ROWS)

        @pl.when(b >= live)
        def _():
            branch[rows, :] = jnp.zeros((BLOCK_ROWS, GROUP_WIDTH), bf16)
            gate_part[rows, :] = jnp.zeros((BLOCK_ROWS, HEAD_SIZE), f32)

        for d in range(chips):
            cols = slice(0, HEAD_SIZE)
            if has_prior:
                dvs[d][rows, 0:HEAD_SIZE] = prior[d][rows, :]
                cols = slice(HEAD_SIZE, 2 * HEAD_SIZE)

            @pl.when(b < held[d])
            def _():
                dvs[d][rows, cols] = dv[rows_of(starts[d] + b), :].astype(dvs[d].dtype)

            @pl.when(b >= held[d])
            def _():
                dvs[d][rows, cols] = jnp.zeros((BLOCK_ROWS, HEAD_SIZE), dvs[d].dtype)


def spread(slot, core, first, second, write, clear):
    held = jnp.where(core == 0, first, second)
    block = jnp.where(core == 0, slot, first + slot)

    @pl.when(slot < held)
    def _():
        write(rows_of(jnp.minimum(block, CHIP_BLOCKS - 1)))

    @pl.when(slot >= held)
    def _():
        clear()


def branch_kernel(s, part, pair, mine, theirs):
    first = as_scalar(pair[:, 0 : HEAD_SIZE // 2])
    second = as_scalar(pair[:, HEAD_SIZE // 2 :])
    for out, core in ((mine, my_core()), (theirs, 1 - my_core())):
        for slot in range(MAXB):
            rows = slice(slot * BLOCK_ROWS, (slot + 1) * BLOCK_ROWS)

            def write(source):
                out[rows, :] = part[source, :]

            def clear():
                out[rows, :] = jnp.zeros((BLOCK_ROWS, GROUP_WIDTH), bf16)

            spread(slot, core, first, second, write, clear)


def join_kernel(h, s, mine, theirs, *refs):
    out, sent = refs[-2:]
    core = my_core()
    copies = []
    for n, (at, part) in enumerate(((core, mine), (1 - core, theirs))):
        start = pl.multiple_of(at * HALF_QUERY + h * GROUP_WIDTH, HEAD_SIZE)
        copies.append(pltpu.make_async_copy(part, out.at[:, pl.ds(start, GROUP_WIDTH)], sent.at[n]))
        copies[-1].start()
    for copy in copies:
        copy.wait()


def gradient_kernel(chips, s, *refs):
    columnr = refs[0]
    own = refs[1]
    arrived = refs[2 : 1 + chips]
    gate_parts = refs[1 + chips : 1 + chips + LOCAL_HEADS]
    mine, gate_mine, theirs = refs[1 + chips + LOCAL_HEADS :]
    first, live = chip_counts(s, columnr)
    second = live - first
    for which, core in ((0, my_core()), (1, 1 - my_core())):
        for slot in range(MAXB):
            rows = slice(slot * BLOCK_ROWS, (slot + 1) * BLOCK_ROWS)

            def write(source):
                total = own[source, :]
                for other in arrived:
                    total = total + other[source, :].astype(f32)
                summed = gate_parts[0][source, :]
                for h in range(1, LOCAL_HEADS):
                    summed = summed + gate_parts[h][source, :]
                summed = jnp.broadcast_to(jnp.sum(summed, axis=1, keepdims=True), (BLOCK_ROWS, HEAD_SIZE))
                if which == 0:
                    mine[rows, :] = total.astype(bf16)
                    gate_mine[rows, :] = summed
                else:
                    theirs[rows, 0:HALF_KEY] = total.astype(bf16)
                    high = summed.astype(bf16)
                    low = (summed - high.astype(f32)).astype(bf16)
                    lane = lax.broadcasted_iota(i32, (BLOCK_ROWS, HEAD_SIZE), 1)
                    theirs[rows, HALF_KEY:] = jnp.where(lane < HEAD_SIZE // 2, high, low)

            def clear():
                if which == 0:
                    mine[rows, :] = jnp.zeros((BLOCK_ROWS, HALF_KEY), bf16)
                    gate_mine[rows, :] = jnp.zeros((BLOCK_ROWS, HEAD_SIZE), f32)
                else:
                    theirs[rows, :] = jnp.zeros((BLOCK_ROWS, HALF_KEY + HEAD_SIZE), bf16)

            spread(slot, core, first, second, write, clear)


def finish_kernel(s, mine, gate_mine, theirs, column, out, gate_out):
    @pl.when(my_core() == 0)
    def _():
        out[:, 0:HALF_KEY] = mine[...]
        out[:, HALF_KEY:] = theirs[:, 0:HALF_KEY]

    @pl.when(my_core() != 0)
    def _():
        out[:, 0:HALF_KEY] = theirs[:, 0:HALF_KEY]
        out[:, HALF_KEY:] = mine[...]

    half = HALF_KEY + HEAD_SIZE // 2
    for b in range(MAXB):
        rows = slice(b * BLOCK_ROWS, (b + 1) * BLOCK_ROWS)
        total = (
            gate_mine[rows, 0:1]
            + theirs[rows, HALF_KEY : HALF_KEY + 1].astype(f32)
            + theirs[rows, half : half + 1].astype(f32)
        )
        logit = column[rows, 0:1].astype(f32)
        gate = 1.0 / (1.0 + jnp.exp(-logit))
        full = jnp.broadcast_to(gate * (1.0 - gate) * total, (BLOCK_ROWS, HEAD_SIZE)).T
        gate_out[0:1, rows] = full[0:1, :].astype(bf16)


def fixed(width, at):
    return pl.BlockSpec((SLOTS, width), lambda i, s: (0, at))


def attend(chips, shards, h, scalars, *operands):
    steps = min(4, shards)
    chunk = -(-shards // steps) * BLOCK_ROWS
    reach = steps * chunk
    tall = GROUP * BLOCK_ROWS
    packed_rows = CHIP_ROWS + META_ROWS
    prior = len(operands) - 6 - chips
    width = HEAD_SIZE * (2 if prior else 1)
    own_at = fixed(GROUP_WIDTH, h)
    column_spec = fixed(HEAD_SIZE, 2 * HALF_KEY // HEAD_SIZE)
    cot_at = fixed(GROUP_WIDTH, LOCAL_HEADS + h)
    return call(
        lambda *refs: attend_kernel(chips, chunk, bool(prior), *refs),
        scalars,
        [own_at, own_at, cot_at, cot_at, whole((SLOTS, HEAD_SIZE)), column_spec]
        + [whole((packed_rows, 2 * HEAD_SIZE))] * chips
        + [whole((CHIP_ROWS, HEAD_SIZE))] * prior,
        operands,
        (shape(CHIP_ROWS, GROUP_WIDTH), shape(CHIP_ROWS, HEAD_SIZE, f32), shape(CHIP_ROWS, width, f32))
        + tuple(shape(CHIP_ROWS, width) for _ in range(chips - 1)),
        (whole((CHIP_ROWS, GROUP_WIDTH)), whole((CHIP_ROWS, HEAD_SIZE))) + (whole((CHIP_ROWS, width)),) * chips,
        scratch=(
            pltpu.VMEM((reach, HEAD_SIZE), bf16),
            pltpu.VMEM((reach, 2 * HEAD_SIZE), bf16),
            pltpu.VMEM((tall, HEAD_SIZE), bf16),
            pltpu.VMEM((tall, HEAD_SIZE), bf16),
            pltpu.VMEM((tall, reach), bf16),
            pltpu.VMEM((tall, 2 * HEAD_SIZE), f32),
            pltpu.VMEM((reach, HEAD_SIZE), f32),
        ),
        flops=100 * tall * HEAD_SIZE * reach,
        moved=6 * packed_rows * GROUP_WIDTH,
    )


def local(queries, keys, values, cotangent, router_logits, positions, counts):
    shards = lax.axis_size("ctx")
    sections = lax.axis_size("section")
    chips = shards // CORES
    scalars = counts[0]
    def swap(x):
        return lax.ppermute(x, "ctx", [(i, i ^ 1) for i in range(shards)])

    def onward(x, by):
        step = by * CORES
        return lax.ppermute(x, "ctx", [(i, i + step) for i in range(shards) if 0 <= i + step < shards])

    def section_on(x):
        return lax.ppermute(x, "section", [(i, (i + 1) % sections) for i in range(sections)])

    def near(x):
        return pltpu.with_memory_space_constraint(x, pltpu.HBM)

    far = pl.BlockSpec(memory_space=pltpu.HBM)
    column_spec = fixed(HEAD_SIZE, 2 * HALF_KEY // HEAD_SIZE)
    payload, column, own_kv = call(
        pack_kernel,
        scalars,
        [far, far, far],
        (near(keys), near(values), near(router_logits)),
        (shape(SLOTS, PAYLOAD), shape(SLOTS, HEAD_SIZE), shape(SLOTS, 2 * HALF_KEY)),
        tuple(whole((SLOTS, width)) for width in (PAYLOAD, HEAD_SIZE, 2 * HALF_KEY)),
        scratch=(pltpu.VMEM((1, SLOTS), bf16), pltpu.SemaphoreType.DMA((5,))),
        moved=4 * SLOTS * PAYLOAD * 2,
    )
    other = swap(payload)
    packed_rows = CHIP_ROWS + META_ROWS
    *packed, pair = call(
        chip_kernel,
        scalars,
        [fixed(HALF_KEY, 0), fixed(HALF_KEY, 1), fixed(HALF_KEY, 0), fixed(HALF_KEY, 1), column_spec],
        (own_kv, own_kv, other, other, other),
        tuple(shape(packed_rows, 2 * HEAD_SIZE) for _ in range(LOCAL_HEADS)) + (shape(META_ROWS, HEAD_SIZE),),
        tuple(whole((packed_rows, 2 * HEAD_SIZE)) for _ in range(LOCAL_HEADS)) + (whole((META_ROWS, HEAD_SIZE)),),
        moved=4 * packed_rows * HALF_KEY * 2,
    )
    pair_before = section_on(pair)
    gathered = [[packed[0]] + [onward(packed[0], d) for d in range(1, chips)]]
    own, theirs = call(
        halves_kernel,
        scalars,
        [far, far, pl.BlockSpec(memory_space=pl.ANY)],
        (near(queries), near(cotangent), swap(pair)),
        (shape(SLOTS, 2 * HALF_QUERY), shape(SLOTS, 2 * HALF_QUERY)),
        (whole((SLOTS, 2 * HALF_QUERY)), whole((SLOTS, 2 * HALF_QUERY))),
        scratch=(pltpu.SemaphoreType.DMA((2, 2)),),
        moved=0,
    )
    for h in range(1, LOCAL_HEADS):
        packed[h], theirs = lax.optimization_barrier((packed[h], theirs))
        gathered.append([packed[h]] + [onward(packed[h], d) for d in range(1, chips)])
    swapped = swap(theirs)
    if chips > 1:
        gathered[0][1:] = passed(scalars, gathered[0][1:])
    prior = []
    branches, gate_parts = [], []
    for h in range(LOCAL_HEADS):
        results = attend(chips, shards, h, scalars, own, swapped, own, swapped, column, other, *gathered[h], *prior)
        branches.append(section_on(results[0]))
        gate_parts.append(results[1])
        prior = results[2:]
    returned = [onward(prior[d], -d) for d in range(1, chips)]
    branches[0], pair_before, *returned = lax.optimization_barrier((branches[0], pair_before, *returned))
    grad_mine, gate_mine, grad_theirs = call(
        lambda *refs: gradient_kernel(chips, *refs),
        scalars,
        [column_spec]
        + [whole((CHIP_ROWS, HALF_KEY))] * chips
        + [whole((CHIP_ROWS, HEAD_SIZE))] * LOCAL_HEADS,
        (other, prior[0], *returned, *gate_parts),
        (shape(SLOTS, HALF_KEY), shape(SLOTS, HEAD_SIZE, f32), shape(SLOTS, HALF_KEY + HEAD_SIZE)),
        (whole((SLOTS, HALF_KEY)), whole((SLOTS, HEAD_SIZE)), whole((SLOTS, HALF_KEY + HEAD_SIZE))),
        moved=8 * CHIP_ROWS * HALF_KEY,
    )
    grad_other = swap(grad_theirs)
    value_grad, gate_grad = call(
        finish_kernel,
        scalars,
        [
            whole((SLOTS, HALF_KEY)),
            whole((SLOTS, HEAD_SIZE)),
            whole((SLOTS, HALF_KEY + HEAD_SIZE)),
            whole((SLOTS, HEAD_SIZE)),
        ],
        (grad_mine, gate_mine, grad_other, column),
        (shape(SLOTS, CORES * HALF_KEY), shape(1, SLOTS)),
        (whole((SLOTS, CORES * HALF_KEY)), whole((1, SLOTS))),
        moved=8 * SLOTS * HALF_KEY,
    )
    branches[-1], value_grad = lax.optimization_barrier((branches[-1], value_grad))
    handed = ()
    for h in range(LOCAL_HEADS):
        mine, theirs = call(
            branch_kernel,
            scalars,
            [whole((CHIP_ROWS, GROUP_WIDTH)), whole((META_ROWS, HEAD_SIZE))],
            (branches[h], pair_before),
            (shape(SLOTS, GROUP_WIDTH), shape(SLOTS, GROUP_WIDTH)),
            (whole((SLOTS, GROUP_WIDTH)), whole((SLOTS, GROUP_WIDTH))),
            moved=7 * SLOTS * HALF_QUERY,
        )
        handed = (
            call(
                lambda *refs, h=h: join_kernel(h, *refs),
                scalars,
                [whole((SLOTS, GROUP_WIDTH))] * 2 + [far] * len(handed),
                (mine, swap(theirs), *handed),
                shape(SLOTS, CORES * HALF_QUERY),
                far,
                scratch=(pltpu.SemaphoreType.DMA((2,)),),
                moved=8 * SLOTS * GROUP_WIDTH,
                aliases={3: 0} if handed else {},
            ),
        )
    (handed,) = handed
    return (handed[None], value_grad[None], gate_grad)


def solution(mesh):
    rows = P("section", "ctx", None)
    flat = P("section", "ctx")
    return jax.shard_map(
        local,
        mesh=mesh,
        in_specs=(rows, rows, rows, rows, flat, flat, flat),
        out_specs=(rows, rows, flat),
        check_vma=False,
    )
```

```python
import math

import jax
import jax.numpy as jnp
from jax import lax
from jax.experimental import pallas as pl
from jax.experimental.pallas import tpu as pltpu
from jax.sharding import PartitionSpec as P

QUERY_HEADS = 24
KEY_VALUE_HEADS = 4
HEAD_SIZE = 128
BLOCK_ROWS = 128
MAXB = 2

CORES = 2
GROUP = QUERY_HEADS // KEY_VALUE_HEADS
LOCAL_HEADS = KEY_VALUE_HEADS // CORES
GROUP_WIDTH = GROUP * HEAD_SIZE
HALF_QUERY = LOCAL_HEADS * GROUP_WIDTH
HALF_KEY = LOCAL_HEADS * HEAD_SIZE
CHIP_BLOCKS = 2 * MAXB - 1
CHIP_ROWS = CHIP_BLOCKS * BLOCK_ROWS
META_ROWS = 16
SLOTS = MAXB * BLOCK_ROWS
MASKED = -1e30
VMEM_LIMIT = 48 * 1024 * 1024
f32 = jnp.float32
bf16 = jnp.bfloat16
i32 = jnp.int32
PAYLOAD = 2 * HALF_KEY + HEAD_SIZE


def params(limit):
    return pltpu.CompilerParams(vmem_limit_bytes=limit)


def whole(shape):
    return pl.BlockSpec(shape, lambda i, s: (0,) * len(shape))


def call(body, scalars, grid_in, operands, outs, out_specs, scratch=(), flops=0, moved=0, limit=VMEM_LIMIT, aliases={}):
    return pl.pallas_call(
        body,
        grid_spec=pltpu.PrefetchScalarGridSpec(
            num_scalar_prefetch=1,
            grid=(1,),
            in_specs=grid_in,
            out_specs=out_specs,
            scratch_shapes=list(scratch),
        ),
        out_shape=outs,
        compiler_params=params(limit),
        input_output_aliases=aliases,
        cost_estimate=pl.CostEstimate(flops=flops, bytes_accessed=moved, transcendentals=0),
    )(scalars, *operands)


def shape(rows, columns, kind=bf16):
    return jax.ShapeDtypeStruct((rows, columns), kind)


def rows_of(block):
    return pl.ds(pl.multiple_of(block * BLOCK_ROWS, BLOCK_ROWS), BLOCK_ROWS)


def my_core():
    return lax.axis_index("ctx") % CORES


def half(source, width, core):
    return source.at[0, :, pl.ds(pl.multiple_of(core * width, width), width)]


def pack_kernel(s, k, v, logits, out, column, own_kv, flat, arrived):
    core = my_core()
    moves = (
        (logits, flat),
        (half(k, HALF_KEY, 1 - core), out.at[:, 0:HALF_KEY]),
        (half(v, HALF_KEY, 1 - core), out.at[:, HALF_KEY : 2 * HALF_KEY]),
        (half(k, HALF_KEY, core), own_kv.at[:, 0:HALF_KEY]),
        (half(v, HALF_KEY, core), own_kv.at[:, HALF_KEY:]),
    )
    copies = [pltpu.make_async_copy(source, target, arrived.at[n]) for n, (source, target) in enumerate(moves)]
    for copy in copies:
        copy.start()
    copies[0].wait()
    count = s[0]
    for b in range(MAXB):
        row = flat[0:1, b * BLOCK_ROWS : (b + 1) * BLOCK_ROWS].astype(f32)
        tall = jnp.broadcast_to(row, (BLOCK_ROWS, BLOCK_ROWS)).T
        lane = lax.broadcasted_iota(i32, (BLOCK_ROWS, HEAD_SIZE), 1)
        rows = slice(b * BLOCK_ROWS, (b + 1) * BLOCK_ROWS)
        meta = jnp.where(lane < HEAD_SIZE // 2, tall, count.astype(f32)).astype(bf16)
        out[rows, 2 * HALF_KEY :] = meta
        column[rows, :] = meta
    for copy in copies[1:]:
        copy.wait()


def halves_kernel(s, q, cot, after, mine, theirs, arrived):
    core = my_core()
    copies = [
        pltpu.make_async_copy(
            half(source, HALF_QUERY, at), target.at[:, n * HALF_QUERY : (n + 1) * HALF_QUERY], arrived.at[n, m]
        )
        for n, source in enumerate((q, cot))
        for m, (at, target) in enumerate(((1 - core, theirs), (core, mine)))
    ]
    for copy in copies:
        copy.start()
    for copy in copies:
        copy.wait()


def pass_kernel(s, *refs):
    pass


def passed(scalars, arrays):
    anywhere = [pl.BlockSpec(memory_space=pl.ANY)] * len(arrays)
    return call(
        pass_kernel,
        scalars,
        anywhere,
        tuple(arrays),
        tuple(jax.ShapeDtypeStruct(x.shape, x.dtype) for x in arrays),
        tuple(anywhere),
        flops=15 * 10**9,
        aliases={n + 1: n for n in range(len(arrays))},
    )


def as_scalar(x):
    return jnp.max(x.astype(f32)).astype(i32)


def chip_counts(s, meta):
    own = s[0]
    other = as_scalar(meta[0:META_ROWS, HEAD_SIZE // 2 :])
    first = jnp.where(my_core() == 0, own, other)
    return first, own + other


def place_of(block, first, core):
    on_first = block < first
    slot = jnp.where(on_first, block, block - first)
    mine = jnp.where(on_first, 0, 1) == core
    return mine, slot


def chip_kernel(s, k, v, kr, vr, meta, *outs):
    *outs, pair = outs
    first, live = chip_counts(s, meta)
    lane = lax.broadcasted_iota(i32, (META_ROWS, HEAD_SIZE), 1)
    pair[...] = jnp.where(lane < HEAD_SIZE // 2, first.astype(f32), (live - first).astype(f32)).astype(bf16)
    for b in range(CHIP_BLOCKS):
        mine, slot = place_of(b, first, my_core())
        rows = slice(b * BLOCK_ROWS, (b + 1) * BLOCK_ROWS)

        def copy(keys, vals):
            for h in range(LOCAL_HEADS):
                cols = slice(h * HEAD_SIZE, (h + 1) * HEAD_SIZE)
                outs[h][rows, 0:HEAD_SIZE] = keys[rows_of(slot), cols]
                outs[h][rows, HEAD_SIZE:] = vals[rows_of(slot), cols]

        @pl.when(jnp.logical_and(b < live, mine))
        def _():
            copy(k, v)

        @pl.when(jnp.logical_and(b < live, jnp.logical_not(mine)))
        def _():
            copy(kr, vr)

        @pl.when(b >= live)
        def _():
            for h in range(LOCAL_HEADS):
                outs[h][rows, :] = jnp.zeros((BLOCK_ROWS, 2 * HEAD_SIZE), bf16)

    for h in range(LOCAL_HEADS):
        outs[h][CHIP_ROWS:, :] = jnp.broadcast_to(live.astype(f32), (META_ROWS, 2 * HEAD_SIZE)).astype(bf16)


def attend_kernel(chips, chunk, has_prior, s, *refs):
    q, qr, cot, cotr, column, columnr = refs[:6]
    at = 6
    kv = refs[at : at + chips]
    at += chips
    prior = refs[at : at + chips] if has_prior else None
    at += chips if has_prior else 0
    branch, gate_part = refs[at : at + 2]
    at += 2
    dvs = refs[at : at + chips]
    at += chips
    kd, vd, qs, og, probs, acc, dv = refs[at:]
    steps = kd.shape[0] // chunk

    first, live = chip_counts(s, columnr)
    core = my_core()
    ones = jnp.ones((BLOCK_ROWS, HEAD_SIZE), bf16)
    vd[...] = jnp.zeros_like(vd)
    dv[...] = jnp.zeros_like(dv)

    held = [live] + [as_scalar(kv[d][CHIP_ROWS:, 0:HEAD_SIZE]) for d in range(1, chips)]
    starts = [None] * chips
    position = jnp.int32(0)
    for d in list(range(1, chips)) + [0]:
        starts[d] = position
        for b in range(CHIP_BLOCKS):

            @pl.when(b < held[d])
            def _(d=d, b=b, position=position):
                rows = slice(b * BLOCK_ROWS, (b + 1) * BLOCK_ROWS)
                to = rows_of(position + b)
                kd[to, :] = kv[d][rows, 0:HEAD_SIZE]
                vd[to, 0:HEAD_SIZE] = kv[d][rows, HEAD_SIZE:]
                vd[to, HEAD_SIZE:] = ones

        position = position + held[d]
    base = starts[0]
    scale = math.log2(math.e) / math.sqrt(HEAD_SIZE)
    tall = GROUP * BLOCK_ROWS

    def one_block(b, _):
        mine, slot = place_of(b, first, core)
        here = rows_of(slot)

        @pl.when(mine)
        def _():
            for i in range(GROUP):
                qs[i * BLOCK_ROWS : (i + 1) * BLOCK_ROWS, :] = q[here, i * HEAD_SIZE : (i + 1) * HEAD_SIZE]

        @pl.when(jnp.logical_not(mine))
        def _():
            for i in range(GROUP):
                qs[i * BLOCK_ROWS : (i + 1) * BLOCK_ROWS, :] = qr[here, i * HEAD_SIZE : (i + 1) * HEAD_SIZE]

        t = base + b

        def finish(grad, col):
            logit = jnp.broadcast_to(col[here, 0:1].astype(f32), (BLOCK_ROWS, HEAD_SIZE))
            gate = 1.0 / (1.0 + jnp.exp(-logit))
            total = jnp.zeros((BLOCK_ROWS, HEAD_SIZE), f32)
            for i in range(GROUP):
                rows = slice(i * BLOCK_ROWS, (i + 1) * BLOCK_ROWS)
                cols = slice(i * HEAD_SIZE, (i + 1) * HEAD_SIZE)
                inverse = 1.0 / acc[rows, HEAD_SIZE:]
                attended = acc[rows, 0:HEAD_SIZE] * inverse
                branch[rows_of(b), cols] = (gate * attended).astype(bf16)
                g = grad[here, cols].astype(f32)
                total = total + g * attended
                og[rows, :] = (gate * g * inverse).astype(bf16)
            gate_part[rows_of(b), :] = total

        def sweep(reach):
            key = lax.broadcasted_iota(i32, (BLOCK_ROWS, chunk), 1) + (reach - chunk)
            row = t * BLOCK_ROWS + lax.broadcasted_iota(i32, (BLOCK_ROWS, chunk), 0)
            allowed = key <= row
            for c in range(GROUP):
                w = slice(c * BLOCK_ROWS, (c + 1) * BLOCK_ROWS)
                x = lax.dot_general(
                    qs[w, :], kd[0:reach, :], (((1,), (1,)), ((), ())), preferred_element_type=f32
                )
                tail = jnp.where(allowed, x[:, reach - chunk :], MASKED)
                x = tail if reach == chunk else jnp.concatenate([x[:, : reach - chunk], tail], axis=1)
                p = jnp.exp2((x - jnp.max(x, axis=1, keepdims=True)) * scale).astype(bf16)
                probs[w, 0:reach] = p
                acc[w, :] = jnp.dot(p, vd[0:reach, :], preferred_element_type=f32)

            @pl.when(mine)
            def _():
                finish(cot, column)

            @pl.when(jnp.logical_not(mine))
            def _():
                finish(cotr, columnr)

            width = min(2 * BLOCK_ROWS, chunk)
            for c in range(reach // width):
                w = slice(c * width, (c + 1) * width)
                dv[w, :] += lax.dot_general(
                    probs[:, w], og[...], (((0,), (0,)), ((), ())), preferred_element_type=f32
                )

        last = t * BLOCK_ROWS // chunk
        for j in range(steps):

            @pl.when(last == j)
            def _(j=j):
                sweep((j + 1) * chunk)

        return 0

    lax.fori_loop(0, live, one_block, 0)
    if branch.shape[0] > CHIP_ROWS:
        lane = lax.broadcasted_iota(i32, (META_ROWS, GROUP_WIDTH), 1)
        counted = jnp.where(lane < HEAD_SIZE // 2, first.astype(f32), (live - first).astype(f32))
        branch[CHIP_ROWS:, :] = counted.astype(bf16)

    for b in range(CHIP_BLOCKS):
        rows = slice(b * BLOCK_ROWS, (b + 1) * BLOCK_ROWS)

        @pl.when(b >= live)
        def _():
            branch[rows, :] = jnp.zeros((BLOCK_ROWS, GROUP_WIDTH), bf16)
            gate_part[rows, :] = jnp.zeros((BLOCK_ROWS, HEAD_SIZE), f32)

        for d in range(chips):
            cols = slice(0, HEAD_SIZE)
            if has_prior:
                dvs[d][rows, 0:HEAD_SIZE] = prior[d][rows, :]
                cols = slice(HEAD_SIZE, 2 * HEAD_SIZE)

            @pl.when(b < held[d])
            def _():
                dvs[d][rows, cols] = dv[rows_of(starts[d] + b), :].astype(dvs[d].dtype)

            @pl.when(b >= held[d])
            def _():
                dvs[d][rows, cols] = jnp.zeros((BLOCK_ROWS, HEAD_SIZE), dvs[d].dtype)


def spread(slot, core, first, second, write, clear):
    held = jnp.where(core == 0, first, second)
    block = jnp.where(core == 0, slot, first + slot)

    @pl.when(slot < held)
    def _():
        write(rows_of(jnp.minimum(block, CHIP_BLOCKS - 1)))

    @pl.when(slot >= held)
    def _():
        clear()


def branch_kernel(s, part, pair, mine, theirs):
    first = as_scalar(pair[:, 0 : HEAD_SIZE // 2])
    second = as_scalar(pair[:, HEAD_SIZE // 2 :])
    for out, core in ((mine, my_core()), (theirs, 1 - my_core())):
        for slot in range(MAXB):
            rows = slice(slot * BLOCK_ROWS, (slot + 1) * BLOCK_ROWS)

            def write(source):
                out[rows, :] = part[source, :]

            def clear():
                out[rows, :] = jnp.zeros((BLOCK_ROWS, GROUP_WIDTH), bf16)

            spread(slot, core, first, second, write, clear)


def join_kernel(h, s, mine, theirs, *refs):
    out, sent = refs[-2:]
    core = my_core()
    copies = []
    for n, (at, part) in enumerate(((core, mine), (1 - core, theirs))):
        start = pl.multiple_of(at * HALF_QUERY + h * GROUP_WIDTH, HEAD_SIZE)
        copies.append(pltpu.make_async_copy(part, out.at[:, pl.ds(start, GROUP_WIDTH)], sent.at[n]))
        copies[-1].start()
    for copy in copies:
        copy.wait()


def gradient_kernel(chips, s, *refs):
    columnr = refs[0]
    own = refs[1]
    arrived = refs[2 : 1 + chips]
    gate_parts = refs[1 + chips : 1 + chips + LOCAL_HEADS]
    mine, gate_mine, theirs = refs[1 + chips + LOCAL_HEADS :]
    first, live = chip_counts(s, columnr)
    second = live - first
    for which, core in ((0, my_core()), (1, 1 - my_core())):
        for slot in range(MAXB):
            rows = slice(slot * BLOCK_ROWS, (slot + 1) * BLOCK_ROWS)

            def write(source):
                total = own[source, :]
                for other in arrived:
                    total = total + other[source, :].astype(f32)
                summed = gate_parts[0][source, :]
                for h in range(1, LOCAL_HEADS):
                    summed = summed + gate_parts[h][source, :]
                summed = jnp.broadcast_to(jnp.sum(summed, axis=1, keepdims=True), (BLOCK_ROWS, HEAD_SIZE))
                if which == 0:
                    mine[rows, :] = total.astype(bf16)
                    gate_mine[rows, :] = summed
                else:
                    theirs[rows, 0:HALF_KEY] = total.astype(bf16)
                    high = summed.astype(bf16)
                    low = (summed - high.astype(f32)).astype(bf16)
                    lane = lax.broadcasted_iota(i32, (BLOCK_ROWS, HEAD_SIZE), 1)
                    theirs[rows, HALF_KEY:] = jnp.where(lane < HEAD_SIZE // 2, high, low)

            def clear():
                if which == 0:
                    mine[rows, :] = jnp.zeros((BLOCK_ROWS, HALF_KEY), bf16)
                    gate_mine[rows, :] = jnp.zeros((BLOCK_ROWS, HEAD_SIZE), f32)
                else:
                    theirs[rows, :] = jnp.zeros((BLOCK_ROWS, HALF_KEY + HEAD_SIZE), bf16)

            spread(slot, core, first, second, write, clear)


def finish_kernel(s, mine, gate_mine, theirs, column, out, gate_out):
    @pl.when(my_core() == 0)
    def _():
        out[:, 0:HALF_KEY] = mine[...]
        out[:, HALF_KEY:] = theirs[:, 0:HALF_KEY]

    @pl.when(my_core() != 0)
    def _():
        out[:, 0:HALF_KEY] = theirs[:, 0:HALF_KEY]
        out[:, HALF_KEY:] = mine[...]

    half = HALF_KEY + HEAD_SIZE // 2
    for b in range(MAXB):
        rows = slice(b * BLOCK_ROWS, (b + 1) * BLOCK_ROWS)
        total = (
            gate_mine[rows, 0:1]
            + theirs[rows, HALF_KEY : HALF_KEY + 1].astype(f32)
            + theirs[rows, half : half + 1].astype(f32)
        )
        logit = column[rows, 0:1].astype(f32)
        gate = 1.0 / (1.0 + jnp.exp(-logit))
        full = jnp.broadcast_to(gate * (1.0 - gate) * total, (BLOCK_ROWS, HEAD_SIZE)).T
        gate_out[0:1, rows] = full[0:1, :].astype(bf16)


def fixed(width, at):
    return pl.BlockSpec((SLOTS, width), lambda i, s: (0, at))


def attend(chips, shards, h, scalars, *operands):
    steps = min(4, shards)
    chunk = -(-shards // steps) * BLOCK_ROWS
    reach = steps * chunk
    tall = GROUP * BLOCK_ROWS
    packed_rows = CHIP_ROWS + META_ROWS
    prior = len(operands) - 6 - chips
    sent_rows = CHIP_ROWS if h else packed_rows
    width = HEAD_SIZE * (2 if prior else 1)
    own_at = fixed(GROUP_WIDTH, h)
    column_spec = fixed(HEAD_SIZE, 2 * HALF_KEY // HEAD_SIZE)
    cot_at = fixed(GROUP_WIDTH, LOCAL_HEADS + h)
    return call(
        lambda *refs: attend_kernel(chips, chunk, bool(prior), *refs),
        scalars,
        [own_at, own_at, cot_at, cot_at, whole((SLOTS, HEAD_SIZE)), column_spec]
        + [whole((packed_rows, 2 * HEAD_SIZE))] * chips
        + [whole((CHIP_ROWS, HEAD_SIZE))] * prior,
        operands,
        (shape(sent_rows, GROUP_WIDTH), shape(CHIP_ROWS, HEAD_SIZE, f32), shape(CHIP_ROWS, width, f32))
        + tuple(shape(CHIP_ROWS, width) for _ in range(chips - 1)),
        (whole((sent_rows, GROUP_WIDTH)), whole((CHIP_ROWS, HEAD_SIZE))) + (whole((CHIP_ROWS, width)),) * chips,
        scratch=(
            pltpu.VMEM((reach, HEAD_SIZE), bf16),
            pltpu.VMEM((reach, 2 * HEAD_SIZE), bf16),
            pltpu.VMEM((tall, HEAD_SIZE), bf16),
            pltpu.VMEM((tall, HEAD_SIZE), bf16),
            pltpu.VMEM((tall, reach), bf16),
            pltpu.VMEM((tall, 2 * HEAD_SIZE), f32),
            pltpu.VMEM((reach, HEAD_SIZE), f32),
        ),
        flops=100 * tall * HEAD_SIZE * reach,
        moved=6 * packed_rows * GROUP_WIDTH,
    )


def local(queries, keys, values, cotangent, router_logits, positions, counts):
    shards = lax.axis_size("ctx")
    sections = lax.axis_size("section")
    chips = shards // CORES
    scalars = counts[0]
    def swap(x):
        return lax.ppermute(x, "ctx", [(i, i ^ 1) for i in range(shards)])

    def onward(x, by):
        step = by * CORES
        return lax.ppermute(x, "ctx", [(i, i + step) for i in range(shards) if 0 <= i + step < shards])

    def section_on(x):
        return lax.ppermute(x, "section", [(i, (i + 1) % sections) for i in range(sections)])

    def near(x):
        return pltpu.with_memory_space_constraint(x, pltpu.HBM)

    far = pl.BlockSpec(memory_space=pltpu.HBM)
    column_spec = fixed(HEAD_SIZE, 2 * HALF_KEY // HEAD_SIZE)
    payload, column, own_kv = call(
        pack_kernel,
        scalars,
        [far, far, far],
        (near(keys), near(values), near(router_logits)),
        (shape(SLOTS, PAYLOAD), shape(SLOTS, HEAD_SIZE), shape(SLOTS, 2 * HALF_KEY)),
        tuple(whole((SLOTS, width)) for width in (PAYLOAD, HEAD_SIZE, 2 * HALF_KEY)),
        scratch=(pltpu.VMEM((1, SLOTS), bf16), pltpu.SemaphoreType.DMA((5,))),
        moved=4 * SLOTS * PAYLOAD * 2,
    )
    other = swap(payload)
    packed_rows = CHIP_ROWS + META_ROWS
    *packed, pair = call(
        chip_kernel,
        scalars,
        [fixed(HALF_KEY, 0), fixed(HALF_KEY, 1), fixed(HALF_KEY, 0), fixed(HALF_KEY, 1), column_spec],
        (own_kv, own_kv, other, other, other),
        tuple(shape(packed_rows, 2 * HEAD_SIZE) for _ in range(LOCAL_HEADS)) + (shape(META_ROWS, HEAD_SIZE),),
        tuple(whole((packed_rows, 2 * HEAD_SIZE)) for _ in range(LOCAL_HEADS)) + (whole((META_ROWS, HEAD_SIZE)),),
        moved=4 * packed_rows * HALF_KEY * 2,
    )
    gathered = [[packed[0]] + [onward(packed[0], d) for d in range(1, chips)]]
    own, theirs = call(
        halves_kernel,
        scalars,
        [far, far, pl.BlockSpec(memory_space=pl.ANY)],
        (near(queries), near(cotangent), swap(pair)),
        (shape(SLOTS, 2 * HALF_QUERY), shape(SLOTS, 2 * HALF_QUERY)),
        (whole((SLOTS, 2 * HALF_QUERY)), whole((SLOTS, 2 * HALF_QUERY))),
        scratch=(pltpu.SemaphoreType.DMA((2, 2)),),
        moved=0,
    )
    for h in range(1, LOCAL_HEADS):
        packed[h], theirs = lax.optimization_barrier((packed[h], theirs))
        gathered.append([packed[h]] + [onward(packed[h], d) for d in range(1, chips)])
    swapped = swap(theirs)
    if chips > 1:
        gathered[0][1:] = passed(scalars, gathered[0][1:])
    prior = []
    branches, gate_parts = [], []
    for h in range(LOCAL_HEADS):
        results = attend(chips, shards, h, scalars, own, swapped, own, swapped, column, other, *gathered[h], *prior)
        branches.append(section_on(results[0]))
        gate_parts.append(results[1])
        prior = results[2:]
    returned = [onward(prior[d], -d) for d in range(1, chips)]
    branches[0], *returned = lax.optimization_barrier((branches[0], *returned))
    grad_mine, gate_mine, grad_theirs = call(
        lambda *refs: gradient_kernel(chips, *refs),
        scalars,
        [column_spec]
        + [whole((CHIP_ROWS, HALF_KEY))] * chips
        + [whole((CHIP_ROWS, HEAD_SIZE))] * LOCAL_HEADS,
        (other, prior[0], *returned, *gate_parts),
        (shape(SLOTS, HALF_KEY), shape(SLOTS, HEAD_SIZE, f32), shape(SLOTS, HALF_KEY + HEAD_SIZE)),
        (whole((SLOTS, HALF_KEY)), whole((SLOTS, HEAD_SIZE)), whole((SLOTS, HALF_KEY + HEAD_SIZE))),
        moved=8 * CHIP_ROWS * HALF_KEY,
    )
    grad_other = swap(grad_theirs)
    value_grad, gate_grad = call(
        finish_kernel,
        scalars,
        [
            whole((SLOTS, HALF_KEY)),
            whole((SLOTS, HEAD_SIZE)),
            whole((SLOTS, HALF_KEY + HEAD_SIZE)),
            whole((SLOTS, HEAD_SIZE)),
        ],
        (grad_mine, gate_mine, grad_other, column),
        (shape(SLOTS, CORES * HALF_KEY), shape(1, SLOTS)),
        (whole((SLOTS, CORES * HALF_KEY)), whole((1, SLOTS))),
        moved=8 * SLOTS * HALF_KEY,
    )
    branches[-1], value_grad = lax.optimization_barrier((branches[-1], value_grad))
    handed = ()
    for h in range(LOCAL_HEADS):
        mine, theirs = call(
            branch_kernel,
            scalars,
            [
                whole((CHIP_ROWS, GROUP_WIDTH)),
                pl.BlockSpec((META_ROWS, HEAD_SIZE), lambda i, s: (CHIP_ROWS // META_ROWS, 0)),
            ],
            (branches[h], branches[0]),
            (shape(SLOTS, GROUP_WIDTH), shape(SLOTS, GROUP_WIDTH)),
            (whole((SLOTS, GROUP_WIDTH)), whole((SLOTS, GROUP_WIDTH))),
            moved=7 * SLOTS * HALF_QUERY,
        )
        handed = (
            call(
                lambda *refs, h=h: join_kernel(h, *refs),
                scalars,
                [whole((SLOTS, GROUP_WIDTH))] * 2 + [far] * len(handed),
                (mine, swap(theirs), *handed),
                shape(SLOTS, CORES * HALF_QUERY),
                far,
                scratch=(pltpu.SemaphoreType.DMA((2,)),),
                moved=8 * SLOTS * GROUP_WIDTH,
                aliases={3: 0} if handed else {},
            ),
        )
    (handed,) = handed
    return (handed[None], value_grad[None], gate_grad)


def solution(mesh):
    rows = P("section", "ctx", None)
    flat = P("section", "ctx")
    return jax.shard_map(
        local,
        mesh=mesh,
        in_specs=(rows, rows, rows, rows, flat, flat, flat),
        out_specs=(rows, rows, flat),
        check_vma=False,
    )
```

```python
import math

import jax
import jax.numpy as jnp
from jax import lax
from jax.experimental import pallas as pl
from jax.experimental.pallas import tpu as pltpu
from jax.sharding import PartitionSpec as P

QUERY_HEADS = 24
KEY_VALUE_HEADS = 4
HEAD_SIZE = 128
BLOCK_ROWS = 128
MAXB = 2

CORES = 2
GROUP = QUERY_HEADS // KEY_VALUE_HEADS
LOCAL_HEADS = KEY_VALUE_HEADS // CORES
GROUP_WIDTH = GROUP * HEAD_SIZE
HALF_QUERY = LOCAL_HEADS * GROUP_WIDTH
HALF_KEY = LOCAL_HEADS * HEAD_SIZE
CHIP_BLOCKS = 2 * MAXB - 1
CHIP_ROWS = CHIP_BLOCKS * BLOCK_ROWS
META_ROWS = 16
SLOTS = MAXB * BLOCK_ROWS
MASKED = -1e30
VMEM_LIMIT = 48 * 1024 * 1024
f32 = jnp.float32
bf16 = jnp.bfloat16
i32 = jnp.int32
PAYLOAD = 2 * HALF_KEY + HEAD_SIZE


def params(limit):
    return pltpu.CompilerParams(vmem_limit_bytes=limit)


def whole(shape):
    return pl.BlockSpec(shape, lambda i, s: (0,) * len(shape))


def call(body, scalars, grid_in, operands, outs, out_specs, scratch=(), flops=0, moved=0, limit=VMEM_LIMIT, aliases={}):
    return pl.pallas_call(
        body,
        grid_spec=pltpu.PrefetchScalarGridSpec(
            num_scalar_prefetch=1,
            grid=(1,),
            in_specs=grid_in,
            out_specs=out_specs,
            scratch_shapes=list(scratch),
        ),
        out_shape=outs,
        compiler_params=params(limit),
        input_output_aliases=aliases,
        cost_estimate=pl.CostEstimate(flops=flops, bytes_accessed=moved, transcendentals=0),
    )(scalars, *operands)


def shape(rows, columns, kind=bf16):
    return jax.ShapeDtypeStruct((rows, columns), kind)


def rows_of(block):
    return pl.ds(pl.multiple_of(block * BLOCK_ROWS, BLOCK_ROWS), BLOCK_ROWS)


def my_core():
    return lax.axis_index("ctx") % CORES


def half(source, width, core):
    return source.at[0, :, pl.ds(pl.multiple_of(core * width, width), width)]


def pack_kernel(s, k, v, logits, out, column, own_kv, flat, arrived):
    core = my_core()
    moves = (
        (logits, flat),
        (half(k, HALF_KEY, 1 - core), out.at[:, 0:HALF_KEY]),
        (half(v, HALF_KEY, 1 - core), out.at[:, HALF_KEY : 2 * HALF_KEY]),
        (half(k, HALF_KEY, core), own_kv.at[:, 0:HALF_KEY]),
        (half(v, HALF_KEY, core), own_kv.at[:, HALF_KEY:]),
    )
    copies = [pltpu.make_async_copy(source, target, arrived.at[n]) for n, (source, target) in enumerate(moves)]
    for copy in copies:
        copy.start()
    copies[0].wait()
    count = s[0]
    for b in range(MAXB):
        row = flat[0:1, b * BLOCK_ROWS : (b + 1) * BLOCK_ROWS].astype(f32)
        tall = jnp.broadcast_to(row, (BLOCK_ROWS, BLOCK_ROWS)).T
        lane = lax.broadcasted_iota(i32, (BLOCK_ROWS, HEAD_SIZE), 1)
        rows = slice(b * BLOCK_ROWS, (b + 1) * BLOCK_ROWS)
        meta = jnp.where(lane < HEAD_SIZE // 2, tall, count.astype(f32)).astype(bf16)
        out[rows, 2 * HALF_KEY :] = meta
        column[rows, :] = meta
    for copy in copies[1:]:
        copy.wait()


def halves_kernel(s, q, cot, after, mine, theirs, arrived):
    core = my_core()
    copies = [
        pltpu.make_async_copy(
            half(source, HALF_QUERY, at), target.at[:, n * HALF_QUERY : (n + 1) * HALF_QUERY], arrived.at[n, m]
        )
        for n, source in enumerate((q, cot))
        for m, (at, target) in enumerate(((1 - core, theirs), (core, mine)))
    ]
    for copy in copies:
        copy.start()
    for copy in copies:
        copy.wait()


def pass_kernel(s, *refs):
    pass


def passed(scalars, arrays):
    anywhere = [pl.BlockSpec(memory_space=pl.ANY)] * len(arrays)
    return call(
        pass_kernel,
        scalars,
        anywhere,
        tuple(arrays),
        tuple(jax.ShapeDtypeStruct(x.shape, x.dtype) for x in arrays),
        tuple(anywhere),
        flops=15 * 10**9,
        aliases={n + 1: n for n in range(len(arrays))},
    )


def as_scalar(x):
    return jnp.max(x.astype(f32)).astype(i32)


def chip_counts(s, meta):
    own = s[0]
    other = as_scalar(meta[0:META_ROWS, HEAD_SIZE // 2 :])
    first = jnp.where(my_core() == 0, own, other)
    return first, own + other


def place_of(block, first, core):
    on_first = block < first
    slot = jnp.where(on_first, block, block - first)
    mine = jnp.where(on_first, 0, 1) == core
    return mine, slot


def chip_kernel(s, k, v, kr, vr, meta, *outs):
    *outs, pair = outs
    first, live = chip_counts(s, meta)
    lane = lax.broadcasted_iota(i32, (META_ROWS, HEAD_SIZE), 1)
    pair[...] = jnp.where(lane < HEAD_SIZE // 2, first.astype(f32), (live - first).astype(f32)).astype(bf16)
    for b in range(CHIP_BLOCKS):
        mine, slot = place_of(b, first, my_core())
        rows = slice(b * BLOCK_ROWS, (b + 1) * BLOCK_ROWS)

        def copy(keys, vals):
            for h in range(LOCAL_HEADS):
                cols = slice(h * HEAD_SIZE, (h + 1) * HEAD_SIZE)
                outs[h][rows, 0:HEAD_SIZE] = keys[rows_of(slot), cols]
                outs[h][rows, HEAD_SIZE:] = vals[rows_of(slot), cols]

        @pl.when(jnp.logical_and(b < live, mine))
        def _():
            copy(k, v)

        @pl.when(jnp.logical_and(b < live, jnp.logical_not(mine)))
        def _():
            copy(kr, vr)

        @pl.when(b >= live)
        def _():
            for h in range(LOCAL_HEADS):
                outs[h][rows, :] = jnp.zeros((BLOCK_ROWS, 2 * HEAD_SIZE), bf16)

    for h in range(LOCAL_HEADS):
        outs[h][CHIP_ROWS:, :] = jnp.broadcast_to(live.astype(f32), (META_ROWS, 2 * HEAD_SIZE)).astype(bf16)


def attend_kernel(chips, chunk, has_prior, s, *refs):
    q, qr, cot, cotr, column, columnr = refs[:6]
    at = 6
    kv = refs[at : at + 1] + refs[at + 1 : at + chips][::-1]
    at += chips
    prior = refs[at : at + chips] if has_prior else None
    at += chips if has_prior else 0
    branch, gate_part = refs[at : at + 2]
    at += 2
    dvs = refs[at : at + chips]
    at += chips
    kd, vd, qs, og, probs, acc, dv = refs[at:]
    steps = kd.shape[0] // chunk

    first, live = chip_counts(s, columnr)
    core = my_core()
    ones = jnp.ones((BLOCK_ROWS, HEAD_SIZE), bf16)
    vd[...] = jnp.zeros_like(vd)
    dv[...] = jnp.zeros_like(dv)

    held = [live] + [as_scalar(kv[d][CHIP_ROWS:, 0:HEAD_SIZE]) for d in range(1, chips)]
    starts = [None] * chips
    position = jnp.int32(0)
    for d in list(range(1, chips)) + [0]:
        starts[d] = position
        for b in range(CHIP_BLOCKS):

            @pl.when(b < held[d])
            def _(d=d, b=b, position=position):
                rows = slice(b * BLOCK_ROWS, (b + 1) * BLOCK_ROWS)
                to = rows_of(position + b)
                kd[to, :] = kv[d][rows, 0:HEAD_SIZE]
                vd[to, 0:HEAD_SIZE] = kv[d][rows, HEAD_SIZE:]
                vd[to, HEAD_SIZE:] = ones

        position = position + held[d]
    base = starts[0]
    scale = math.log2(math.e) / math.sqrt(HEAD_SIZE)
    tall = GROUP * BLOCK_ROWS

    def one_block(b, _):
        mine, slot = place_of(b, first, core)
        here = rows_of(slot)

        @pl.when(mine)
        def _():
            for i in range(GROUP):
                qs[i * BLOCK_ROWS : (i + 1) * BLOCK_ROWS, :] = q[here, i * HEAD_SIZE : (i + 1) * HEAD_SIZE]

        @pl.when(jnp.logical_not(mine))
        def _():
            for i in range(GROUP):
                qs[i * BLOCK_ROWS : (i + 1) * BLOCK_ROWS, :] = qr[here, i * HEAD_SIZE : (i + 1) * HEAD_SIZE]

        t = base + b

        def finish(grad, col):
            logit = jnp.broadcast_to(col[here, 0:1].astype(f32), (BLOCK_ROWS, HEAD_SIZE))
            gate = 1.0 / (1.0 + jnp.exp(-logit))
            total = jnp.zeros((BLOCK_ROWS, HEAD_SIZE), f32)
            for i in range(GROUP):
                rows = slice(i * BLOCK_ROWS, (i + 1) * BLOCK_ROWS)
                cols = slice(i * HEAD_SIZE, (i + 1) * HEAD_SIZE)
                inverse = 1.0 / acc[rows, HEAD_SIZE:]
                attended = acc[rows, 0:HEAD_SIZE] * inverse
                branch[rows_of(b), cols] = (gate * attended).astype(bf16)
                g = grad[here, cols].astype(f32)
                total = total + g * attended
                og[rows, :] = (gate * g * inverse).astype(bf16)
            gate_part[rows_of(b), :] = total

        def sweep(reach):
            key = lax.broadcasted_iota(i32, (BLOCK_ROWS, chunk), 1) + (reach - chunk)
            row = t * BLOCK_ROWS + lax.broadcasted_iota(i32, (BLOCK_ROWS, chunk), 0)
            allowed = key <= row
            for c in range(GROUP):
                w = slice(c * BLOCK_ROWS, (c + 1) * BLOCK_ROWS)
                x = lax.dot_general(
                    qs[w, :], kd[0:reach, :], (((1,), (1,)), ((), ())), preferred_element_type=f32
                )
                tail = jnp.where(allowed, x[:, reach - chunk :], MASKED)
                x = tail if reach == chunk else jnp.concatenate([x[:, : reach - chunk], tail], axis=1)
                p = jnp.exp2((x - jnp.max(x, axis=1, keepdims=True)) * scale).astype(bf16)
                probs[w, 0:reach] = p
                acc[w, :] = jnp.dot(p, vd[0:reach, :], preferred_element_type=f32)

            @pl.when(mine)
            def _():
                finish(cot, column)

            @pl.when(jnp.logical_not(mine))
            def _():
                finish(cotr, columnr)

            width = min(2 * BLOCK_ROWS, chunk)
            for c in range(reach // width):
                w = slice(c * width, (c + 1) * width)
                dv[w, :] += lax.dot_general(
                    probs[:, w], og[...], (((0,), (0,)), ((), ())), preferred_element_type=f32
                )

        last = t * BLOCK_ROWS // chunk
        for j in range(steps):

            @pl.when(last == j)
            def _(j=j):
                sweep((j + 1) * chunk)

        return 0

    lax.fori_loop(0, live, one_block, 0)
    if branch.shape[0] > CHIP_ROWS:
        lane = lax.broadcasted_iota(i32, (META_ROWS, GROUP_WIDTH), 1)
        counted = jnp.where(lane < HEAD_SIZE // 2, first.astype(f32), (live - first).astype(f32))
        branch[CHIP_ROWS:, :] = counted.astype(bf16)

    for b in range(CHIP_BLOCKS):
        rows = slice(b * BLOCK_ROWS, (b + 1) * BLOCK_ROWS)

        @pl.when(b >= live)
        def _():
            branch[rows, :] = jnp.zeros((BLOCK_ROWS, GROUP_WIDTH), bf16)
            gate_part[rows, :] = jnp.zeros((BLOCK_ROWS, HEAD_SIZE), f32)

        for d in range(chips):
            cols = slice(0, HEAD_SIZE)
            if has_prior:
                dvs[d][rows, 0:HEAD_SIZE] = prior[d][rows, :]
                cols = slice(HEAD_SIZE, 2 * HEAD_SIZE)

            @pl.when(b < held[d])
            def _():
                dvs[d][rows, cols] = dv[rows_of(starts[d] + b), :].astype(dvs[d].dtype)

            @pl.when(b >= held[d])
            def _():
                dvs[d][rows, cols] = jnp.zeros((BLOCK_ROWS, HEAD_SIZE), dvs[d].dtype)


def spread(slot, core, first, second, write, clear):
    held = jnp.where(core == 0, first, second)
    block = jnp.where(core == 0, slot, first + slot)

    @pl.when(slot < held)
    def _():
        write(rows_of(jnp.minimum(block, CHIP_BLOCKS - 1)))

    @pl.when(slot >= held)
    def _():
        clear()


def branch_kernel(s, part, pair, mine, theirs):
    first = as_scalar(pair[:, 0 : HEAD_SIZE // 2])
    second = as_scalar(pair[:, HEAD_SIZE // 2 :])
    for out, core in ((mine, my_core()), (theirs, 1 - my_core())):
        for slot in range(MAXB):
            rows = slice(slot * BLOCK_ROWS, (slot + 1) * BLOCK_ROWS)

            def write(source):
                out[rows, :] = part[source, :]

            def clear():
                out[rows, :] = jnp.zeros((BLOCK_ROWS, GROUP_WIDTH), bf16)

            spread(slot, core, first, second, write, clear)


def join_kernel(h, s, mine, theirs, *refs):
    out, sent = refs[-2:]
    core = my_core()
    copies = []
    for n, (at, part) in enumerate(((core, mine), (1 - core, theirs))):
        start = pl.multiple_of(at * HALF_QUERY + h * GROUP_WIDTH, HEAD_SIZE)
        copies.append(pltpu.make_async_copy(part, out.at[:, pl.ds(start, GROUP_WIDTH)], sent.at[n]))
        copies[-1].start()
    for copy in copies:
        copy.wait()


def gradient_kernel(chips, s, *refs):
    columnr = refs[0]
    own = refs[1]
    arrived = refs[2 : 1 + chips]
    gate_parts = refs[1 + chips : 1 + chips + LOCAL_HEADS]
    mine, gate_mine, theirs = refs[1 + chips + LOCAL_HEADS :]
    first, live = chip_counts(s, columnr)
    second = live - first
    for which, core in ((0, my_core()), (1, 1 - my_core())):
        for slot in range(MAXB):
            rows = slice(slot * BLOCK_ROWS, (slot + 1) * BLOCK_ROWS)

            def write(source):
                total = own[source, :]
                for other in arrived:
                    total = total + other[source, :].astype(f32)
                summed = gate_parts[0][source, :]
                for h in range(1, LOCAL_HEADS):
                    summed = summed + gate_parts[h][source, :]
                summed = jnp.broadcast_to(jnp.sum(summed, axis=1, keepdims=True), (BLOCK_ROWS, HEAD_SIZE))
                if which == 0:
                    mine[rows, :] = total.astype(bf16)
                    gate_mine[rows, :] = summed
                else:
                    theirs[rows, 0:HALF_KEY] = total.astype(bf16)
                    high = summed.astype(bf16)
                    low = (summed - high.astype(f32)).astype(bf16)
                    lane = lax.broadcasted_iota(i32, (BLOCK_ROWS, HEAD_SIZE), 1)
                    theirs[rows, HALF_KEY:] = jnp.where(lane < HEAD_SIZE // 2, high, low)

            def clear():
                if which == 0:
                    mine[rows, :] = jnp.zeros((BLOCK_ROWS, HALF_KEY), bf16)
                    gate_mine[rows, :] = jnp.zeros((BLOCK_ROWS, HEAD_SIZE), f32)
                else:
                    theirs[rows, :] = jnp.zeros((BLOCK_ROWS, HALF_KEY + HEAD_SIZE), bf16)

            spread(slot, core, first, second, write, clear)


def finish_kernel(s, mine, gate_mine, theirs, column, out, gate_out):
    @pl.when(my_core() == 0)
    def _():
        out[:, 0:HALF_KEY] = mine[...]
        out[:, HALF_KEY:] = theirs[:, 0:HALF_KEY]

    @pl.when(my_core() != 0)
    def _():
        out[:, 0:HALF_KEY] = theirs[:, 0:HALF_KEY]
        out[:, HALF_KEY:] = mine[...]

    half = HALF_KEY + HEAD_SIZE // 2
    for b in range(MAXB):
        rows = slice(b * BLOCK_ROWS, (b + 1) * BLOCK_ROWS)
        total = (
            gate_mine[rows, 0:1]
            + theirs[rows, HALF_KEY : HALF_KEY + 1].astype(f32)
            + theirs[rows, half : half + 1].astype(f32)
        )
        logit = column[rows, 0:1].astype(f32)
        gate = 1.0 / (1.0 + jnp.exp(-logit))
        full = jnp.broadcast_to(gate * (1.0 - gate) * total, (BLOCK_ROWS, HEAD_SIZE)).T
        gate_out[0:1, rows] = full[0:1, :].astype(bf16)


def fixed(width, at):
    return pl.BlockSpec((SLOTS, width), lambda i, s: (0, at))


def attend(chips, shards, h, scalars, *operands):
    steps = min(4, shards)
    chunk = -(-shards // steps) * BLOCK_ROWS
    reach = steps * chunk
    tall = GROUP * BLOCK_ROWS
    packed_rows = CHIP_ROWS + META_ROWS
    prior = len(operands) - 6 - chips
    sent_rows = CHIP_ROWS if h else packed_rows
    width = HEAD_SIZE * (2 if prior else 1)
    own_at = fixed(GROUP_WIDTH, h)
    column_spec = fixed(HEAD_SIZE, 2 * HALF_KEY // HEAD_SIZE)
    cot_at = fixed(GROUP_WIDTH, LOCAL_HEADS + h)
    return call(
        lambda *refs: attend_kernel(chips, chunk, bool(prior), *refs),
        scalars,
        [own_at, own_at, cot_at, cot_at, whole((SLOTS, HEAD_SIZE)), column_spec]
        + [whole((packed_rows, 2 * HEAD_SIZE))] * chips
        + [whole((CHIP_ROWS, HEAD_SIZE))] * prior,
        operands,
        (shape(sent_rows, GROUP_WIDTH), shape(CHIP_ROWS, HEAD_SIZE, f32), shape(CHIP_ROWS, width, f32))
        + tuple(shape(CHIP_ROWS, width) for _ in range(chips - 1)),
        (whole((sent_rows, GROUP_WIDTH)), whole((CHIP_ROWS, HEAD_SIZE))) + (whole((CHIP_ROWS, width)),) * chips,
        scratch=(
            pltpu.VMEM((reach, HEAD_SIZE), bf16),
            pltpu.VMEM((reach, 2 * HEAD_SIZE), bf16),
            pltpu.VMEM((tall, HEAD_SIZE), bf16),
            pltpu.VMEM((tall, HEAD_SIZE), bf16),
            pltpu.VMEM((tall, reach), bf16),
            pltpu.VMEM((tall, 2 * HEAD_SIZE), f32),
            pltpu.VMEM((reach, HEAD_SIZE), f32),
        ),
        flops=100 * tall * HEAD_SIZE * reach,
        moved=6 * packed_rows * GROUP_WIDTH,
    )


def local(queries, keys, values, cotangent, router_logits, positions, counts):
    shards = lax.axis_size("ctx")
    sections = lax.axis_size("section")
    chips = shards // CORES
    scalars = counts[0]
    def swap(x):
        return lax.ppermute(x, "ctx", [(i, i ^ 1) for i in range(shards)])

    def onward(x, by):
        step = by * CORES
        return lax.ppermute(x, "ctx", [(i, i + step) for i in range(shards) if 0 <= i + step < shards])

    def to_later(x):
        return [onward(x, d) for d in reversed(range(1, chips))][::-1]

    def section_on(x):
        return lax.ppermute(x, "section", [(i, (i + 1) % sections) for i in range(sections)])

    def near(x):
        return pltpu.with_memory_space_constraint(x, pltpu.HBM)

    far = pl.BlockSpec(memory_space=pltpu.HBM)
    column_spec = fixed(HEAD_SIZE, 2 * HALF_KEY // HEAD_SIZE)
    payload, column, own_kv = call(
        pack_kernel,
        scalars,
        [far, far, far],
        (near(keys), near(values), near(router_logits)),
        (shape(SLOTS, PAYLOAD), shape(SLOTS, HEAD_SIZE), shape(SLOTS, 2 * HALF_KEY)),
        tuple(whole((SLOTS, width)) for width in (PAYLOAD, HEAD_SIZE, 2 * HALF_KEY)),
        scratch=(pltpu.VMEM((1, SLOTS), bf16), pltpu.SemaphoreType.DMA((5,))),
        moved=4 * SLOTS * PAYLOAD * 2,
    )
    other = swap(payload)
    packed_rows = CHIP_ROWS + META_ROWS
    *packed, pair = call(
        chip_kernel,
        scalars,
        [fixed(HALF_KEY, 0), fixed(HALF_KEY, 1), fixed(HALF_KEY, 0), fixed(HALF_KEY, 1), column_spec],
        (own_kv, own_kv, other, other, other),
        tuple(shape(packed_rows, 2 * HEAD_SIZE) for _ in range(LOCAL_HEADS)) + (shape(META_ROWS, HEAD_SIZE),),
        tuple(whole((packed_rows, 2 * HEAD_SIZE)) for _ in range(LOCAL_HEADS)) + (whole((META_ROWS, HEAD_SIZE)),),
        moved=4 * packed_rows * HALF_KEY * 2,
    )
    gathered = [[packed[0]] + to_later(packed[0])]
    own, theirs = call(
        halves_kernel,
        scalars,
        [far, far, pl.BlockSpec(memory_space=pl.ANY)],
        (near(queries), near(cotangent), swap(pair)),
        (shape(SLOTS, 2 * HALF_QUERY), shape(SLOTS, 2 * HALF_QUERY)),
        (whole((SLOTS, 2 * HALF_QUERY)), whole((SLOTS, 2 * HALF_QUERY))),
        scratch=(pltpu.SemaphoreType.DMA((2, 2)),),
        moved=0,
    )
    for h in range(1, LOCAL_HEADS):
        packed[h], theirs = lax.optimization_barrier((packed[h], theirs))
        gathered.append([packed[h]] + to_later(packed[h]))
    swapped = swap(theirs)
    if chips > 1:
        gathered[0][:0:-1] = passed(scalars, gathered[0][:0:-1])
    prior = []
    branches, gate_parts = [], []
    for h in range(LOCAL_HEADS):
        results = attend(chips, shards, h, scalars, own, swapped, own, swapped, column, other, gathered[h][0], *gathered[h][:0:-1], *prior)
        branches.append(section_on(results[0]))
        gate_parts.append(results[1])
        prior = results[2:]
    returned = [onward(prior[d], -d) for d in range(1, chips)]
    branches[0], *returned = lax.optimization_barrier((branches[0], *returned))
    grad_mine, gate_mine, grad_theirs = call(
        lambda *refs: gradient_kernel(chips, *refs),
        scalars,
        [column_spec]
        + [whole((CHIP_ROWS, HALF_KEY))] * chips
        + [whole((CHIP_ROWS, HEAD_SIZE))] * LOCAL_HEADS,
        (other, prior[0], *returned, *gate_parts),
        (shape(SLOTS, HALF_KEY), shape(SLOTS, HEAD_SIZE, f32), shape(SLOTS, HALF_KEY + HEAD_SIZE)),
        (whole((SLOTS, HALF_KEY)), whole((SLOTS, HEAD_SIZE)), whole((SLOTS, HALF_KEY + HEAD_SIZE))),
        moved=8 * CHIP_ROWS * HALF_KEY,
    )
    grad_other = swap(grad_theirs)
    value_grad, gate_grad = call(
        finish_kernel,
        scalars,
        [
            whole((SLOTS, HALF_KEY)),
            whole((SLOTS, HEAD_SIZE)),
            whole((SLOTS, HALF_KEY + HEAD_SIZE)),
            whole((SLOTS, HEAD_SIZE)),
        ],
        (grad_mine, gate_mine, grad_other, column),
        (shape(SLOTS, CORES * HALF_KEY), shape(1, SLOTS)),
        (whole((SLOTS, CORES * HALF_KEY)), whole((1, SLOTS))),
        moved=8 * SLOTS * HALF_KEY,
    )
    branches[-1], value_grad = lax.optimization_barrier((branches[-1], value_grad))
    handed = ()
    for h in range(LOCAL_HEADS):
        mine, theirs = call(
            branch_kernel,
            scalars,
            [
                whole((CHIP_ROWS, GROUP_WIDTH)),
                pl.BlockSpec((META_ROWS, HEAD_SIZE), lambda i, s: (CHIP_ROWS // META_ROWS, 0)),
            ],
            (branches[h], branches[0]),
            (shape(SLOTS, GROUP_WIDTH), shape(SLOTS, GROUP_WIDTH)),
            (whole((SLOTS, GROUP_WIDTH)), whole((SLOTS, GROUP_WIDTH))),
            moved=7 * SLOTS * HALF_QUERY,
        )
        handed = (
            call(
                lambda *refs, h=h: join_kernel(h, *refs),
                scalars,
                [whole((SLOTS, GROUP_WIDTH))] * 2 + [far] * len(handed),
                (mine, swap(theirs), *handed),
                shape(SLOTS, CORES * HALF_QUERY),
                far,
                scratch=(pltpu.SemaphoreType.DMA((2,)),),
                moved=8 * SLOTS * GROUP_WIDTH,
                aliases={3: 0} if handed else {},
            ),
        )
    (handed,) = handed
    return (handed[None], value_grad[None], gate_grad)


def solution(mesh):
    rows = P("section", "ctx", None)
    flat = P("section", "ctx")
    return jax.shard_map(
        local,
        mesh=mesh,
        in_specs=(rows, rows, rows, rows, flat, flat, flat),
        out_specs=(rows, rows, flat),
        check_vma=False,
    )
```

```python
import math

import jax
import jax.numpy as jnp
from jax import lax
from jax.experimental import pallas as pl
from jax.experimental.pallas import tpu as pltpu
from jax.sharding import PartitionSpec as P

QUERY_HEADS = 24
KEY_VALUE_HEADS = 4
HEAD_SIZE = 128
BLOCK_ROWS = 128
MAXB = 2

CORES = 2
GROUP = QUERY_HEADS // KEY_VALUE_HEADS
LOCAL_HEADS = KEY_VALUE_HEADS // CORES
GROUP_WIDTH = GROUP * HEAD_SIZE
HALF_QUERY = LOCAL_HEADS * GROUP_WIDTH
HALF_KEY = LOCAL_HEADS * HEAD_SIZE
CHIP_BLOCKS = 2 * MAXB - 1
CHIP_ROWS = CHIP_BLOCKS * BLOCK_ROWS
META_ROWS = 16
SLOTS = MAXB * BLOCK_ROWS
MASKED = -1e30
VMEM_LIMIT = 48 * 1024 * 1024
f32 = jnp.float32
bf16 = jnp.bfloat16
i32 = jnp.int32
PAYLOAD = 2 * HALF_KEY + HEAD_SIZE


def params(limit):
    return pltpu.CompilerParams(vmem_limit_bytes=limit)


def whole(shape):
    return pl.BlockSpec(shape, lambda i, s: (0,) * len(shape))


def call(body, scalars, grid_in, operands, outs, out_specs, scratch=(), flops=0, moved=0, limit=VMEM_LIMIT, aliases={}):
    return pl.pallas_call(
        body,
        grid_spec=pltpu.PrefetchScalarGridSpec(
            num_scalar_prefetch=1,
            grid=(1,),
            in_specs=grid_in,
            out_specs=out_specs,
            scratch_shapes=list(scratch),
        ),
        out_shape=outs,
        compiler_params=params(limit),
        input_output_aliases=aliases,
        cost_estimate=pl.CostEstimate(flops=flops, bytes_accessed=moved, transcendentals=0),
    )(scalars, *operands)


def shape(rows, columns, kind=bf16):
    return jax.ShapeDtypeStruct((rows, columns), kind)


def rows_of(block):
    return pl.ds(pl.multiple_of(block * BLOCK_ROWS, BLOCK_ROWS), BLOCK_ROWS)


def my_core():
    return lax.axis_index("ctx") % CORES


def half(source, width, core):
    return source.at[0, :, pl.ds(pl.multiple_of(core * width, width), width)]


def pack_kernel(s, k, v, logits, out, column, own_kv, flat, arrived):
    core = my_core()
    moves = (
        (logits, flat),
        (half(k, HALF_KEY, 1 - core), out.at[:, 0:HALF_KEY]),
        (half(v, HALF_KEY, 1 - core), out.at[:, HALF_KEY : 2 * HALF_KEY]),
        (half(k, HALF_KEY, core), own_kv.at[:, 0:HALF_KEY]),
        (half(v, HALF_KEY, core), own_kv.at[:, HALF_KEY:]),
    )
    copies = [pltpu.make_async_copy(source, target, arrived.at[n]) for n, (source, target) in enumerate(moves)]
    for copy in copies:
        copy.start()
    copies[0].wait()
    count = s[0]
    for b in range(MAXB):
        row = flat[0:1, b * BLOCK_ROWS : (b + 1) * BLOCK_ROWS].astype(f32)
        tall = jnp.broadcast_to(row, (BLOCK_ROWS, BLOCK_ROWS)).T
        lane = lax.broadcasted_iota(i32, (BLOCK_ROWS, HEAD_SIZE), 1)
        rows = slice(b * BLOCK_ROWS, (b + 1) * BLOCK_ROWS)
        meta = jnp.where(lane < HEAD_SIZE // 2, tall, count.astype(f32)).astype(bf16)
        out[rows, 2 * HALF_KEY :] = meta
        column[rows, :] = meta
    for copy in copies[1:]:
        copy.wait()


def halves_kernel(s, q, cot, after, mine, theirs, arrived):
    core = my_core()
    copies = [
        pltpu.make_async_copy(
            half(source, HALF_QUERY, at), target.at[:, n * HALF_QUERY : (n + 1) * HALF_QUERY], arrived.at[n, m]
        )
        for n, source in enumerate((q, cot))
        for m, (at, target) in enumerate(((1 - core, theirs), (core, mine)))
    ]
    for copy in copies:
        copy.start()
    for copy in copies:
        copy.wait()


def pass_kernel(s, *refs):
    pass


def passed(scalars, arrays):
    anywhere = [pl.BlockSpec(memory_space=pl.ANY)] * len(arrays)
    return call(
        pass_kernel,
        scalars,
        anywhere,
        tuple(arrays),
        tuple(jax.ShapeDtypeStruct(x.shape, x.dtype) for x in arrays),
        tuple(anywhere),
        flops=15 * 10**9,
        aliases={n + 1: n for n in range(len(arrays))},
    )


def as_scalar(x):
    return jnp.max(x.astype(f32)).astype(i32)


def chip_counts(s, meta):
    own = s[0]
    other = as_scalar(meta[0:META_ROWS, HEAD_SIZE // 2 :])
    first = jnp.where(my_core() == 0, own, other)
    return first, own + other


def place_of(block, first, core):
    on_first = block < first
    slot = jnp.where(on_first, block, block - first)
    mine = jnp.where(on_first, 0, 1) == core
    return mine, slot


def chip_kernel(s, k, v, kr, vr, meta, *outs):
    *outs, pair = outs
    first, live = chip_counts(s, meta)
    lane = lax.broadcasted_iota(i32, (META_ROWS, HEAD_SIZE), 1)
    pair[...] = jnp.where(lane < HEAD_SIZE // 2, first.astype(f32), (live - first).astype(f32)).astype(bf16)
    for b in range(CHIP_BLOCKS):
        mine, slot = place_of(b, first, my_core())
        rows = slice(b * BLOCK_ROWS, (b + 1) * BLOCK_ROWS)

        def copy(keys, vals):
            for h in range(LOCAL_HEADS):
                cols = slice(h * HEAD_SIZE, (h + 1) * HEAD_SIZE)
                outs[h][rows, 0:HEAD_SIZE] = keys[rows_of(slot), cols]
                outs[h][rows, HEAD_SIZE:] = vals[rows_of(slot), cols]

        @pl.when(jnp.logical_and(b < live, mine))
        def _():
            copy(k, v)

        @pl.when(jnp.logical_and(b < live, jnp.logical_not(mine)))
        def _():
            copy(kr, vr)

        @pl.when(b >= live)
        def _():
            for h in range(LOCAL_HEADS):
                outs[h][rows, :] = jnp.zeros((BLOCK_ROWS, 2 * HEAD_SIZE), bf16)

    for h in range(LOCAL_HEADS):
        outs[h][CHIP_ROWS:, :] = jnp.broadcast_to(live.astype(f32), (META_ROWS, 2 * HEAD_SIZE)).astype(bf16)


def attend_kernel(chips, chunk, has_prior, s, *refs):
    q, qr, cot, cotr, column, columnr = refs[:6]
    at = 6
    kv = refs[at : at + chips]
    at += chips
    prior = refs[at : at + chips] if has_prior else None
    at += chips if has_prior else 0
    branch, gate_part = refs[at : at + 2]
    at += 2
    dvs = refs[at : at + chips]
    at += chips
    kd, vd, qs, og, probs, acc, dv = refs[at:]
    steps = kd.shape[0] // chunk

    first, live = chip_counts(s, columnr)
    core = my_core()
    ones = jnp.ones((BLOCK_ROWS, HEAD_SIZE), bf16)
    vd[...] = jnp.zeros_like(vd)
    dv[...] = jnp.zeros_like(dv)

    held = [live] + [as_scalar(kv[d][CHIP_ROWS:, 0:HEAD_SIZE]) for d in range(1, chips)]
    starts = [None] * chips
    position = jnp.int32(0)
    for d in list(range(1, chips)) + [0]:
        starts[d] = position
        for b in range(CHIP_BLOCKS):

            @pl.when(b < held[d])
            def _(d=d, b=b, position=position):
                rows = slice(b * BLOCK_ROWS, (b + 1) * BLOCK_ROWS)
                to = rows_of(position + b)
                kd[to, :] = kv[d][rows, 0:HEAD_SIZE]
                vd[to, 0:HEAD_SIZE] = kv[d][rows, HEAD_SIZE:]
                vd[to, HEAD_SIZE:] = ones

        position = position + held[d]
    base = starts[0]
    scale = math.log2(math.e) / math.sqrt(HEAD_SIZE)
    tall = GROUP * BLOCK_ROWS

    def one_block(b, _):
        mine, slot = place_of(b, first, core)
        here = rows_of(slot)

        @pl.when(mine)
        def _():
            for i in range(GROUP):
                qs[i * BLOCK_ROWS : (i + 1) * BLOCK_ROWS, :] = q[here, i * HEAD_SIZE : (i + 1) * HEAD_SIZE]

        @pl.when(jnp.logical_not(mine))
        def _():
            for i in range(GROUP):
                qs[i * BLOCK_ROWS : (i + 1) * BLOCK_ROWS, :] = qr[here, i * HEAD_SIZE : (i + 1) * HEAD_SIZE]

        t = base + b

        def finish(grad, col):
            logit = jnp.broadcast_to(col[here, 0:1].astype(f32), (BLOCK_ROWS, HEAD_SIZE))
            gate = 1.0 / (1.0 + jnp.exp(-logit))
            total = jnp.zeros((BLOCK_ROWS, HEAD_SIZE), f32)
            for i in range(GROUP):
                rows = slice(i * BLOCK_ROWS, (i + 1) * BLOCK_ROWS)
                cols = slice(i * HEAD_SIZE, (i + 1) * HEAD_SIZE)
                inverse = 1.0 / acc[rows, HEAD_SIZE:]
                attended = acc[rows, 0:HEAD_SIZE] * inverse
                branch[rows_of(b), cols] = (gate * attended).astype(bf16)
                g = grad[here, cols].astype(f32)
                total = total + g * attended
                og[rows, :] = (gate * g * inverse).astype(bf16)
            gate_part[rows_of(b), :] = total

        def sweep(reach):
            key = lax.broadcasted_iota(i32, (BLOCK_ROWS, chunk), 1) + (reach - chunk)
            row = t * BLOCK_ROWS + lax.broadcasted_iota(i32, (BLOCK_ROWS, chunk), 0)
            allowed = key <= row
            for c in range(GROUP):
                w = slice(c * BLOCK_ROWS, (c + 1) * BLOCK_ROWS)
                x = lax.dot_general(
                    qs[w, :], kd[0:reach, :], (((1,), (1,)), ((), ())), preferred_element_type=f32
                )
                tail = jnp.where(allowed, x[:, reach - chunk :], MASKED)
                x = tail if reach == chunk else jnp.concatenate([x[:, : reach - chunk], tail], axis=1)
                p = jnp.exp2((x - jnp.max(x, axis=1, keepdims=True)) * scale).astype(bf16)
                probs[w, 0:reach] = p
                acc[w, :] = jnp.dot(p, vd[0:reach, :], preferred_element_type=f32)

            @pl.when(mine)
            def _():
                finish(cot, column)

            @pl.when(jnp.logical_not(mine))
            def _():
                finish(cotr, columnr)

            width = min(2 * BLOCK_ROWS, chunk)
            for c in range(reach // width):
                w = slice(c * width, (c + 1) * width)
                dv[w, :] += lax.dot_general(
                    probs[:, w], og[...], (((0,), (0,)), ((), ())), preferred_element_type=f32
                )

        last = t * BLOCK_ROWS // chunk
        for j in range(steps):

            @pl.when(last == j)
            def _(j=j):
                sweep((j + 1) * chunk)

        return 0

    lax.fori_loop(0, live, one_block, 0)
    if branch.shape[0] > CHIP_ROWS:
        lane = lax.broadcasted_iota(i32, (META_ROWS, GROUP_WIDTH), 1)
        counted = jnp.where(lane < HEAD_SIZE // 2, first.astype(f32), (live - first).astype(f32))
        branch[CHIP_ROWS:, :] = counted.astype(bf16)

    for b in range(CHIP_BLOCKS):
        rows = slice(b * BLOCK_ROWS, (b + 1) * BLOCK_ROWS)

        @pl.when(b >= live)
        def _():
            branch[rows, :] = jnp.zeros((BLOCK_ROWS, GROUP_WIDTH), bf16)
            gate_part[rows, :] = jnp.zeros((BLOCK_ROWS, HEAD_SIZE), f32)

        for d in range(chips):
            cols = slice(0, HEAD_SIZE)
            if has_prior:
                dvs[d][rows, 0:HEAD_SIZE] = prior[d][rows, :]
                cols = slice(HEAD_SIZE, 2 * HEAD_SIZE)

            @pl.when(b < held[d])
            def _():
                dvs[d][rows, cols] = dv[rows_of(starts[d] + b), :].astype(dvs[d].dtype)

            @pl.when(b >= held[d])
            def _():
                dvs[d][rows, cols] = jnp.zeros((BLOCK_ROWS, HEAD_SIZE), dvs[d].dtype)


def spread(slot, core, first, second, write, clear):
    held = jnp.where(core == 0, first, second)
    block = jnp.where(core == 0, slot, first + slot)

    @pl.when(slot < held)
    def _():
        write(rows_of(jnp.minimum(block, CHIP_BLOCKS - 1)))

    @pl.when(slot >= held)
    def _():
        clear()


def branch_kernel(s, part, pair, mine, theirs):
    first = as_scalar(pair[:, 0 : HEAD_SIZE // 2])
    second = as_scalar(pair[:, HEAD_SIZE // 2 :])
    for out, core in ((mine, my_core()), (theirs, 1 - my_core())):
        for slot in range(MAXB):
            rows = slice(slot * BLOCK_ROWS, (slot + 1) * BLOCK_ROWS)

            def write(source):
                out[rows, :] = part[source, :]

            def clear():
                out[rows, :] = jnp.zeros((BLOCK_ROWS, GROUP_WIDTH), bf16)

            spread(slot, core, first, second, write, clear)


def join_kernel(h, s, mine, theirs, *refs):
    out, sent = refs[-2:]
    core = my_core()
    copies = []
    for n, (at, part) in enumerate(((core, mine), (1 - core, theirs))):
        start = pl.multiple_of(at * HALF_QUERY + h * GROUP_WIDTH, HEAD_SIZE)
        copies.append(pltpu.make_async_copy(part, out.at[:, pl.ds(start, GROUP_WIDTH)], sent.at[n]))
        copies[-1].start()
    for copy in copies:
        copy.wait()


def gradient_kernel(chips, s, *refs):
    columnr = refs[0]
    own = refs[1]
    arrived = refs[2 : 1 + chips]
    gate_parts = refs[1 + chips : 1 + chips + LOCAL_HEADS]
    mine, gate_mine, theirs = refs[1 + chips + LOCAL_HEADS :]
    first, live = chip_counts(s, columnr)
    second = live - first
    for which, core in ((0, my_core()), (1, 1 - my_core())):
        for slot in range(MAXB):
            rows = slice(slot * BLOCK_ROWS, (slot + 1) * BLOCK_ROWS)

            def write(source):
                total = own[source, :]
                for other in arrived:
                    total = total + other[source, :].astype(f32)
                summed = gate_parts[0][source, :]
                for h in range(1, LOCAL_HEADS):
                    summed = summed + gate_parts[h][source, :]
                summed = jnp.broadcast_to(jnp.sum(summed, axis=1, keepdims=True), (BLOCK_ROWS, HEAD_SIZE))
                if which == 0:
                    mine[rows, :] = total.astype(bf16)
                    gate_mine[rows, :] = summed
                else:
                    theirs[rows, 0:HALF_KEY] = total.astype(bf16)
                    high = summed.astype(bf16)
                    low = (summed - high.astype(f32)).astype(bf16)
                    lane = lax.broadcasted_iota(i32, (BLOCK_ROWS, HEAD_SIZE), 1)
                    theirs[rows, HALF_KEY:] = jnp.where(lane < HEAD_SIZE // 2, high, low)

            def clear():
                if which == 0:
                    mine[rows, :] = jnp.zeros((BLOCK_ROWS, HALF_KEY), bf16)
                    gate_mine[rows, :] = jnp.zeros((BLOCK_ROWS, HEAD_SIZE), f32)
                else:
                    theirs[rows, :] = jnp.zeros((BLOCK_ROWS, HALF_KEY + HEAD_SIZE), bf16)

            spread(slot, core, first, second, write, clear)


def finish_kernel(s, mine, gate_mine, theirs, column, out, gate_out):
    @pl.when(my_core() == 0)
    def _():
        out[:, 0:HALF_KEY] = mine[...]
        out[:, HALF_KEY:] = theirs[:, 0:HALF_KEY]

    @pl.when(my_core() != 0)
    def _():
        out[:, 0:HALF_KEY] = theirs[:, 0:HALF_KEY]
        out[:, HALF_KEY:] = mine[...]

    half = HALF_KEY + HEAD_SIZE // 2
    for b in range(MAXB):
        rows = slice(b * BLOCK_ROWS, (b + 1) * BLOCK_ROWS)
        total = (
            gate_mine[rows, 0:1]
            + theirs[rows, HALF_KEY : HALF_KEY + 1].astype(f32)
            + theirs[rows, half : half + 1].astype(f32)
        )
        logit = column[rows, 0:1].astype(f32)
        gate = 1.0 / (1.0 + jnp.exp(-logit))
        full = jnp.broadcast_to(gate * (1.0 - gate) * total, (BLOCK_ROWS, HEAD_SIZE)).T
        gate_out[0:1, rows] = full[0:1, :].astype(bf16)


def fixed(width, at):
    return pl.BlockSpec((SLOTS, width), lambda i, s: (0, at))


def attend(chips, shards, h, scalars, *operands):
    steps = min(4, shards)
    chunk = -(-shards // steps) * BLOCK_ROWS
    reach = steps * chunk
    tall = GROUP * BLOCK_ROWS
    packed_rows = CHIP_ROWS + META_ROWS
    prior = len(operands) - 6 - chips
    sent_rows = CHIP_ROWS if h else packed_rows
    width = HEAD_SIZE * (2 if prior else 1)
    own_at = fixed(GROUP_WIDTH, h)
    column_spec = fixed(HEAD_SIZE, 2 * HALF_KEY // HEAD_SIZE)
    cot_at = fixed(GROUP_WIDTH, LOCAL_HEADS + h)
    return call(
        lambda *refs: attend_kernel(chips, chunk, bool(prior), *refs),
        scalars,
        [own_at, own_at, cot_at, cot_at, whole((SLOTS, HEAD_SIZE)), column_spec]
        + [whole((packed_rows, 2 * HEAD_SIZE))] * chips
        + [whole((CHIP_ROWS, HEAD_SIZE))] * prior,
        operands,
        (shape(sent_rows, GROUP_WIDTH), shape(CHIP_ROWS, HEAD_SIZE, f32), shape(CHIP_ROWS, width, f32))
        + tuple(shape(CHIP_ROWS, width) for _ in range(chips - 1)),
        (whole((sent_rows, GROUP_WIDTH)), whole((CHIP_ROWS, HEAD_SIZE))) + (whole((CHIP_ROWS, width)),) * chips,
        scratch=(
            pltpu.VMEM((reach, HEAD_SIZE), bf16),
            pltpu.VMEM((reach, 2 * HEAD_SIZE), bf16),
            pltpu.VMEM((tall, HEAD_SIZE), bf16),
            pltpu.VMEM((tall, HEAD_SIZE), bf16),
            pltpu.VMEM((tall, reach), bf16),
            pltpu.VMEM((tall, 2 * HEAD_SIZE), f32),
            pltpu.VMEM((reach, HEAD_SIZE), f32),
        ),
        flops=100 * tall * HEAD_SIZE * reach,
        moved=6 * packed_rows * GROUP_WIDTH,
    )


def local(queries, keys, values, cotangent, router_logits, positions, counts):
    shards = lax.axis_size("ctx")
    sections = lax.axis_size("section")
    chips = shards // CORES
    scalars = counts[0]
    def swap(x):
        return lax.ppermute(x, "ctx", [(i, i ^ 1) for i in range(shards)])

    def onward(x, by):
        step = by * CORES
        return lax.ppermute(x, "ctx", [(i, i + step) for i in range(shards) if 0 <= i + step < shards])

    def to_later(x):
        return [onward(x, d) for d in reversed(range(1, chips))][::-1]

    def section_on(x):
        return lax.ppermute(x, "section", [(i, (i + 1) % sections) for i in range(sections)])

    def near(x):
        return pltpu.with_memory_space_constraint(x, pltpu.HBM)

    far = pl.BlockSpec(memory_space=pltpu.HBM)
    column_spec = fixed(HEAD_SIZE, 2 * HALF_KEY // HEAD_SIZE)
    payload, column, own_kv = call(
        pack_kernel,
        scalars,
        [far, far, far],
        (near(keys), near(values), near(router_logits)),
        (shape(SLOTS, PAYLOAD), shape(SLOTS, HEAD_SIZE), shape(SLOTS, 2 * HALF_KEY)),
        tuple(whole((SLOTS, width)) for width in (PAYLOAD, HEAD_SIZE, 2 * HALF_KEY)),
        scratch=(pltpu.VMEM((1, SLOTS), bf16), pltpu.SemaphoreType.DMA((5,))),
        moved=4 * SLOTS * PAYLOAD * 2,
    )
    other = swap(payload)
    packed_rows = CHIP_ROWS + META_ROWS
    *packed, pair = call(
        chip_kernel,
        scalars,
        [fixed(HALF_KEY, 0), fixed(HALF_KEY, 1), fixed(HALF_KEY, 0), fixed(HALF_KEY, 1), column_spec],
        (own_kv, own_kv, other, other, other),
        tuple(shape(packed_rows, 2 * HEAD_SIZE) for _ in range(LOCAL_HEADS)) + (shape(META_ROWS, HEAD_SIZE),),
        tuple(whole((packed_rows, 2 * HEAD_SIZE)) for _ in range(LOCAL_HEADS)) + (whole((META_ROWS, HEAD_SIZE)),),
        moved=4 * packed_rows * HALF_KEY * 2,
    )
    gathered = [[packed[0]] + to_later(packed[0])]
    own, theirs = call(
        halves_kernel,
        scalars,
        [far, far, pl.BlockSpec(memory_space=pl.ANY)],
        (near(queries), near(cotangent), swap(pair)),
        (shape(SLOTS, 2 * HALF_QUERY), shape(SLOTS, 2 * HALF_QUERY)),
        (whole((SLOTS, 2 * HALF_QUERY)), whole((SLOTS, 2 * HALF_QUERY))),
        scratch=(pltpu.SemaphoreType.DMA((2, 2)),),
        moved=0,
    )
    for h in range(1, LOCAL_HEADS):
        packed[h], theirs = lax.optimization_barrier((packed[h], theirs))
        gathered.append([packed[h]] + to_later(packed[h]))
    swapped = swap(theirs)
    if chips > 1:
        gathered[0][:0:-1] = passed(scalars, gathered[0][:0:-1])
    prior = []
    branches, gate_parts = [], []
    for h in range(LOCAL_HEADS):
        results = attend(chips, shards, h, scalars, own, swapped, own, swapped, column, other, *gathered[h], *prior)
        branches.append(section_on(results[0]))
        gate_parts.append(results[1])
        prior = results[2:]
    returned = [onward(prior[d], -d) for d in range(1, chips)]
    branches[0], *returned = lax.optimization_barrier((branches[0], *returned))
    grad_mine, gate_mine, grad_theirs = call(
        lambda *refs: gradient_kernel(chips, *refs),
        scalars,
        [column_spec]
        + [whole((CHIP_ROWS, HALF_KEY))] * chips
        + [whole((CHIP_ROWS, HEAD_SIZE))] * LOCAL_HEADS,
        (other, prior[0], *returned, *gate_parts),
        (shape(SLOTS, HALF_KEY), shape(SLOTS, HEAD_SIZE, f32), shape(SLOTS, HALF_KEY + HEAD_SIZE)),
        (whole((SLOTS, HALF_KEY)), whole((SLOTS, HEAD_SIZE)), whole((SLOTS, HALF_KEY + HEAD_SIZE))),
        moved=8 * CHIP_ROWS * HALF_KEY,
    )
    grad_other = swap(grad_theirs)
    value_grad, gate_grad = call(
        finish_kernel,
        scalars,
        [
            whole((SLOTS, HALF_KEY)),
            whole((SLOTS, HEAD_SIZE)),
            whole((SLOTS, HALF_KEY + HEAD_SIZE)),
            whole((SLOTS, HEAD_SIZE)),
        ],
        (grad_mine, gate_mine, grad_other, column),
        (shape(SLOTS, CORES * HALF_KEY), shape(1, SLOTS)),
        (whole((SLOTS, CORES * HALF_KEY)), whole((1, SLOTS))),
        moved=8 * SLOTS * HALF_KEY,
    )
    branches[-1], value_grad = lax.optimization_barrier((branches[-1], value_grad))
    handed = ()
    for h in range(LOCAL_HEADS):
        mine, theirs = call(
            branch_kernel,
            scalars,
            [
                whole((CHIP_ROWS, GROUP_WIDTH)),
                pl.BlockSpec((META_ROWS, HEAD_SIZE), lambda i, s: (CHIP_ROWS // META_ROWS, 0)),
            ],
            (branches[h], branches[0]),
            (shape(SLOTS, GROUP_WIDTH), shape(SLOTS, GROUP_WIDTH)),
            (whole((SLOTS, GROUP_WIDTH)), whole((SLOTS, GROUP_WIDTH))),
            moved=7 * SLOTS * HALF_QUERY,
        )
        handed = (
            call(
                lambda *refs, h=h: join_kernel(h, *refs),
                scalars,
                [whole((SLOTS, GROUP_WIDTH))] * 2 + [far] * len(handed),
                (mine, swap(theirs), *handed),
                shape(SLOTS, CORES * HALF_QUERY),
                far,
                scratch=(pltpu.SemaphoreType.DMA((2,)),),
                moved=8 * SLOTS * GROUP_WIDTH,
                aliases={3: 0} if handed else {},
            ),
        )
    (handed,) = handed
    return (handed[None], value_grad[None], gate_grad)


def solution(mesh):
    rows = P("section", "ctx", None)
    flat = P("section", "ctx")
    return jax.shard_map(
        local,
        mesh=mesh,
        in_specs=(rows, rows, rows, rows, flat, flat, flat),
        out_specs=(rows, rows, flat),
        check_vma=False,
    )
```

```python
import math

import jax
import jax.numpy as jnp
from jax import lax
from jax.experimental import pallas as pl
from jax.experimental.pallas import tpu as pltpu
from jax.sharding import PartitionSpec as P

QUERY_HEADS = 24
KEY_VALUE_HEADS = 4
HEAD_SIZE = 128
BLOCK_ROWS = 128
MAXB = 2

CORES = 2
GROUP = QUERY_HEADS // KEY_VALUE_HEADS
LOCAL_HEADS = KEY_VALUE_HEADS // CORES
GROUP_WIDTH = GROUP * HEAD_SIZE
HALF_QUERY = LOCAL_HEADS * GROUP_WIDTH
HALF_KEY = LOCAL_HEADS * HEAD_SIZE
CHIP_BLOCKS = 2 * MAXB - 1
CHIP_ROWS = CHIP_BLOCKS * BLOCK_ROWS
META_ROWS = 16
SLOTS = MAXB * BLOCK_ROWS
MASKED = -1e30
VMEM_LIMIT = 48 * 1024 * 1024
f32 = jnp.float32
bf16 = jnp.bfloat16
i32 = jnp.int32
PAYLOAD = 2 * HALF_KEY + HEAD_SIZE


def params(limit):
    return pltpu.CompilerParams(vmem_limit_bytes=limit)


def whole(shape):
    return pl.BlockSpec(shape, lambda i, s: (0,) * len(shape))


def call(body, scalars, grid_in, operands, outs, out_specs, scratch=(), flops=0, moved=0, limit=VMEM_LIMIT, aliases={}):
    return pl.pallas_call(
        body,
        grid_spec=pltpu.PrefetchScalarGridSpec(
            num_scalar_prefetch=1,
            grid=(1,),
            in_specs=grid_in,
            out_specs=out_specs,
            scratch_shapes=list(scratch),
        ),
        out_shape=outs,
        compiler_params=params(limit),
        input_output_aliases=aliases,
        cost_estimate=pl.CostEstimate(flops=flops, bytes_accessed=moved, transcendentals=0),
    )(scalars, *operands)


def shape(rows, columns, kind=bf16):
    return jax.ShapeDtypeStruct((rows, columns), kind)


def rows_of(block):
    return pl.ds(pl.multiple_of(block * BLOCK_ROWS, BLOCK_ROWS), BLOCK_ROWS)


def my_core():
    return lax.axis_index("ctx") % CORES


def half(source, width, core):
    return source.at[0, :, pl.ds(pl.multiple_of(core * width, width), width)]


def pack_kernel(s, k, v, logits, out, column, own_kv, flat, arrived):
    core = my_core()
    moves = (
        (logits, flat),
        (half(k, HALF_KEY, 1 - core), out.at[:, 0:HALF_KEY]),
        (half(v, HALF_KEY, 1 - core), out.at[:, HALF_KEY : 2 * HALF_KEY]),
        (half(k, HALF_KEY, core), own_kv.at[:, 0:HALF_KEY]),
        (half(v, HALF_KEY, core), own_kv.at[:, HALF_KEY:]),
    )
    copies = [pltpu.make_async_copy(source, target, arrived.at[n]) for n, (source, target) in enumerate(moves)]
    for copy in copies:
        copy.start()
    copies[0].wait()
    count = s[0]
    for b in range(MAXB):
        row = flat[0:1, b * BLOCK_ROWS : (b + 1) * BLOCK_ROWS].astype(f32)
        tall = jnp.broadcast_to(row, (BLOCK_ROWS, BLOCK_ROWS)).T
        lane = lax.broadcasted_iota(i32, (BLOCK_ROWS, HEAD_SIZE), 1)
        rows = slice(b * BLOCK_ROWS, (b + 1) * BLOCK_ROWS)
        meta = jnp.where(lane < HEAD_SIZE // 2, tall, count.astype(f32)).astype(bf16)
        out[rows, 2 * HALF_KEY :] = meta
        column[rows, :] = meta
    for copy in copies[1:]:
        copy.wait()


def halves_kernel(s, q, cot, after, mine, theirs, arrived):
    core = my_core()
    copies = [
        pltpu.make_async_copy(
            half(source, HALF_QUERY, at), target.at[:, n * HALF_QUERY : (n + 1) * HALF_QUERY], arrived.at[n, m]
        )
        for n, source in enumerate((q, cot))
        for m, (at, target) in enumerate(((1 - core, theirs), (core, mine)))
    ]
    for copy in copies:
        copy.start()
    for copy in copies:
        copy.wait()


def pass_kernel(s, *refs):
    pass


def passed(scalars, arrays):
    anywhere = [pl.BlockSpec(memory_space=pl.ANY)] * len(arrays)
    return call(
        pass_kernel,
        scalars,
        anywhere,
        tuple(arrays),
        tuple(jax.ShapeDtypeStruct(x.shape, x.dtype) for x in arrays),
        tuple(anywhere),
        flops=15 * 10**9,
        aliases={n + 1: n for n in range(len(arrays))},
    )


def as_scalar(x):
    return jnp.max(x.astype(f32)).astype(i32)


def chip_counts(s, meta):
    own = s[0]
    other = as_scalar(meta[0:META_ROWS, HEAD_SIZE // 2 :])
    first = jnp.where(my_core() == 0, own, other)
    return first, own + other


def place_of(block, first, core):
    on_first = block < first
    slot = jnp.where(on_first, block, block - first)
    mine = jnp.where(on_first, 0, 1) == core
    return mine, slot


def chip_kernel(s, k, v, kr, vr, meta, *outs):
    *outs, pair = outs
    first, live = chip_counts(s, meta)
    lane = lax.broadcasted_iota(i32, (META_ROWS, HEAD_SIZE), 1)
    pair[...] = jnp.where(lane < HEAD_SIZE // 2, first.astype(f32), (live - first).astype(f32)).astype(bf16)
    for b in range(CHIP_BLOCKS):
        mine, slot = place_of(b, first, my_core())
        rows = slice(b * BLOCK_ROWS, (b + 1) * BLOCK_ROWS)

        def copy(keys, vals):
            for h in range(LOCAL_HEADS):
                cols = slice(h * HEAD_SIZE, (h + 1) * HEAD_SIZE)
                outs[h][rows, 0:HEAD_SIZE] = keys[rows_of(slot), cols]
                outs[h][rows, HEAD_SIZE:] = vals[rows_of(slot), cols]

        @pl.when(jnp.logical_and(b < live, mine))
        def _():
            copy(k, v)

        @pl.when(jnp.logical_and(b < live, jnp.logical_not(mine)))
        def _():
            copy(kr, vr)

        @pl.when(b >= live)
        def _():
            for h in range(LOCAL_HEADS):
                outs[h][rows, :] = jnp.zeros((BLOCK_ROWS, 2 * HEAD_SIZE), bf16)

    for h in range(LOCAL_HEADS):
        outs[h][CHIP_ROWS:, :] = jnp.broadcast_to(live.astype(f32), (META_ROWS, 2 * HEAD_SIZE)).astype(bf16)


def attend_kernel(chips, chunk, has_prior, s, *refs):
    q, qr, cot, cotr, column, columnr = refs[:6]
    at = 6
    far = refs[at + 1 : at + chips]
    kv = refs[at : at + 1] + far[-1:] + far[:-1]
    at += chips
    prior = refs[at : at + chips] if has_prior else None
    at += chips if has_prior else 0
    branch, gate_part = refs[at : at + 2]
    at += 2
    dvs = refs[at : at + chips]
    at += chips
    kd, vd, qs, og, probs, acc, dv = refs[at:]
    steps = kd.shape[0] // chunk

    first, live = chip_counts(s, columnr)
    core = my_core()
    ones = jnp.ones((BLOCK_ROWS, HEAD_SIZE), bf16)
    vd[...] = jnp.zeros_like(vd)
    dv[...] = jnp.zeros_like(dv)

    held = [live] + [as_scalar(kv[d][CHIP_ROWS:, 0:HEAD_SIZE]) for d in range(1, chips)]
    starts = [None] * chips
    position = jnp.int32(0)
    for d in list(range(1, chips)) + [0]:
        starts[d] = position
        for b in range(CHIP_BLOCKS):

            @pl.when(b < held[d])
            def _(d=d, b=b, position=position):
                rows = slice(b * BLOCK_ROWS, (b + 1) * BLOCK_ROWS)
                to = rows_of(position + b)
                kd[to, :] = kv[d][rows, 0:HEAD_SIZE]
                vd[to, 0:HEAD_SIZE] = kv[d][rows, HEAD_SIZE:]
                vd[to, HEAD_SIZE:] = ones

        position = position + held[d]
    base = starts[0]
    scale = math.log2(math.e) / math.sqrt(HEAD_SIZE)
    tall = GROUP * BLOCK_ROWS

    def one_block(b, _):
        mine, slot = place_of(b, first, core)
        here = rows_of(slot)

        @pl.when(mine)
        def _():
            for i in range(GROUP):
                qs[i * BLOCK_ROWS : (i + 1) * BLOCK_ROWS, :] = q[here, i * HEAD_SIZE : (i + 1) * HEAD_SIZE]

        @pl.when(jnp.logical_not(mine))
        def _():
            for i in range(GROUP):
                qs[i * BLOCK_ROWS : (i + 1) * BLOCK_ROWS, :] = qr[here, i * HEAD_SIZE : (i + 1) * HEAD_SIZE]

        t = base + b

        def finish(grad, col):
            logit = jnp.broadcast_to(col[here, 0:1].astype(f32), (BLOCK_ROWS, HEAD_SIZE))
            gate = 1.0 / (1.0 + jnp.exp(-logit))
            total = jnp.zeros((BLOCK_ROWS, HEAD_SIZE), f32)
            for i in range(GROUP):
                rows = slice(i * BLOCK_ROWS, (i + 1) * BLOCK_ROWS)
                cols = slice(i * HEAD_SIZE, (i + 1) * HEAD_SIZE)
                inverse = 1.0 / acc[rows, HEAD_SIZE:]
                attended = acc[rows, 0:HEAD_SIZE] * inverse
                branch[rows_of(b), cols] = (gate * attended).astype(bf16)
                g = grad[here, cols].astype(f32)
                total = total + g * attended
                og[rows, :] = (gate * g * inverse).astype(bf16)
            gate_part[rows_of(b), :] = total

        def sweep(reach):
            key = lax.broadcasted_iota(i32, (BLOCK_ROWS, chunk), 1) + (reach - chunk)
            row = t * BLOCK_ROWS + lax.broadcasted_iota(i32, (BLOCK_ROWS, chunk), 0)
            allowed = key <= row
            for c in range(GROUP):
                w = slice(c * BLOCK_ROWS, (c + 1) * BLOCK_ROWS)
                x = lax.dot_general(
                    qs[w, :], kd[0:reach, :], (((1,), (1,)), ((), ())), preferred_element_type=f32
                )
                tail = jnp.where(allowed, x[:, reach - chunk :], MASKED)
                x = tail if reach == chunk else jnp.concatenate([x[:, : reach - chunk], tail], axis=1)
                p = jnp.exp2((x - jnp.max(x, axis=1, keepdims=True)) * scale).astype(bf16)
                probs[w, 0:reach] = p
                acc[w, :] = jnp.dot(p, vd[0:reach, :], preferred_element_type=f32)

            @pl.when(mine)
            def _():
                finish(cot, column)

            @pl.when(jnp.logical_not(mine))
            def _():
                finish(cotr, columnr)

            width = min(2 * BLOCK_ROWS, chunk)
            for c in range(reach // width):
                w = slice(c * width, (c + 1) * width)
                dv[w, :] += lax.dot_general(
                    probs[:, w], og[...], (((0,), (0,)), ((), ())), preferred_element_type=f32
                )

        last = t * BLOCK_ROWS // chunk
        for j in range(steps):

            @pl.when(last == j)
            def _(j=j):
                sweep((j + 1) * chunk)

        return 0

    lax.fori_loop(0, live, one_block, 0)
    if branch.shape[0] > CHIP_ROWS:
        lane = lax.broadcasted_iota(i32, (META_ROWS, GROUP_WIDTH), 1)
        counted = jnp.where(lane < HEAD_SIZE // 2, first.astype(f32), (live - first).astype(f32))
        branch[CHIP_ROWS:, :] = counted.astype(bf16)

    for b in range(CHIP_BLOCKS):
        rows = slice(b * BLOCK_ROWS, (b + 1) * BLOCK_ROWS)

        @pl.when(b >= live)
        def _():
            branch[rows, :] = jnp.zeros((BLOCK_ROWS, GROUP_WIDTH), bf16)
            gate_part[rows, :] = jnp.zeros((BLOCK_ROWS, HEAD_SIZE), f32)

        for d in range(chips):
            cols = slice(0, HEAD_SIZE)
            if has_prior:
                dvs[d][rows, 0:HEAD_SIZE] = prior[d][rows, :]
                cols = slice(HEAD_SIZE, 2 * HEAD_SIZE)

            @pl.when(b < held[d])
            def _():
                dvs[d][rows, cols] = dv[rows_of(starts[d] + b), :].astype(dvs[d].dtype)

            @pl.when(b >= held[d])
            def _():
                dvs[d][rows, cols] = jnp.zeros((BLOCK_ROWS, HEAD_SIZE), dvs[d].dtype)


def spread(slot, core, first, second, write, clear):
    held = jnp.where(core == 0, first, second)
    block = jnp.where(core == 0, slot, first + slot)

    @pl.when(slot < held)
    def _():
        write(rows_of(jnp.minimum(block, CHIP_BLOCKS - 1)))

    @pl.when(slot >= held)
    def _():
        clear()


def branch_kernel(s, part, pair, mine, theirs):
    first = as_scalar(pair[:, 0 : HEAD_SIZE // 2])
    second = as_scalar(pair[:, HEAD_SIZE // 2 :])
    for out, core in ((mine, my_core()), (theirs, 1 - my_core())):
        for slot in range(MAXB):
            rows = slice(slot * BLOCK_ROWS, (slot + 1) * BLOCK_ROWS)

            def write(source):
                out[rows, :] = part[source, :]

            def clear():
                out[rows, :] = jnp.zeros((BLOCK_ROWS, GROUP_WIDTH), bf16)

            spread(slot, core, first, second, write, clear)


def join_kernel(h, s, mine, theirs, *refs):
    out, sent = refs[-2:]
    core = my_core()
    copies = []
    for n, (at, part) in enumerate(((core, mine), (1 - core, theirs))):
        start = pl.multiple_of(at * HALF_QUERY + h * GROUP_WIDTH, HEAD_SIZE)
        copies.append(pltpu.make_async_copy(part, out.at[:, pl.ds(start, GROUP_WIDTH)], sent.at[n]))
        copies[-1].start()
    for copy in copies:
        copy.wait()


def gradient_kernel(chips, s, *refs):
    columnr = refs[0]
    own = refs[1]
    arrived = refs[2 : 1 + chips]
    gate_parts = refs[1 + chips : 1 + chips + LOCAL_HEADS]
    mine, gate_mine, theirs = refs[1 + chips + LOCAL_HEADS :]
    first, live = chip_counts(s, columnr)
    second = live - first
    for which, core in ((0, my_core()), (1, 1 - my_core())):
        for slot in range(MAXB):
            rows = slice(slot * BLOCK_ROWS, (slot + 1) * BLOCK_ROWS)

            def write(source):
                total = own[source, :]
                for other in arrived:
                    total = total + other[source, :].astype(f32)
                summed = gate_parts[0][source, :]
                for h in range(1, LOCAL_HEADS):
                    summed = summed + gate_parts[h][source, :]
                summed = jnp.broadcast_to(jnp.sum(summed, axis=1, keepdims=True), (BLOCK_ROWS, HEAD_SIZE))
                if which == 0:
                    mine[rows, :] = total.astype(bf16)
                    gate_mine[rows, :] = summed
                else:
                    theirs[rows, 0:HALF_KEY] = total.astype(bf16)
                    high = summed.astype(bf16)
                    low = (summed - high.astype(f32)).astype(bf16)
                    lane = lax.broadcasted_iota(i32, (BLOCK_ROWS, HEAD_SIZE), 1)
                    theirs[rows, HALF_KEY:] = jnp.where(lane < HEAD_SIZE // 2, high, low)

            def clear():
                if which == 0:
                    mine[rows, :] = jnp.zeros((BLOCK_ROWS, HALF_KEY), bf16)
                    gate_mine[rows, :] = jnp.zeros((BLOCK_ROWS, HEAD_SIZE), f32)
                else:
                    theirs[rows, :] = jnp.zeros((BLOCK_ROWS, HALF_KEY + HEAD_SIZE), bf16)

            spread(slot, core, first, second, write, clear)


def finish_kernel(s, mine, gate_mine, theirs, column, out, gate_out):
    @pl.when(my_core() == 0)
    def _():
        out[:, 0:HALF_KEY] = mine[...]
        out[:, HALF_KEY:] = theirs[:, 0:HALF_KEY]

    @pl.when(my_core() != 0)
    def _():
        out[:, 0:HALF_KEY] = theirs[:, 0:HALF_KEY]
        out[:, HALF_KEY:] = mine[...]

    half = HALF_KEY + HEAD_SIZE // 2
    for b in range(MAXB):
        rows = slice(b * BLOCK_ROWS, (b + 1) * BLOCK_ROWS)
        total = (
            gate_mine[rows, 0:1]
            + theirs[rows, HALF_KEY : HALF_KEY + 1].astype(f32)
            + theirs[rows, half : half + 1].astype(f32)
        )
        logit = column[rows, 0:1].astype(f32)
        gate = 1.0 / (1.0 + jnp.exp(-logit))
        full = jnp.broadcast_to(gate * (1.0 - gate) * total, (BLOCK_ROWS, HEAD_SIZE)).T
        gate_out[0:1, rows] = full[0:1, :].astype(bf16)


def fixed(width, at):
    return pl.BlockSpec((SLOTS, width), lambda i, s: (0, at))


def attend(chips, shards, h, scalars, *operands):
    steps = min(4, shards)
    chunk = -(-shards // steps) * BLOCK_ROWS
    reach = steps * chunk
    tall = GROUP * BLOCK_ROWS
    packed_rows = CHIP_ROWS + META_ROWS
    prior = len(operands) - 6 - chips
    sent_rows = CHIP_ROWS if h else packed_rows
    width = HEAD_SIZE * (2 if prior else 1)
    own_at = fixed(GROUP_WIDTH, h)
    column_spec = fixed(HEAD_SIZE, 2 * HALF_KEY // HEAD_SIZE)
    cot_at = fixed(GROUP_WIDTH, LOCAL_HEADS + h)
    return call(
        lambda *refs: attend_kernel(chips, chunk, bool(prior), *refs),
        scalars,
        [own_at, own_at, cot_at, cot_at, whole((SLOTS, HEAD_SIZE)), column_spec]
        + [whole((packed_rows, 2 * HEAD_SIZE))] * chips
        + [whole((CHIP_ROWS, HEAD_SIZE))] * prior,
        operands,
        (shape(sent_rows, GROUP_WIDTH), shape(CHIP_ROWS, HEAD_SIZE, f32), shape(CHIP_ROWS, width, f32))
        + tuple(shape(CHIP_ROWS, width) for _ in range(chips - 1)),
        (whole((sent_rows, GROUP_WIDTH)), whole((CHIP_ROWS, HEAD_SIZE))) + (whole((CHIP_ROWS, width)),) * chips,
        scratch=(
            pltpu.VMEM((reach, HEAD_SIZE), bf16),
            pltpu.VMEM((reach, 2 * HEAD_SIZE), bf16),
            pltpu.VMEM((tall, HEAD_SIZE), bf16),
            pltpu.VMEM((tall, HEAD_SIZE), bf16),
            pltpu.VMEM((tall, reach), bf16),
            pltpu.VMEM((tall, 2 * HEAD_SIZE), f32),
            pltpu.VMEM((reach, HEAD_SIZE), f32),
        ),
        flops=100 * tall * HEAD_SIZE * reach,
        moved=6 * packed_rows * GROUP_WIDTH,
    )


def local(queries, keys, values, cotangent, router_logits, positions, counts):
    shards = lax.axis_size("ctx")
    sections = lax.axis_size("section")
    chips = shards // CORES
    scalars = counts[0]
    def swap(x):
        return lax.ppermute(x, "ctx", [(i, i ^ 1) for i in range(shards)])

    def onward(x, by):
        step = by * CORES
        return lax.ppermute(x, "ctx", [(i, i + step) for i in range(shards) if 0 <= i + step < shards])

    def to_later(x):
        return [onward(x, d) for d in reversed(range(1, chips))][::-1]

    def section_on(x):
        return lax.ppermute(x, "section", [(i, (i + 1) % sections) for i in range(sections)])

    def near(x):
        return pltpu.with_memory_space_constraint(x, pltpu.HBM)

    far = pl.BlockSpec(memory_space=pltpu.HBM)
    column_spec = fixed(HEAD_SIZE, 2 * HALF_KEY // HEAD_SIZE)
    payload, column, own_kv = call(
        pack_kernel,
        scalars,
        [far, far, far],
        (near(keys), near(values), near(router_logits)),
        (shape(SLOTS, PAYLOAD), shape(SLOTS, HEAD_SIZE), shape(SLOTS, 2 * HALF_KEY)),
        tuple(whole((SLOTS, width)) for width in (PAYLOAD, HEAD_SIZE, 2 * HALF_KEY)),
        scratch=(pltpu.VMEM((1, SLOTS), bf16), pltpu.SemaphoreType.DMA((5,))),
        moved=4 * SLOTS * PAYLOAD * 2,
    )
    other = swap(payload)
    packed_rows = CHIP_ROWS + META_ROWS
    *packed, pair = call(
        chip_kernel,
        scalars,
        [fixed(HALF_KEY, 0), fixed(HALF_KEY, 1), fixed(HALF_KEY, 0), fixed(HALF_KEY, 1), column_spec],
        (own_kv, own_kv, other, other, other),
        tuple(shape(packed_rows, 2 * HEAD_SIZE) for _ in range(LOCAL_HEADS)) + (shape(META_ROWS, HEAD_SIZE),),
        tuple(whole((packed_rows, 2 * HEAD_SIZE)) for _ in range(LOCAL_HEADS)) + (whole((META_ROWS, HEAD_SIZE)),),
        moved=4 * packed_rows * HALF_KEY * 2,
    )
    gathered = [[packed[0]] + to_later(packed[0])]
    own, theirs = call(
        halves_kernel,
        scalars,
        [far, far, pl.BlockSpec(memory_space=pl.ANY)],
        (near(queries), near(cotangent), swap(pair)),
        (shape(SLOTS, 2 * HALF_QUERY), shape(SLOTS, 2 * HALF_QUERY)),
        (whole((SLOTS, 2 * HALF_QUERY)), whole((SLOTS, 2 * HALF_QUERY))),
        scratch=(pltpu.SemaphoreType.DMA((2, 2)),),
        moved=0,
    )
    for h in range(1, LOCAL_HEADS):
        packed[h], theirs = lax.optimization_barrier((packed[h], theirs))
        gathered.append([packed[h]] + to_later(packed[h]))
    swapped = swap(theirs)
    if chips > 1:
        gathered[0][:0:-1] = passed(scalars, gathered[0][:0:-1])
    prior = []
    branches, gate_parts = [], []
    for h in range(LOCAL_HEADS):
        results = attend(chips, shards, h, scalars, own, swapped, own, swapped, column, other, gathered[h][0], *gathered[h][2:], *gathered[h][1:2], *prior)
        branches.append(section_on(results[0]))
        gate_parts.append(results[1])
        prior = results[2:]
    returned = [onward(prior[d], -d) for d in range(1, chips)]
    branches[0], *returned = lax.optimization_barrier((branches[0], *returned))
    grad_mine, gate_mine, grad_theirs = call(
        lambda *refs: gradient_kernel(chips, *refs),
        scalars,
        [column_spec]
        + [whole((CHIP_ROWS, HALF_KEY))] * chips
        + [whole((CHIP_ROWS, HEAD_SIZE))] * LOCAL_HEADS,
        (other, prior[0], *returned, *gate_parts),
        (shape(SLOTS, HALF_KEY), shape(SLOTS, HEAD_SIZE, f32), shape(SLOTS, HALF_KEY + HEAD_SIZE)),
        (whole((SLOTS, HALF_KEY)), whole((SLOTS, HEAD_SIZE)), whole((SLOTS, HALF_KEY + HEAD_SIZE))),
        moved=8 * CHIP_ROWS * HALF_KEY,
    )
    grad_other = swap(grad_theirs)
    value_grad, gate_grad = call(
        finish_kernel,
        scalars,
        [
            whole((SLOTS, HALF_KEY)),
            whole((SLOTS, HEAD_SIZE)),
            whole((SLOTS, HALF_KEY + HEAD_SIZE)),
            whole((SLOTS, HEAD_SIZE)),
        ],
        (grad_mine, gate_mine, grad_other, column),
        (shape(SLOTS, CORES * HALF_KEY), shape(1, SLOTS)),
        (whole((SLOTS, CORES * HALF_KEY)), whole((1, SLOTS))),
        moved=8 * SLOTS * HALF_KEY,
    )
    branches[-1], value_grad = lax.optimization_barrier((branches[-1], value_grad))
    handed = ()
    for h in range(LOCAL_HEADS):
        mine, theirs = call(
            branch_kernel,
            scalars,
            [
                whole((CHIP_ROWS, GROUP_WIDTH)),
                pl.BlockSpec((META_ROWS, HEAD_SIZE), lambda i, s: (CHIP_ROWS // META_ROWS, 0)),
            ],
            (branches[h], branches[0]),
            (shape(SLOTS, GROUP_WIDTH), shape(SLOTS, GROUP_WIDTH)),
            (whole((SLOTS, GROUP_WIDTH)), whole((SLOTS, GROUP_WIDTH))),
            moved=7 * SLOTS * HALF_QUERY,
        )
        handed = (
            call(
                lambda *refs, h=h: join_kernel(h, *refs),
                scalars,
                [whole((SLOTS, GROUP_WIDTH))] * 2 + [far] * len(handed),
                (mine, swap(theirs), *handed),
                shape(SLOTS, CORES * HALF_QUERY),
                far,
                scratch=(pltpu.SemaphoreType.DMA((2,)),),
                moved=8 * SLOTS * GROUP_WIDTH,
                aliases={3: 0} if handed else {},
            ),
        )
    (handed,) = handed
    return (handed[None], value_grad[None], gate_grad)


def solution(mesh):
    rows = P("section", "ctx", None)
    flat = P("section", "ctx")
    return jax.shard_map(
        local,
        mesh=mesh,
        in_specs=(rows, rows, rows, rows, flat, flat, flat),
        out_specs=(rows, rows, flat),
        check_vma=False,
    )
```
